32 devices in a mesh: dp: 2 (over core), wide: 8 (over z, y), narrow: 2 (over x).
Axes of the slice: x: 2, y: 2, z: 4, core: 2. Of those that a mesh axis runs over, the one named last changes fastest.
Arguments:
- layer_input: bfloat16 [8192, 1088], P(('dp', 'wide'), 'narrow'), may hold values from -6 to 6
- doc_segments: int32 [2, 4096], replicated, may hold values from 0 to 7, as said below
- first_gain: bfloat16 [1088], P('narrow'), may hold values from 0.25 to 1.75
- first_shift: bfloat16 [1088], P('narrow'), may hold values from -2 to 2
- heads_weight: bfloat16 [1088, 3, 1088], P('narrow', None, 'wide'), may hold values from -1 to 1
- query_bias: bfloat16 [1088], P('wide'), may hold values from -2 to 2
- value_bias: bfloat16 [1088], P('wide'), may hold values from -2 to 2
- merge_weight: bfloat16 [1088, 1088], P('wide', 'narrow'), may hold values from -0.1875 to 0.1875
- merge_bias: bfloat16 [1088], P('narrow'), may hold values from -2 to 2
- second_gain: bfloat16 [1088], P('narrow'), may hold values from 0.25 to 1.75
- second_shift: bfloat16 [1088], P('narrow'), may hold values from -2 to 2
- up_weight: bfloat16 [1088, 4352], P('narrow', 'wide'), may hold values from -1 to 1
- up_bias: bfloat16 [4352], P('wide'), may hold values from -2 to 2
- down_weight: bfloat16 [4352, 1088], P('wide', 'narrow'), may hold values from -0.09375 to 0.09375
- down_bias: bfloat16 [1088], P('narrow'), may hold values from -2 to 2
- out_cotangent: bfloat16 [8192, 1088], P(('dp', 'wide'), 'narrow'), may hold values from -6 to 6
Outputs:
- layer_output: bfloat16 [8192, 1088], P(('dp', 'wide'), 'narrow')
- input_grad: bfloat16 [8192, 1088], P(('dp', 'wide'), 'narrow')
- first_gain_grad: float32 [1088], P('narrow')
- first_shift_grad: float32 [1088], P('narrow')
- heads_weight_grad: float32 [1088, 3, 1088], P('narrow', None, 'wide')
- query_bias_grad: float32 [1088], P('wide')
- value_bias_grad: float32 [1088], P('wide')
- merge_weight_grad: float32 [1088, 1088], P('wide', 'narrow')
- merge_bias_grad: float32 [1088], P('narrow')
- second_gain_grad: float32 [1088], P('narrow')
- second_shift_grad: float32 [1088], P('narrow')
- up_weight_grad: float32 [1088, 4352], P('narrow', 'wide')
- up_bias_grad: float32 [4352], P('wide')
- down_weight_grad: float32 [4352, 1088], P('wide', 'narrow')
- down_bias_grad: float32 [1088], P('narrow')
The draws below stay inside these ranges and needn't reach their ends.
Inputs may be any that keep to these rules, and one draw needn't show every extreme that they name: `doc_segments`: in each sequence's row, numbers rise by one at each document's start and every number is used; each run of 4096 positions from the row's start holds 8 whole documents, three of them of exactly 1024 tokens, and no document is longer.
All inputs are finite; a program needn't handle non-finite values.
Results may differ from the reference program's by a relative error of at most 0.0228.
The reference program's roundings to bfloat16 on the way count: a program that leaves them out, or rounds other values in their place, can miss the bound.
Values may be sent and summed in bfloat16 or wider, within the bound.
A program may use at most 320 MiB of HBM per device.

```python
import jax
import jax.numpy as jnp
from jax import lax

HEAD = 64
FF = 4352
TOK_DEV = 256
REACH = 4
D = 1088
SEQ = 4096
SEQS = 2
TOKENS = 8192


def segment_rows(key):
    block_rows = TOK_DEV
    groups = SEQ // (16 * block_rows)
    low_key = jax.random.fold_in(key, 21)
    split_key = jax.random.fold_in(key, 22)
    offsets = jax.random.randint(low_key, (SEQS, groups, 3), block_rows // 8, block_rows // 2)
    first_gap = offsets[..., 0]
    second = offsets[..., 1]
    third_gap = offsets[..., 2]
    fourth = jax.random.randint(split_key, (SEQS, groups), 1, 2 * block_rows - third_gap)
    fifth_len = 2 * block_rows - third_gap - fourth
    longest = jnp.full((SEQS, groups), 4 * block_rows, jnp.int32)
    lengths = jnp.stack([first_gap, longest, block_rows + second - first_gap, longest, block_rows + third_gap - second, longest, fourth, fifth_len], 2).astype(jnp.int32).reshape(SEQS, groups * 8)
    doc_ends = jnp.cumsum(lengths, 1).astype(jnp.int32)
    places = jnp.arange(SEQ, dtype=jnp.int32)
    return jnp.sum((places[None, :, None] >= doc_ends[:, None, :]).astype(jnp.int32), 2).astype(jnp.int32)


def sign_vector(key, salt_value, length):
    picked = jax.random.bernoulli(jax.random.fold_in(key, salt_value), 0.5, (length,))
    return jnp.where(picked, 1.0, -1.0).astype(jnp.float32)


def draw_doc_segments(key, part):
    return segment_rows(key)


def draw_layer_input(key, part):
    segments = segment_rows(key).reshape(TOKENS)
    previous = jnp.concatenate([jnp.full((1,), -1, jnp.int32), segments[:-1]])
    places = jnp.arange(TOKENS, dtype=jnp.int32) % SEQ
    starts = (segments != previous) | (places == 0)
    direction = sign_vector(key, 31, D)
    noise_key = jax.random.fold_in(key, 32)
    jitter = jnp.clip(jax.random.normal(noise_key, (TOKENS, D), jnp.float32), -4.0, 4.0)
    token_rows = 0.58 * direction[None, :] + jitter
    sink_rows = 2.2 * direction[None, :] + 0.8 * jitter
    return jnp.where(starts[:, None], sink_rows, token_rows).astype(jnp.bfloat16)


def draw_heads_weight(key, part):
    direction = sign_vector(key, 31, D)
    pattern = sign_vector(key, 34, D)
    base_key = jax.random.fold_in(key, 35)
    jitter = jnp.clip(jax.random.normal(base_key, (D, 3, D), jnp.float32), -5.0, 5.0)
    strength = 2.5
    slot_mask = jnp.array([1.0, 1.0, 0.0], jnp.float32)
    aligned = direction[:, None, None] * slot_mask[None, :, None] * pattern[None, None, :] * (strength / D)
    return (jitter * D ** (-0.5) + aligned).astype(jnp.bfloat16)


def draw_up_weight(key, part):
    columns = sign_vector(key, 41, FF)
    base_key = jax.random.fold_in(key, 42)
    jitter = jnp.clip(jax.random.normal(base_key, (D, FF), jnp.float32), -5.0, 5.0)
    return ((jitter + columns[None, :]) * D ** (-0.5)).astype(jnp.bfloat16)


def block_scale(own_key, dims, pieces, smallest, largest):
    level = 1.0
    for dim, parts in pieces:
        heights = jax.random.uniform(jax.random.fold_in(jax.random.fold_in(own_key, 6), dim), (parts,), jnp.float32, smallest / len(pieces), largest / len(pieces))
        level = level * jnp.repeat(jnp.exp(heights), dims[dim] // parts).reshape((-1,) + (1,) * (len(dims) - 1 - dim))
    return level


def gaussian(rng, extent, deviation, most, shards=(), kind=jnp.bfloat16):
    level = block_scale(rng, extent, shards, -0.22, 0.18) if shards else 1.0
    entries = jax.random.normal(rng, extent, jnp.float32) * deviation * level
    return jnp.minimum(jnp.maximum(entries, -most), most).astype(kind)


def setup_inputs(seed: int = 0) -> dict:
    keys = jax.random.split(jax.random.key(seed), 17)
    layer_input = draw_layer_input(jax.random.fold_in(keys[16], 71), 0)
    doc_segments = draw_doc_segments(jax.random.fold_in(keys[16], 71), 0)
    first_gain = jnp.clip(1.0 + 0.15 * jax.random.normal(keys[2], (D,), jnp.float32), 0.25, 1.75).astype(jnp.bfloat16)
    first_shift = gaussian(keys[3], (D,), 0.3, 2.0, ((0, 2),))
    heads_weight = draw_heads_weight(jax.random.fold_in(keys[16], 71), 0)
    query_bias = gaussian(keys[5], (D,), 0.3, 2.0, ((0, 8),))
    value_bias = gaussian(keys[6], (D,), 0.3, 2.0, ((0, 8),))
    merge_weight = gaussian(keys[7], (D, D), D ** -0.5, 0.1875, ((0, 8), (1, 2)))
    merge_bias = gaussian(keys[8], (D,), 0.3, 2.0, ((0, 2),))
    second_gain = jnp.clip(1.0 + 0.15 * jax.random.normal(keys[9], (D,), jnp.float32), 0.25, 1.75).astype(jnp.bfloat16)
    second_shift = gaussian(keys[10], (D,), 0.3, 2.0, ((0, 2),))
    up_weight = draw_up_weight(jax.random.fold_in(keys[16], 71), 0)
    up_bias = gaussian(keys[12], (FF,), 0.3, 2.0, ((0, 8),))
    down_weight = gaussian(keys[13], (FF, D), FF ** -0.5, 0.09375, ((0, 8), (1, 2)))
    down_bias = gaussian(keys[14], (D,), 0.3, 2.0, ((0, 2),))
    out_cotangent = gaussian(keys[15], (TOKENS, D), 1.0, 6.0, ((0, 16), (1, 2)))
    return {"layer_input": layer_input, "doc_segments": doc_segments, "first_gain": first_gain, "first_shift": first_shift, "heads_weight": heads_weight, "query_bias": query_bias, "value_bias": value_bias, "merge_weight": merge_weight, "merge_bias": merge_bias, "second_gain": second_gain, "second_shift": second_shift, "up_weight": up_weight, "up_bias": up_bias, "down_weight": down_weight, "down_bias": down_bias, "out_cotangent": out_cotangent}


HIGH = lax.Precision.HIGHEST
EPS = 1e-05
NEGATIVE = -1e+30

@jax.custom_vjp
def low(v):
    return lax.optimization_barrier(v.astype(jnp.bfloat16)).astype(jnp.float32)

@jax.custom_vjp
def low_back(v):
    return v

def low_keep(v):
    return (low(v), None)

def low_pass(kept, grad):
    return (grad,)

def back_keep(v):
    return (v, None)

def back_low(kept, grad):
    return (low(grad),)
low.defvjp(low_keep, low_pass)
low_back.defvjp(back_keep, back_low)

def product(left, right):
    return jnp.dot(left, right, precision=HIGH)

def layer_norm(values, gain, shift):
    mean = lax.optimization_barrier(jnp.mean(values, 1, keepdims=True))
    centred = values - mean
    spread = lax.optimization_barrier(jnp.mean(centred * centred, 1, keepdims=True))
    return centred * lax.rsqrt(spread + EPS) * gain + shift

def gelu_unit(values):
    return jax.nn.gelu(values, approximate=False)

def attention(packed, segments):
    heads = D // HEAD
    scale = HEAD ** (-0.5)
    margin = REACH * TOK_DEV
    span = (REACH + 1) * TOK_DEV
    query = packed[:, 0].reshape(SEQ, heads, HEAD)
    padding = jnp.zeros((margin, heads, HEAD), jnp.float32)
    key = jnp.concatenate([padding, packed[:, 1].reshape(SEQ, heads, HEAD)], 0)
    value = jnp.concatenate([padding, packed[:, 2].reshape(SEQ, heads, HEAD)], 0)
    seg_padded = jnp.concatenate([jnp.full((margin,), -1, jnp.int32), segments.astype(jnp.int32)], 0)

    def one_block(index):
        start = (index * TOK_DEV).astype(jnp.int32)
        block_query = lax.dynamic_slice_in_dim(query, start, TOK_DEV, 0)
        block_key = lax.dynamic_slice_in_dim(key, start, span, 0)
        block_value = lax.dynamic_slice_in_dim(value, start, span, 0)
        query_seg = lax.dynamic_slice_in_dim(segments.astype(jnp.int32), start, TOK_DEV, 0)
        key_seg = lax.dynamic_slice_in_dim(seg_padded, start, span, 0)
        query_pos = jnp.arange(TOK_DEV, dtype=jnp.int32) + margin
        key_pos = jnp.arange(span, dtype=jnp.int32)
        allowed = (query_seg[:, None] == key_seg[None, :]) & (key_pos[None, :] <= query_pos[:, None])
        logits = jnp.einsum('qhd,khd->hqk', block_query, block_key, precision=HIGH) * scale
        logits = low_back(logits)
        logits = jnp.where(allowed[None], logits, NEGATIVE)
        probs = low(jax.nn.softmax(logits, axis=-1))
        return jnp.einsum('hqk,khd->qhd', probs, block_value, precision=HIGH).reshape(TOK_DEV, D)
    blocks = lax.map(jax.checkpoint(one_block), jnp.arange(SEQ // TOK_DEV, dtype=jnp.int32))
    return blocks.reshape(SEQ, D)

def layer(values, segments, first_gain, first_shift, heads_weight, query_bias, value_bias, merge_weight, merge_bias, second_gain, second_shift, up_weight, up_bias, down_weight, down_bias):
    low1 = low(layer_norm(values, first_gain, first_shift))
    packed = product(low1, heads_weight.reshape(D, 3 * D)).reshape(SEQ, 3, D)
    packed = packed + jnp.stack([query_bias, jnp.zeros_like(query_bias), value_bias])[None]
    packed = low(low_back(packed))
    mixed = low(low_back(attention(packed, segments)))
    residual = values + low_back(product(mixed, merge_weight) + merge_bias)
    low2 = low(layer_norm(residual, second_gain, second_shift))
    before = low_back(product(low2, up_weight) + up_bias)
    hidden = low(gelu_unit(before))
    return residual + product(hidden, down_weight) + down_bias

def reference(layer_input, doc_segments, first_gain, first_shift, heads_weight, query_bias, value_bias, merge_weight, merge_bias, second_gain, second_shift, up_weight, up_bias, down_weight, down_bias, out_cotangent):
    params = tuple((p.astype(jnp.float32) for p in (first_gain, first_shift, heads_weight, query_bias, value_bias, merge_weight, merge_bias, second_gain, second_shift, up_weight, up_bias, down_weight, down_bias)))
    inputs = layer_input.astype(jnp.float32).reshape(SEQS, SEQ, D)
    cotangents = out_cotangent.astype(jnp.float32).reshape(SEQS, SEQ, D)
    zeros = tuple((jnp.zeros_like(p) for p in params))

    def step(carry, item):
        values, segments, cotangent = item

        def run(values, *weights):
            return layer(values, segments, *weights)
        output, back = jax.vjp(run, values, *params)
        grads = back(cotangent)
        carry = tuple((c + g for c, g in zip(carry, grads[1:])))
        return (carry, (output.astype(jnp.bfloat16), grads[0].astype(jnp.bfloat16)))
    totals, (outputs, input_grads) = lax.scan(step, zeros, (inputs, doc_segments, cotangents))
    return (outputs.reshape(TOKENS, D), input_grads.reshape(TOKENS, D), totals[0], totals[1], totals[2], totals[3], totals[4], totals[5], totals[6], totals[7], totals[8], totals[9], totals[10], totals[11], totals[12])
```

```python
import functools

import jax
import jax.numpy as jnp
from jax import lax
from jax.experimental import pallas as pl
from jax.experimental.pallas import tpu as pltpu
from jax.sharding import PartitionSpec as P

HEAD = 64
REACH = 4
EPS = 1e-05
NEGATIVE = -1e30
LANES = 128
BF = jnp.bfloat16
F32 = jnp.float32
MESH = pl.DeviceIdType.MESH
ANY = pl.BlockSpec(memory_space=pl.ANY)
DMA = pltpu.SemaphoreType.DMA
SCALE = HEAD ** (-0.5)
LIMIT = 58 * 1024 * 1024


def widths(half):
    main = half // LANES * LANES
    return main, half - main


def rem_rows(rows, half):
    main, rem = widths(half)
    return up16(-(-rows // (main // rem)))


def up16(rows):
    return -(-rows // 16) * 16


def pack(block):
    rows, half = block.shape[-2:]
    main, rem = widths(half)
    count = main // rem
    extra = rem_rows(rows, half)
    lead = block.shape[:-2]
    none = [(0, 0)] * len(lead)
    tail = jnp.pad(block[..., main:], none + [(0, count * extra - rows), (0, 0)])
    tail = jnp.swapaxes(tail.reshape(lead + (count, extra, rem)), -2, -3).reshape(lead + (extra, main))
    return jnp.concatenate([block[..., :main], tail], -2)


def unpack(block, rows, half):
    main, rem = widths(half)
    count = main // rem
    extra = rem_rows(rows, half)
    lead = block.shape[:-2]
    tail = block[..., rows : rows + extra, :].reshape(lead + (extra, count, rem))
    tail = jnp.swapaxes(tail, -2, -3).reshape(lead + (count * extra, rem))[..., :rows, :]
    return block[..., :rows, :], tail


def unpack_half(block, rows, half):
    return jnp.concatenate(unpack(block, rows, half), -1)


def join(blocks, rows, half):
    body, tail = unpack(blocks, rows, half)
    return jnp.concatenate([body[0], body[1], tail[0], tail[1]], -1)


def halves(full):
    half = full.shape[-1] // 2
    main, rem = widths(half)
    edge = 2 * main
    return jnp.stack(
        [
            jnp.concatenate([full[..., :main], full[..., edge : edge + rem]], -1),
            jnp.concatenate([full[..., main:edge], full[..., edge + rem :]], -1),
        ]
    )


def place():
    c, w, n = lax.axis_index("dp"), lax.axis_index("wide"), lax.axis_index("narrow")
    z, y = lax.div(w, 2), lax.rem(w, 2)
    first = (y + c * (1 - 2 * y), n + (1 - c) * (1 - 2 * n))
    second = (y + (1 - c) * (1 - 2 * y), n + c * (1 - 2 * n))
    return c, z, y, n, first, second


def wide_of(z, y):
    return z * 2 + y


def remote(src, dst, send, recv, device):
    return pltpu.make_async_remote_copy(
        src_ref=src, dst_ref=dst, send_sem=send, recv_sem=recv, device_id=device, device_id_type=MESH
    )


def greet(devices):
    barrier = pltpu.get_barrier_semaphore()
    for device in devices:
        pl.semaphore_signal(barrier, inc=1, device_id=device, device_id_type=MESH)
    pl.semaphore_wait(barrier, len(devices))


def partners(outer):
    c, z, y, n, _, _ = place()
    out = [(c, wide_of(lax.rem(z + d, outer), y), n) for d in range(1, outer)]
    out.append((c, wide_of(z, 1 - y), n))
    out.append((c, wide_of(z, y), 1 - n))
    out.append((1 - c, wide_of(z, y), n))
    return out


class Gather:
    def __init__(self, outer, src, out, both, sems):
        self.outer, self.src, self.out, self.both = outer, src, out, both
        self.zs, self.zr, self.fs, self.fr, self.ss, self.sr, self.cs, self.cr, self.local = sems
        self.sent = []

    def block(self, z, y, n):
        c = lax.axis_index("dp")
        return self.out.at[c, wide_of(z, y), n] if self.both else self.out.at[wide_of(z, y), n]

    def go(self, copy):
        copy.start()
        self.sent.append(copy)

    def z_at(self, d):
        return lax.rem(place()[1] + self.outer - d, self.outer)

    def to_first(self, d, src):
        c, z, y, n, first, second = place()
        device = (c, wide_of(z, first[0]), first[1])
        self.go(remote(src, self.block(self.z_at(d), y, n), self.fs.at[d], self.fr.at[d], device))

    def to_second(self, d, src, k):
        c, z, y, n, first, second = place()
        device = (c, wide_of(z, second[0]), second[1])
        dst = self.block(self.z_at(d), y, n) if k == 0 else self.block(self.z_at(d), *first)
        i = k * self.outer + d
        self.go(remote(src, dst, self.ss.at[i], self.sr.at[i], device))

    def to_core(self, i, src, dst):
        if self.both:
            c, z, y, n, _, _ = place()
            self.go(remote(src, dst, self.cs.at[i], self.cr.at[i], (1 - c, wide_of(z, y), n)))

    def start(self):
        c, z, y, n, first, second = place()
        own = self.block(z, y, n)
        self.keep = pltpu.make_async_copy(self.src, own, self.local)
        self.keep.start()
        for d in range(1, self.outer):
            device = (c, wide_of(lax.rem(z + d, self.outer), y), n)
            self.go(remote(self.src, own, self.zs.at[d - 1], self.zr.at[d - 1], device))
        self.to_first(0, self.src)
        self.to_second(0, self.src, 0)
        self.to_core(0, self.src, own)

    def arrived(self, dst, recv):
        c, z, y, n, _, _ = place()
        remote(dst, dst, recv, recv, (1 - c, wide_of(z, y), n)).wait_recv()

    def along_z(self, d):
        c, z, y, n, first, second = place()
        got = self.block(self.z_at(d), y, n)
        self.arrived(got, self.zr.at[d - 1])
        self.to_first(d, got)
        self.to_second(d, got, 0)
        self.to_core(d, got, got)

    def along_first(self, d):
        c, z, y, n, first, second = place()
        got = self.block(self.z_at(d), *first)
        self.arrived(got, self.fr.at[d])
        self.to_second(d, got, 1)
        self.to_core(self.outer + d, got, got)

    def along_second(self, d, k):
        c, z, y, n, first, second = place()
        got = self.block(self.z_at(d), *second) if k == 0 else self.block(self.z_at(d), 1 - y, 1 - n)
        i = k * self.outer + d
        self.arrived(got, self.sr.at[i])
        self.to_core(2 * self.outer + i, got, got)

    def rest(self):
        for d in range(1, self.outer):
            self.along_z(d)
        for d in range(self.outer):
            self.along_first(d)
        for k in range(2):
            for d in range(self.outer):
                self.along_second(d, k)

    def finish(self):
        c, z, y, n, first, second = place()
        if self.both:
            spots = [(y, n), first, second, (1 - y, 1 - n)]
            for k, spot in enumerate(spots):
                for d in range(self.outer):
                    got = self.out.at[1 - c, wide_of(self.z_at(d), spot[0]), spot[1]]
                    self.arrived(got, self.cr.at[k * self.outer + d])
        self.keep.wait()
        for copy in self.sent:
            copy.wait_send()


def gather_sems(outer):
    return [
        DMA((outer,)),
        DMA((outer,)),
        DMA((outer,)),
        DMA((outer,)),
        DMA((2 * outer,)),
        DMA((2 * outer,)),
        DMA((4 * outer,)),
        DMA((4 * outer,)),
        DMA,
    ]


def enter_kernel(outer, xin, cot, sa, sm, x_out, cot_out, ga, gm, xs, xr, hs, hr, ks, kr, ls, *sems):
    c, z, y, n, first, second = place()
    me = wide_of(z, y)
    greet(partners(outer))
    other_n = (c, me, 1 - n)
    other_y = (c, wide_of(z, 1 - y), n)
    other_c = (1 - c, me, n)
    later = (c, wide_of(lax.rem(z + 1, outer), y), n)
    sent = []

    def go(copy):
        copy.start()
        sent.append(copy)

    def arrived(dst, recv):
        remote(dst, dst, recv, recv, other_c).wait_recv()

    def x_send(j):
        src = x_out.at[n, j + 1 - n] if j < 4 else xin.at[1 - n]
        go(remote(src, x_out.at[n, j + 1 - n], hs.at[j], hr.at[j], other_n))

    own = x_out.at[n, pl.ds(4, 2)]
    keep = pltpu.make_async_copy(xin, own, ls.at[0])
    keep.start()
    keep_cot = pltpu.make_async_copy(cot.at[n], cot_out.at[c, n], ls.at[1])
    keep_cot.start()
    go(remote(xin, x_out.at[n, pl.ds(0, 2)], xs.at[0], xr.at[0], later))
    x_send(4)
    heads = Gather(outer, sa, ga, True, sems[:9])
    heads.start()
    arrived(x_out.at[n, pl.ds(0, 2)], xr.at[0])
    keep.wait()
    x_send(0)
    go(
        remote(
            x_out.at[n, pl.ds(4 * (1 - y), 2)],
            x_out.at[n, pl.ds(2, 2)],
            xs.at[1],
            xr.at[1],
            other_y,
        )
    )
    for d in range(1, outer):
        heads.along_z(d)
    arrived(x_out.at[n, pl.ds(2, 2)], xr.at[1])
    for j in (1, 2, 3):
        x_send(j)
    go(remote(cot.at[1 - n], cot_out.at[c, n], ks.at[0], kr.at[0], other_n))
    go(remote(cot.at[n], cot_out.at[c, n], ks.at[1], kr.at[1], other_c))
    for d in range(outer):
        heads.along_first(d)
    mlp = Gather(outer, sm, gm, False, sems[9:])
    mlp.start()
    for k in range(2):
        for d in range(outer):
            heads.along_second(d, k)
    for j in range(5):
        arrived(x_out.at[1 - n, j + n], hr.at[j])
    arrived(cot_out.at[c, 1 - n], kr.at[0])
    go(remote(cot_out.at[c, 1 - n], cot_out.at[c, 1 - n], ks.at[2], kr.at[2], other_c))
    mlp.rest()
    arrived(cot_out.at[1 - c, n], kr.at[1])
    arrived(cot_out.at[1 - c, 1 - n], kr.at[2])
    keep_cot.wait()
    for copy in sent:
        copy.wait_send()
    heads.finish()
    mlp.finish()


def enter(xin, cot, sa, sm):
    wide = lax.axis_size("wide")
    outer = wide // 2
    rows = xin.shape[1:]
    return pl.pallas_call(
        functools.partial(enter_kernel, outer),
        out_shape=(
            jax.ShapeDtypeStruct((2, 6) + rows, BF),
            jax.ShapeDtypeStruct((2, 2) + rows, BF),
            jax.ShapeDtypeStruct((2, wide, 2) + sa.shape, BF),
            jax.ShapeDtypeStruct((wide, 2) + sm.shape, BF),
        ),
        in_specs=[ANY] * 4,
        out_specs=(ANY,) * 4,
        scratch_shapes=[DMA((2,)), DMA((2,)), DMA((5,)), DMA((5,)), DMA((3,)), DMA((3,)), DMA((2,))]
        + gather_sems(outer)
        + gather_sems(outer),
        compiler_params=pltpu.CompilerParams(collective_id=0, has_side_effects=True),
    )(xin, cot, sa, sm)


class Scatter:
    def __init__(self, outer, part, one, two, three, total, fin, sems):
        self.outer, self.part = outer, part
        self.one, self.two, self.three, self.total, self.fin = one, two, three, total, fin
        self.ss, self.sr, self.fs, self.fr, self.zs, self.zr, self.cs, self.cr = sems
        self.sent = []

    def go(self, copy):
        copy.start()
        self.sent.append(copy)

    def arrived(self, dst, recv):
        c, z, y, n, _, _ = place()
        remote(dst, dst, recv, recv, (1 - c, wide_of(z, y), n)).wait_recv()

    def z_at(self, d):
        return lax.rem(place()[1] + d, self.outer)

    def order(self):
        return [d for d in range(1, self.outer)] + [0]

    def start(self):
        c, z, y, n, first, second = place()
        device = (c, wide_of(z, second[0]), second[1])
        for k, spot in ((1, (1 - y, 1 - n)), (0, second)):
            for d in self.order():
                i = k * self.outer + d
                self.go(
                    remote(self.part(self.z_at(d), *spot), self.one.at[i], self.ss.at[i], self.sr.at[i], device)
                )

    def to_first(self, d):
        c, z, y, n, first, second = place()
        device = (c, wide_of(z, first[0]), first[1])
        i = self.outer + d
        self.arrived(self.one.at[i], self.sr.at[i])
        self.one[i] = (self.one[i].astype(F32) + self.part(self.z_at(d), *first)[...].astype(F32)).astype(BF)
        self.go(remote(self.one.at[i], self.two.at[d], self.fs.at[d], self.fr.at[d], device))

    def to_z(self, d):
        c, z, y, n, first, second = place()
        self.arrived(self.one.at[d], self.sr.at[d])
        self.arrived(self.two.at[d], self.fr.at[d])
        value = (
            self.one[d].astype(F32) + self.two[d].astype(F32) + self.part(self.z_at(d), y, n)[...].astype(F32)
        )
        if d == 0:
            self.total[...] = value
        else:
            self.one[d] = value.astype(BF)
            device = (c, wide_of(self.z_at(d), y), n)
            self.go(
                remote(self.one.at[d], self.three.at[d - 1], self.zs.at[d - 1], self.zr.at[d - 1], device)
            )

    def close(self):
        c, z, y, n, first, second = place()
        value = self.total[...]
        for d in range(1, self.outer):
            self.arrived(self.three.at[d - 1], self.zr.at[d - 1])
            value = value + self.three[d - 1].astype(F32)
        self.fin[c] = value
        self.go(remote(self.fin.at[c], self.fin.at[c], self.cs, self.cr, (1 - c, wide_of(z, y), n)))

    def finish(self):
        c = lax.axis_index("dp")
        self.arrived(self.fin.at[1 - c], self.cr)
        for copy in self.sent:
            copy.wait_send()


def scatter_scratch(outer, block):
    return [
        pltpu.VMEM((2 * outer,) + block, BF),
        pltpu.VMEM((outer,) + block, BF),
        pltpu.VMEM((outer,) + block, BF),
        pltpu.VMEM(block, F32),
    ]


def scatter_sems(outer):
    return [
        DMA((2 * outer,)),
        DMA((2 * outer,)),
        DMA((outer,)),
        DMA((outer,)),
        DMA((outer,)),
        DMA((outer,)),
        DMA,
        DMA,
    ]


def leave_kernel(
    outer, pm, pa, pg, lo, mo, ao, xg, lo_out, pcore, acc, got_x, got_z, got_y,
    m1, m2, m3, mt, a1, a2, a3, at, xs, xr, ccs, ccr, *sems
):
    c, z, y, n, first, second = place()
    me = wide_of(z, y)
    greet(partners(outer) + [])
    other_n = (c, me, 1 - n)
    other_y = (c, wide_of(z, 1 - y), n)
    other_c = (1 - c, me, n)
    earlier = (c, wide_of(lax.rem(z + outer - 1, outer), y), n)
    sent = []

    def go(copy):
        copy.start()
        sent.append(copy)

    def arrived(dst, recv):
        remote(dst, dst, recv, recv, other_c).wait_recv()

    mlp = Scatter(outer, lambda z, y, n: pm.at[wide_of(z, y), n], m1, m2, m3, mt, mo, sems[:8])
    heads = Scatter(outer, lambda z, y, n: pcore.at[wide_of(z, y), n], a1, a2, a3, at, ao, sems[8:])
    go(remote(pg.at[1 - n], got_x, xs.at[0], xr.at[0], other_n))
    core_copy = remote(pa.at[1 - c], pcore, ccs, ccr, other_c)
    core_copy.start()
    mlp.start()
    acc[...] = jnp.zeros_like(acc)
    for j in range(5):
        acc[n + j] = pg[n, j].astype(F32)
    arrived(got_x, xr.at[0])
    for j in range(5):
        acc[1 - n + j] = acc[1 - n + j] + got_x[j].astype(F32)
    got_x[pl.ds(0, 2)] = acc[pl.ds(2, 2)].astype(BF)
    go(remote(got_x.at[pl.ds(0, 2)], got_y, xs.at[1], xr.at[1], other_y))
    core_copy.wait_recv()

    @pl.loop(0, 2 * outer)
    def _(i):
        for h in range(2):
            pcore[i, h] = (pcore[i, h].astype(F32) + pa[c, i, h].astype(F32)).astype(BF)

    heads.start()
    arrived(got_y, xr.at[1])
    spot = pl.ds(4 * (1 - y), 2)
    acc[spot] = acc[spot] + got_y[...].astype(F32)
    got_x[pl.ds(2, 2)] = acc[pl.ds(0, 2)].astype(BF)
    go(remote(got_x.at[pl.ds(2, 2)], got_z, xs.at[2], xr.at[2], earlier))
    go(remote(lo.at[1 - n], lo_out.at[n], xs.at[3], xr.at[3], other_n))
    lo_out[n] = lo[n]
    for d in mlp.order():
        mlp.to_first(d)
    for d in mlp.order():
        mlp.to_z(d)
    for d in heads.order():
        heads.to_first(d)
    for d in heads.order():
        heads.to_z(d)
    mlp.close()
    arrived(got_z, xr.at[2])
    xg[...] = (acc[pl.ds(4, 2)] + got_z[...].astype(F32)).astype(BF)
    heads.close()
    arrived(lo_out.at[1 - n], xr.at[3])
    core_copy.wait_send()
    for copy in sent:
        copy.wait_send()
    mlp.finish()
    heads.finish()


def leave(pm, pa, pg, lo):
    wide = lax.axis_size("wide")
    outer = wide // 2
    bm, ba, bx = pm.shape[2:], pa.shape[3:], lo.shape[1:]
    vmem = pl.BlockSpec(memory_space=pltpu.VMEM)
    return pl.pallas_call(
        functools.partial(leave_kernel, outer),
        out_shape=(
            jax.ShapeDtypeStruct((2,) + bm, F32),
            jax.ShapeDtypeStruct((2,) + ba, F32),
            jax.ShapeDtypeStruct((2,) + bx, BF),
            jax.ShapeDtypeStruct((2,) + bx, BF),
        ),
        in_specs=[vmem] * 4,
        out_specs=(vmem,) * 4,
        scratch_shapes=[
            pltpu.VMEM(pa.shape[1:], BF),
            pltpu.VMEM((6,) + bx, F32),
            pltpu.VMEM((5,) + bx, BF),
            pltpu.VMEM((2,) + bx, BF),
            pltpu.VMEM((2,) + bx, BF),
        ]
        + scatter_scratch(outer, bm)
        + scatter_scratch(outer, ba)
        + [DMA((4,)), DMA((4,)), DMA, DMA]
        + scatter_sems(outer)
        + scatter_sems(outer),
        compiler_params=pltpu.CompilerParams(
            collective_id=1, has_side_effects=True, vmem_limit_bytes=LIMIT
        ),
    )(pm, pa, pg, lo)


def dot(left, right, dims):
    return lax.dot_general(left, right, ((dims[0], dims[1]), ((), ())), preferred_element_type=F32)


NN = ((1,), (0,))
NT = ((1,), (1,))
TN = ((0,), (0,))


def spread(tail, rows, rem):
    extra = tail.shape[0]
    count = -(-rows // extra)
    return jnp.concatenate([tail[:, k * rem : (k + 1) * rem] for k in range(count)], 0)[:rows]


def squeezed(block, extra, main):
    rows, rem = block.shape
    count = -(-rows // extra)
    short = count * extra - rows
    if short:
        block = jnp.concatenate([block, jnp.zeros((short, rem), block.dtype)], 0)
    parts = [block[k * extra : (k + 1) * extra] for k in range(count)]
    if count * rem < main:
        parts.append(jnp.zeros((extra, main - count * rem), block.dtype))
    return jnp.concatenate(parts, 1)


def store_packed(ref, index, value, main, rem):
    rows = value.shape[0]
    for h in range(2):
        at = ref.at[(h,) + index]
        at[0:rows, :] = value[:, h * main : (h + 1) * main].astype(ref.dtype)
        low = value[:, 2 * main + h * rem : 2 * main + (h + 1) * rem]
        at[rows:, :] = squeezed(low, at.shape[0] - rows, main).astype(ref.dtype)


def gelu_and_slope(u):
    share = 0.5 * (1.0 + lax.erf(u * 0.7071067811865476))
    return u * share, share + u * (jnp.exp(-0.5 * u * u) * 0.3989422804014327)


def mlp_kernel(
    wide, fc, rem, low2, cot_in, gm, residual, normed2, scale2, gain2, bias_u, bias_d,
    pm, lo, grad_res, sums, up_sum,
    weights, grads, tails, cot, low2_all, acc, got, wsem, tsem, psem, qsem, xs, xr
):
    c, w, n = lax.axis_index("dp"), lax.axis_index("wide"), lax.axis_index("narrow")
    other = (1 - c, w, n)
    rows, width = low2.shape
    main = gm.shape[3]
    extra = gm.shape[2] - 2 * fc
    nf = wide * fc
    greet([other])
    mine, theirs = pl.ds(c * rows, rows), pl.ds((1 - c) * rows, rows)
    swap_low = remote(low2, low2_all.at[mine], xs.at[0], xr.at[0], other)
    swap_low.start()

    def weight_copies(i):
        out = []
        for h in range(2):
            for k in range(2):
                out.append(
                    pltpu.make_async_copy(
                        gm.at[i, h, pl.ds(k * fc, fc)],
                        weights.at[k, pl.ds(i * fc, fc), pl.ds(h * main, main)],
                        wsem.at[i, h, k],
                    )
                )
            out.append(pltpu.make_async_copy(gm.at[i, h, pl.ds(2 * fc, extra)], tails.at[i, h], tsem.at[i, h]))
        return out

    @pl.loop(0, wide)
    def _(i):
        for copy in weight_copies(i):
            copy.start()

    low2_all[mine] = low2[...]
    for k in range(2):
        span = slice(k * rows, (k + 1) * rows)
        for h in range(2):
            cot[span, h * main : (h + 1) * main] = cot_in[k, h, 0:rows, :]
        cot[span, 2 * main :] = jnp.concatenate(
            [spread(cot_in[k, h, rows:, :].astype(F32), rows, rem) for h in range(2)], 1
        ).astype(BF)

    @pl.loop(0, wide)
    def _(i):
        for copy in weight_copies(i):
            copy.wait()
        both = jnp.concatenate([spread(tails[i, h].astype(F32), 2 * fc, rem) for h in range(2)], 1).astype(BF)
        for k in range(2):
            weights[k, pl.ds(i * fc, fc), 2 * main :] = both[k * fc : (k + 1) * fc]

    acc[...] = jnp.zeros_like(acc)
    swap_low.wait_recv()

    def step(start, size):
        at = pl.ds(start, size)
        before = dot(low2_all[...], weights[0, at, :], NT) + bias_u[:, at]
        hidden, slope = gelu_and_slope(before)
        hidden = hidden.astype(BF)
        acc[0] += dot(hidden, weights[1, at, :], NN)
        grads[1, at, :] = dot(hidden, cot[...], TN).astype(BF)
        grad = dot(cot[...], weights[1, at, :], NT) * slope
        grad = grad.astype(BF)
        up_sum[:, at] = jnp.sum(grad.astype(F32), 0, keepdims=True)
        acc[1] += dot(grad, weights[0, at, :], NN)
        grads[0, at, :] = dot(grad, low2_all[...], TN).astype(BF)

    size = 256
    full = nf // size

    @pl.loop(0, full)
    def _(j):
        step(pl.multiple_of(j * size, size), size)

    if nf % size:
        step(full * size, nf % size)

    swap_acc = remote(acc.at[:, theirs], got, xs.at[1], xr.at[1], other)
    swap_acc.start()

    def grad_copies(i):
        out = []
        for h in range(2):
            for k in range(2):
                out.append(
                    pltpu.make_async_copy(
                        grads.at[k, pl.ds(i * fc, fc), pl.ds(h * main, main)],
                        pm.at[i, h, pl.ds(k * fc, fc)],
                        psem.at[i, h, k],
                    )
                )
        return out

    def tail_copies(i):
        return [
            pltpu.make_async_copy(tails.at[i, h], pm.at[i, h, pl.ds(2 * fc, extra)], qsem.at[i, h])
            for h in range(2)
        ]

    @pl.loop(0, wide)
    def _(i):
        for copy in grad_copies(i):
            copy.start()
        low = jnp.concatenate([grads[k, pl.ds(i * fc, fc), 2 * main :] for k in range(2)], 0).astype(F32)
        for h in range(2):
            tails[i, h] = squeezed(low[:, h * rem : (h + 1) * rem], extra, main).astype(BF)
        for copy in tail_copies(i):
            copy.start()

    swap_acc.wait_recv()
    result = residual[...] + (acc[0, mine] + got[0]) + bias_d[...]
    store_packed(lo, (), result, main, rem)
    grad_low2 = acc[1, mine] + got[1]
    scaled = grad_low2 * gain2[...]
    first = jnp.mean(scaled, 1, keepdims=True)
    second = jnp.mean(scaled * normed2[...], 1, keepdims=True)
    grad_out = cot[mine].astype(F32)
    total = grad_out + scale2[...] * (scaled - first - normed2[...] * second)
    grad_res[...] = total
    sums[0:1] = jnp.sum(grad_low2 * normed2[...], 0, keepdims=True)
    sums[1:2] = jnp.sum(grad_low2, 0, keepdims=True)
    sums[2:3] = jnp.sum(total.astype(BF).astype(F32), 0, keepdims=True)
    sums[3:4] = jnp.sum(grad_out, 0, keepdims=True)
    sums[4:8] = jnp.zeros((4, width), F32)

    @pl.loop(0, wide)
    def _(i):
        for copy in grad_copies(i) + tail_copies(i):
            copy.wait()

    swap_low.wait_send()
    swap_acc.wait_send()


def mlp(low2, cot_in, gm, residual, normed2, scale2, gain2, bias_u, bias_d, rem):
    wide = gm.shape[0]
    rows, width = low2.shape
    nf = bias_u.shape[1]
    fc = nf // wide
    main = gm.shape[3]
    extra = gm.shape[2] - 2 * fc
    vmem = pl.BlockSpec(memory_space=pltpu.VMEM)
    return pl.pallas_call(
        functools.partial(mlp_kernel, wide, fc, rem),
        out_shape=(
            jax.ShapeDtypeStruct(gm.shape, BF),
            jax.ShapeDtypeStruct((2,) + cot_in.shape[2:], BF),
            jax.ShapeDtypeStruct((rows, width), F32),
            jax.ShapeDtypeStruct((8, width), F32),
            jax.ShapeDtypeStruct((1, nf), F32),
        ),
        in_specs=[vmem, vmem, ANY] + [vmem] * 6,
        out_specs=(ANY, vmem, vmem, vmem, vmem),
        scratch_shapes=[
            pltpu.VMEM((2, nf, width), BF),
            pltpu.VMEM((2, nf, width), BF),
            pltpu.VMEM((wide, 2, extra, main), BF),
            pltpu.VMEM((2 * rows, width), BF),
            pltpu.VMEM((2 * rows, width), BF),
            pltpu.VMEM((2, 2 * rows, width), F32),
            pltpu.VMEM((2, rows, width), F32),
            DMA((wide, 2, 2)),
            DMA((wide, 2)),
            DMA((wide, 2, 2)),
            DMA((wide, 2)),
            DMA((2,)),
            DMA((2,)),
        ],
        compiler_params=pltpu.CompilerParams(
            collective_id=2, has_side_effects=True, vmem_limit_bytes=LIMIT
        ),
    )(low2, cot_in, gm, residual, normed2, scale2, gain2, bias_u, bias_d)


def fill_mask(q_seg, k_seg, mask):
    keys, queries = mask.shape
    key = lax.broadcasted_iota(jnp.int32, (keys, queries), 0)
    query = lax.broadcasted_iota(jnp.int32, (keys, queries), 1) + (keys - queries)
    allowed = (k_seg[...] == q_seg[...]) & (key <= query)
    mask[...] = jnp.where(allowed, 0.0, NEGATIVE)


def turned(block):
    return block.astype(F32).T


def attend_kernel(q, k, v, q_seg, k_seg, out, lse, mask):
    @pl.when(pl.program_id(0) == 0)
    def _():
        fill_mask(q_seg, k_seg, mask)

    q_t = turned(q[...]) * SCALE
    row = lax.broadcasted_iota(jnp.int32, q_t.shape, 0)
    parts = []
    lse[...] = jnp.zeros_like(lse)
    for h in range(2):
        mine = (row >= h * HEAD) & (row < (h + 1) * HEAD)
        q_h = jnp.where(mine, q_t, 0.0).astype(BF)
        s = dot(k[...], q_h, NN) + mask[...]
        top = jnp.max(s, 0, keepdims=True)
        p = jnp.exp(s - top)
        total = jnp.sum(p, 0, keepdims=True)
        p = (p * (1.0 / total)).astype(BF)
        parts.append(dot(v[...], p, TN)[h * HEAD : (h + 1) * HEAD])
        lse[0, pl.ds(h, 1), :] = top + jnp.log(total)
    out[...] = jnp.concatenate(parts, 0).T.astype(BF)


def attend(q, k, v, q_seg, k_seg):
    queries, width = q.shape
    keys = k.shape[0]
    pairs = width // LANES
    return pl.pallas_call(
        attend_kernel,
        grid=(pairs,),
        out_shape=(
            jax.ShapeDtypeStruct((queries, width), BF),
            jax.ShapeDtypeStruct((pairs, 8, queries), F32),
        ),
        in_specs=[
            pl.BlockSpec((queries, LANES), lambda i: (0, i)),
            pl.BlockSpec((keys, LANES), lambda i: (0, i)),
            pl.BlockSpec((keys, LANES), lambda i: (0, i)),
            pl.BlockSpec((1, queries), lambda i: (0, 0)),
            pl.BlockSpec((keys, 1), lambda i: (0, 0)),
        ],
        out_specs=(
            pl.BlockSpec((queries, LANES), lambda i: (0, i)),
            pl.BlockSpec((1, 8, queries), lambda i: (i, 0, 0)),
        ),
        scratch_shapes=[pltpu.VMEM((keys, queries), F32)],
        compiler_params=pltpu.CompilerParams(vmem_limit_bytes=LIMIT),
    )(q, k, v, q_seg, k_seg)


def attend_back_kernel(q, k, v, g, lse, q_seg, k_seg, dq, dk, dv, mask):
    @pl.when(pl.program_id(0) == 0)
    def _():
        fill_mask(q_seg, k_seg, mask)

    q_n = q[...].astype(F32) * SCALE
    g_n = g[...].astype(F32)
    q_t, g_t = q_n.T, g_n.T
    row = lax.broadcasted_iota(jnp.int32, q_t.shape, 0)
    lane = lax.broadcasted_iota(jnp.int32, q_n.shape, 1)
    parts = []
    dk_sum = dv_sum = None
    for h in range(2):
        in_row = (row >= h * HEAD) & (row < (h + 1) * HEAD)
        in_lane = (lane >= h * HEAD) & (lane < (h + 1) * HEAD)
        s = dot(k[...], jnp.where(in_row, q_t, 0.0).astype(BF), NN) + mask[...]
        p = jnp.exp(s - lse[0, pl.ds(h, 1), :])
        dp = dot(v[...], jnp.where(in_row, g_t, 0.0).astype(BF), NN)
        delta = jnp.sum(p * dp, 0, keepdims=True)
        ds = (p * (dp - delta)).astype(BF)
        one = dot(ds, jnp.where(in_lane, q_n, 0.0).astype(BF), NN)
        two = dot(p.astype(BF), jnp.where(in_lane, g_n, 0.0).astype(BF), NN)
        dk_sum = one if dk_sum is None else dk_sum + one
        dv_sum = two if dv_sum is None else dv_sum + two
        parts.append(dot(k[...], ds, TN)[h * HEAD : (h + 1) * HEAD] * SCALE)
    dq[...] = jnp.concatenate(parts, 0).T.astype(BF)
    dk[...] = dk_sum.astype(BF)
    dv[...] = dv_sum.astype(BF)


def attend_back(q, k, v, g, lse, q_seg, k_seg):
    queries, width = q.shape
    keys = k.shape[0]
    pairs = width // LANES
    few = pl.BlockSpec((queries, LANES), lambda i: (0, i))
    many = pl.BlockSpec((keys, LANES), lambda i: (0, i))
    return pl.pallas_call(
        attend_back_kernel,
        grid=(pairs,),
        out_shape=(
            jax.ShapeDtypeStruct((queries, width), BF),
            jax.ShapeDtypeStruct((keys, width), BF),
            jax.ShapeDtypeStruct((keys, width), BF),
        ),
        in_specs=[
            few,
            many,
            many,
            few,
            pl.BlockSpec((1, 8, queries), lambda i: (i, 0, 0)),
            pl.BlockSpec((1, queries), lambda i: (0, 0)),
            pl.BlockSpec((keys, 1), lambda i: (0, 0)),
        ],
        out_specs=(few, many, many),
        scratch_shapes=[pltpu.VMEM((keys, queries), F32)],
        compiler_params=pltpu.CompilerParams(vmem_limit_bytes=LIMIT),
    )(q, k, v, g, lse, q_seg, k_seg)


def norm_forward(values, gain, shift):
    mean = jnp.mean(values, 1, keepdims=True)
    centred = values - mean
    scale = lax.rsqrt(jnp.mean(centred * centred, 1, keepdims=True) + EPS)
    normed = centred * scale
    return normed, scale, (normed * gain + shift).astype(BF)


def norm_backward(grad, normed, scale, gain):
    scaled = grad * gain
    first = jnp.mean(scaled, 1, keepdims=True)
    second = jnp.mean(scaled * normed, 1, keepdims=True)
    back = scale * (scaled - first - normed * second)
    return back, jnp.sum(grad * normed, 0), jnp.sum(grad, 0)


def shards(
    layer_input,
    doc_segments,
    first_gain,
    first_shift,
    heads_weight,
    query_bias,
    value_bias,
    merge_weight,
    merge_bias,
    second_gain,
    second_shift,
    up_weight,
    up_bias,
    down_weight,
    down_bias,
    out_cotangent,
):
    parts = lax.axis_size("narrow")
    wide = lax.axis_size("wide")
    c, w, n = lax.axis_index("dp"), lax.axis_index("wide"), lax.axis_index("narrow")
    half = heads_weight.shape[0]
    width = half * parts
    padded = -(-width // LANES) * LANES
    cols = heads_weight.shape[2]
    units = up_weight.shape[1]
    hc, fc = cols // 2, up16(units // 2)
    short = fc - units // 2
    rows = layer_input.shape[0] // parts
    span = (REACH + 1) * rows

    by_half = heads_weight.transpose(1, 2, 0).reshape(3, 2, hc, half)
    heads_rows = lax.dynamic_index_in_dim(by_half, c, 1, False).reshape(3 * hc, half)
    merge_rows = lax.dynamic_slice_in_dim(merge_weight, c * hc, hc, 0)
    up_rows = lax.dynamic_slice_in_dim(up_weight, c * (units // 2), units // 2, 1).T
    down_rows = lax.dynamic_slice_in_dim(down_weight, c * (units // 2), units // 2, 0)
    up_rows = jnp.pad(up_rows, ((0, short), (0, 0)))
    down_rows = jnp.pad(down_rows, ((0, short), (0, 0)))
    line = lambda *v: jnp.pad(jnp.concatenate(v), (0, half - sum(e.shape[0] for e in v)))
    vectors = jnp.stack(
        [
            first_gain,
            first_shift,
            merge_bias,
            second_gain,
            second_shift,
            down_bias,
            line(query_bias, value_bias),
            line(up_bias),
        ]
    )
    vectors = jnp.pad(vectors, ((0, up16(4 * hc + 8) - 4 * hc - 8), (0, 0)))
    sa = jnp.concatenate([heads_rows, merge_rows, vectors], 0)
    rows_a = sa.shape[0]
    sm = jnp.concatenate([up_rows, down_rows], 0)
    xin = pack(layer_input.reshape(2, rows, half))
    cot_in = pack(out_cotangent.reshape(2, rows, half))

    x_all, cot_all, ga, gm = enter(xin, cot_in, pack(sa), pack(sm))

    x_all = lax.dynamic_slice_in_dim(x_all, n, REACH + 1, 1)
    x = join(x_all, rows, half).reshape(span, width).astype(F32)
    full_a = join(jnp.moveaxis(ga, 2, 0), rows_a, half)
    weight = full_a[:, :, : 3 * hc].reshape(2, wide, 3, hc, width).transpose(2, 1, 0, 3, 4)
    weight = jnp.pad(weight.reshape(3, width, width), ((0, 0), (0, padded - width), (0, 0)))
    merge = full_a[:, :, 3 * hc : 4 * hc].transpose(1, 0, 2, 3).reshape(width, width)
    merge = jnp.pad(merge, ((0, padded - width), (0, 0)))
    gain1, shift1, bias_m, gain2, shift2, bias_d = full_a[0, 0, 4 * hc : 4 * hc + 6].astype(F32)
    wide_rows = unpack_half(ga[0, :, 0], rows_a, half)[:, 4 * hc + 6 : 4 * hc + 8].astype(F32)
    bias_q = jnp.pad(wide_rows[:, 0, :cols].reshape(width), (0, padded - width))
    bias_v = jnp.pad(wide_rows[:, 0, cols : 2 * cols].reshape(width), (0, padded - width))
    bias_u = lax.dynamic_slice_in_dim(wide_rows[:, 1], c * (units // 2), units // 2, 1)
    bias_u = jnp.pad(bias_u, ((0, 0), (0, short))).reshape(1, wide * fc)
    x, weight, merge = lax.optimization_barrier((x, weight, merge))

    normed1, scale1, low1 = norm_forward(x, gain1, shift1)
    own = low1[span - rows :]
    query = (dot(own, weight[0], NT) + bias_q).astype(BF)
    key = dot(low1, weight[1], NT).astype(BF)
    value = (dot(low1, weight[2], NT) + bias_v).astype(BF)
    seg_row = lax.dynamic_index_in_dim(doc_segments, c, 0, keepdims=False)
    start = (w * parts + n) * rows
    key_pos = start - REACH * rows + jnp.arange(span, dtype=jnp.int32)
    ahead = jnp.concatenate([jnp.full((REACH * rows,), -1, jnp.int32), seg_row])
    k_seg = lax.dynamic_slice_in_dim(ahead, start, span, 0)[:, None]
    q_seg = lax.dynamic_slice_in_dim(seg_row, start, rows, 0)[None]
    mixed, lse = attend(query, key, value, q_seg, k_seg)
    residual = x[span - rows :] + dot(mixed, merge, NN) + bias_m
    normed2, scale2, low2 = norm_forward(residual, gain2, shift2)

    pm, lo, grad_residual, sums2, up_sum = mlp(
        low2, cot_all, gm, residual, normed2, scale2, gain2[None], bias_u, bias_d[None], half - widths(half)[0]
    )
    up_bias_grad = up_sum.reshape(wide, fc)[:, : units // 2]
    grad_branch = grad_residual.astype(BF)
    merge_grad = dot(mixed, grad_branch, TN)[:width]
    grad_mixed = dot(grad_branch, merge, NT).astype(BF)
    dq, dk, dv = attend_back(query, key, value, grad_mixed, lse, q_seg, k_seg)
    grad_low1 = dot(dk, weight[1], NN) + dot(dv, weight[2], NN)
    grad_low1 = grad_low1.at[span - rows :].add(dot(dq, weight[0], NN))
    back1, gain1_grad, shift1_grad = norm_backward(grad_low1, normed1, scale1, gain1)
    back1 = back1.at[span - rows :].add(grad_residual)
    heads_grad = jnp.stack(
        [dot(dq, own, TN)[:width], dot(dk, low1, TN)[:width], dot(dv, low1, TN)[:width]]
    )
    pa = jnp.concatenate(
        [
            heads_grad.reshape(3, wide, 2, hc, width).transpose(2, 1, 0, 3, 4).reshape(2, wide, 3 * hc, width),
            merge_grad.reshape(wide, 2, hc, width).transpose(1, 0, 2, 3),
        ],
        2,
    ).astype(BF)
    pa = jnp.pad(pa, ((0, 0), (0, 0), (0, up16(4 * hc) - 4 * hc), (0, 0)))
    pa = jnp.moveaxis(pack(halves(pa)), 0, 2)
    pg = pack(halves(back1.reshape(REACH + 1, rows, width).astype(BF)))

    mo, ao, xg, lo_out = leave(pm, pa, pg, lo)

    layer_output = unpack_half(lo_out, rows, half).reshape(2 * rows, half)
    input_grad = unpack_half(xg, rows, half).reshape(2 * rows, half)
    ao = unpack_half(ao, up16(4 * hc), half)
    heads_total = ao[:, : 3 * hc].reshape(2, 3, hc, half).transpose(3, 1, 0, 2).reshape(half, 3, cols)
    merge_total = ao[:, 3 * hc : 4 * hc].reshape(cols, half)
    mo = unpack_half(mo, 2 * fc, half)
    up_total = mo[:, : units // 2].reshape(units, half).T
    down_total = mo[:, fc : fc + units // 2].reshape(units, half)

    lines = jnp.stack(
        [
            gain1_grad,
            shift1_grad,
            sums2[2],
            sums2[0],
            sums2[1],
            sums2[3],
        ]
    )
    up_lines = jnp.where(jnp.arange(2)[:, None, None] == c, up_bias_grad[None], 0.0)
    lines, q_sum, v_sum, up_lines = lax.psum(
        (lines, jnp.sum(dq, 0, dtype=F32)[:width], jnp.sum(dv, 0, dtype=F32)[:width], up_lines),
        ("dp", "wide", "narrow"),
    )
    lines = lax.dynamic_index_in_dim(halves(lines), n, 0, False)
    query_total = lax.dynamic_slice_in_dim(q_sum, w * cols, cols, 0)
    value_total = lax.dynamic_slice_in_dim(v_sum, w * cols, cols, 0)
    up_bias_total = lax.dynamic_index_in_dim(up_lines, w, 1, False).reshape(units)
    return (
        layer_output,
        input_grad,
        lines[0],
        lines[1],
        heads_total,
        query_total,
        value_total,
        merge_total,
        lines[2],
        lines[3],
        lines[4],
        up_total,
        up_bias_total,
        down_total,
        lines[5],
    )


def solution(mesh):
    return jax.shard_map(
        shards,
        mesh=mesh,
        in_specs=(
            P(("dp", "wide"), "narrow"),
            P(),
            P("narrow"),
            P("narrow"),
            P("narrow", None, "wide"),
            P("wide"),
            P("wide"),
            P("wide", "narrow"),
            P("narrow"),
            P("narrow"),
            P("narrow"),
            P("narrow", "wide"),
            P("wide"),
            P("wide", "narrow"),
            P("narrow"),
            P(("dp", "wide"), "narrow"),
        ),
        out_specs=(
            P(("dp", "wide"), "narrow"),
            P(("dp", "wide"), "narrow"),
            P("narrow"),
            P("narrow"),
            P("narrow", None, "wide"),
            P("wide"),
            P("wide"),
            P("wide", "narrow"),
            P("narrow"),
            P("narrow"),
            P("narrow"),
            P("narrow", "wide"),
            P("wide"),
            P("wide", "narrow"),
            P("narrow"),
        ),
        check_vma=False,
    )
```

```python
import functools

import jax
import jax.numpy as jnp
from jax import lax
from jax.experimental import pallas as pl
from jax.experimental.pallas import tpu as pltpu
from jax.sharding import PartitionSpec as P

HEAD = 64
REACH = 4
EPS = 1e-05
NEGATIVE = -1e30
LANES = 128
BF = jnp.bfloat16
F32 = jnp.float32
MESH = pl.DeviceIdType.MESH
ANY = pl.BlockSpec(memory_space=pl.ANY)
DMA = pltpu.SemaphoreType.DMA
SCALE = HEAD ** (-0.5)
LIMIT = 60 * 1024 * 1024


def widths(half):
    main = half // LANES * LANES
    return main, half - main


def rem_rows(rows, half):
    main, rem = widths(half)
    return up16(-(-rows // (main // rem)))


def up16(rows):
    return -(-rows // 16) * 16


def pack(block, column=None):
    rows, half = block.shape[-2:]
    main, rem = widths(half)
    count = main // rem
    extra = rem_rows(rows, half)
    lead = block.shape[:-2]
    none = [(0, 0)] * len(lead)
    tail = jnp.pad(block[..., main:], none + [(0, count * extra - rows), (0, 0)])
    tail = jnp.swapaxes(tail.reshape(lead + (count, extra, rem)), -2, -3).reshape(lead + (extra, main))
    if column is not None:
        base, groups = column_base(rows, half), -(-rows // extra)
        column = jnp.pad(column, (0, groups * extra - rows)).reshape(groups, extra).T
        tail = jnp.concatenate([tail[:, :base], column, tail[:, base + groups :]], 1)
    return jnp.concatenate([block[..., :main], tail], -2)


def column_base(rows, half):
    return -(-rows // rem_rows(rows, half)) * widths(half)[1]


def column_of(block, rows, half):
    base, extra = column_base(rows, half), rem_rows(rows, half)
    groups = -(-rows // extra)
    tail = block[..., rows : rows + extra, base : base + groups]
    return jnp.swapaxes(tail, -1, -2).reshape(block.shape[:-2] + (groups * extra,))[..., :rows]


def unpack(block, rows, half):
    main, rem = widths(half)
    count = main // rem
    extra = rem_rows(rows, half)
    lead = block.shape[:-2]
    tail = block[..., rows : rows + extra, :].reshape(lead + (extra, count, rem))
    tail = jnp.swapaxes(tail, -2, -3).reshape(lead + (count * extra, rem))[..., :rows, :]
    return block[..., :rows, :], tail


def unpack_half(block, rows, half):
    return jnp.concatenate(unpack(block, rows, half), -1)


def join(blocks, rows, half):
    body, tail = unpack(blocks, rows, half)
    return jnp.concatenate([body[0], body[1], tail[0], tail[1]], -1)


def halves(full):
    half = full.shape[-1] // 2
    main, rem = widths(half)
    edge = 2 * main
    return jnp.stack(
        [
            jnp.concatenate([full[..., :main], full[..., edge : edge + rem]], -1),
            jnp.concatenate([full[..., main:edge], full[..., edge + rem :]], -1),
        ]
    )


def place():
    c, w, n = lax.axis_index("dp"), lax.axis_index("wide"), lax.axis_index("narrow")
    z, y = lax.div(w, 2), lax.rem(w, 2)
    first = (y + c * (1 - 2 * y), n + (1 - c) * (1 - 2 * n))
    second = (y + (1 - c) * (1 - 2 * y), n + c * (1 - 2 * n))
    return c, z, y, n, first, second


def wide_of(z, y):
    return z * 2 + y


def remote(src, dst, send, recv, device):
    return pltpu.make_async_remote_copy(
        src_ref=src, dst_ref=dst, send_sem=send, recv_sem=recv, device_id=device, device_id_type=MESH
    )


def greet(devices):
    barrier = pltpu.get_barrier_semaphore()
    for device in devices:
        pl.semaphore_signal(barrier, inc=1, device_id=device, device_id_type=MESH)
    pl.semaphore_wait(barrier, len(devices))


def partners(outer):
    c, z, y, n, _, _ = place()
    out = [(c, wide_of(lax.rem(z + d, outer), y), n) for d in range(1, outer)]
    out.append((c, wide_of(z, 1 - y), n))
    out.append((c, wide_of(z, y), 1 - n))
    out.append((1 - c, wide_of(z, y), n))
    return out


class Gather:
    def __init__(self, outer, src, out, both, first, second, sems):
        self.outer, self.src, self.out, self.both = outer, src, out, both
        self.first, self.second = first, second
        self.zs, self.zr, self.fs, self.fr, self.ss, self.sr, self.cs, self.cr, self.local = sems
        self.sent = []

    def block(self, z, y, n):
        c = lax.axis_index("dp")
        return self.out.at[c, wide_of(z, y), n] if self.both else self.out.at[wide_of(z, y), n]

    def go(self, copy):
        copy.start()
        self.sent.append(copy)

    def z_at(self, d):
        return lax.rem(place()[1] + self.outer - d, self.outer)

    def to_first(self, d, src):
        c, z, y, n, _, _ = place()
        first, second = self.first, self.second
        device = (c, wide_of(z, first[0]), first[1])
        self.go(remote(src, self.block(self.z_at(d), y, n), self.fs.at[d], self.fr.at[d], device))

    def to_second(self, d, src, k):
        c, z, y, n, _, _ = place()
        first, second = self.first, self.second
        device = (c, wide_of(z, second[0]), second[1])
        dst = self.block(self.z_at(d), y, n) if k == 0 else self.block(self.z_at(d), *first)
        i = k * self.outer + d
        self.go(remote(src, dst, self.ss.at[i], self.sr.at[i], device))

    def to_core(self, i, src, dst):
        if self.both:
            c, z, y, n, _, _ = place()
            self.go(remote(src, dst, self.cs.at[i], self.cr.at[i], (1 - c, wide_of(z, y), n)))

    def start(self):
        c, z, y, n, _, _ = place()
        first, second = self.first, self.second
        own = self.block(z, y, n)
        self.keep = pltpu.make_async_copy(self.src, own, self.local)
        self.keep.start()
        for d in range(1, self.outer):
            device = (c, wide_of(lax.rem(z + d, self.outer), y), n)
            self.go(remote(self.src, own, self.zs.at[d - 1], self.zr.at[d - 1], device))

    def start_rest(self):
        c, z, y, n, _, _ = place()
        own = self.block(z, y, n)
        self.to_first(0, self.src)
        self.to_second(0, self.src, 0)
        self.to_core(0, self.src, own)

    def arrived(self, dst, recv):
        c, z, y, n, _, _ = place()
        remote(dst, dst, recv, recv, (1 - c, wide_of(z, y), n)).wait_recv()

    def along_z(self, d):
        c, z, y, n, _, _ = place()
        first, second = self.first, self.second
        got = self.block(self.z_at(d), y, n)
        self.arrived(got, self.zr.at[d - 1])
        self.to_first(d, got)
        self.to_second(d, got, 0)
        self.to_core(d, got, got)

    def along_first(self, d):
        c, z, y, n, _, _ = place()
        first, second = self.first, self.second
        got = self.block(self.z_at(d), *first)
        self.arrived(got, self.fr.at[d])
        self.to_second(d, got, 1)
        self.to_core(self.outer + d, got, got)

    def along_second(self, d, k):
        c, z, y, n, _, _ = place()
        first, second = self.first, self.second
        got = self.block(self.z_at(d), *second) if k == 0 else self.block(self.z_at(d), 1 - y, 1 - n)
        i = k * self.outer + d
        self.arrived(got, self.sr.at[i])
        self.to_core(2 * self.outer + i, got, got)

    def finish(self):
        c, z, y, n, _, _ = place()
        first, second = self.first, self.second
        if self.both:
            spots = [(y, n), first, second, (1 - y, 1 - n)]
            for k, spot in enumerate(spots):
                for d in range(self.outer):
                    got = self.out.at[1 - c, wide_of(self.z_at(d), spot[0]), spot[1]]
                    self.arrived(got, self.cr.at[k * self.outer + d])
        self.keep.wait()
        for copy in self.sent:
            copy.wait_send()


def gather_sems(outer):
    return [
        DMA((outer,)),
        DMA((outer,)),
        DMA((outer,)),
        DMA((outer,)),
        DMA((2 * outer,)),
        DMA((2 * outer,)),
        DMA((4 * outer,)),
        DMA((4 * outer,)),
        DMA,
    ]


class Scatter:
    def __init__(self, outer, part, value, one, two, three, fin, sems):
        self.outer, self.part, self.value = outer, part, value
        self.one, self.two, self.three, self.fin = one, two, three, fin
        self.ss, self.sr, self.fs, self.fr, self.zs, self.zr, self.cs, self.cr = sems
        self.sent = []

    def go(self, copy):
        copy.start()
        self.sent.append(copy)

    def arrived(self, dst, recv):
        c, z, y, n, _, _ = place()
        remote(dst, dst, recv, recv, (1 - c, wide_of(z, y), n)).wait_recv()

    def z_at(self, d):
        return lax.rem(place()[1] + d, self.outer)

    def order(self):
        return [d for d in range(1, self.outer)] + [0]

    def start(self):
        c, z, y, n, first, second = place()
        device = (c, wide_of(z, second[0]), second[1])
        for k, spot in ((1, (1 - y, 1 - n)), (0, second)):
            for d in self.order():
                i = k * self.outer + d
                self.go(
                    remote(self.part(self.z_at(d), *spot), self.one.at[i], self.ss.at[i], self.sr.at[i], device)
                )

    def to_first(self, d):
        c, z, y, n, first, second = place()
        device = (c, wide_of(z, first[0]), first[1])
        i = self.outer + d
        own = self.value(self.z_at(d), *first)
        self.arrived(self.one.at[i], self.sr.at[i])
        self.one[i] = (self.one[i].astype(F32) + own.astype(F32)).astype(BF)
        self.go(remote(self.one.at[i], self.two.at[d], self.fs.at[d], self.fr.at[d], device))

    def to_z(self, d):
        c, z, y, n, first, second = place()
        own = self.value(self.z_at(d), y, n)
        self.arrived(self.one.at[d], self.sr.at[d])
        self.arrived(self.two.at[d], self.fr.at[d])
        half = (self.one[d].astype(F32) + own.astype(F32)).astype(BF).astype(F32)
        value = half + self.two[d].astype(F32)
        if d == 0:
            self.fin[c] = value
        else:
            self.one[d] = value.astype(BF)
            device = (c, wide_of(self.z_at(d), y), n)
            self.go(
                remote(self.one.at[d], self.three.at[d - 1], self.zs.at[d - 1], self.zr.at[d - 1], device)
            )

    def close(self):
        c, z, y, n, first, second = place()
        for d in range(1, self.outer):
            self.arrived(self.three.at[d - 1], self.zr.at[d - 1])
        value = self.fin[c]
        for d in range(1, self.outer):
            value = value + self.three[d - 1].astype(F32)
        self.fin[c] = value
        self.go(remote(self.fin.at[c], self.fin.at[c], self.cs, self.cr, (1 - c, wide_of(z, y), n)))

    def finish(self):
        c = lax.axis_index("dp")
        self.arrived(self.fin.at[1 - c], self.cr)
        for copy in self.sent:
            copy.wait_send()


def scatter_scratch(outer, block):
    return [
        pltpu.VMEM((2 * outer,) + block, BF),
        pltpu.VMEM((outer,) + block, BF),
        pltpu.VMEM((max(outer - 1, 1),) + block, BF),
    ]


def scatter_sems(outer):
    return [
        DMA((2 * outer,)),
        DMA((2 * outer,)),
        DMA((outer,)),
        DMA((outer,)),
        DMA((outer,)),
        DMA((outer,)),
        DMA,
        DMA,
    ]


def leave_kernel(
    outer, hc, rem, dq, dk, dv, low1, mixed, branch, sums, pg, lo,
    ao, xg, lo_out, vec_out,
    pa, pcore, full, edge, acc, got_x, got_z, got_y, a1, a2, a3, vx, vz, xs, xr, ccs, ccr, vs, vr, *sems
):
    c, z, y, n, first, second = place()
    me = wide_of(z, y)
    wide = 2 * outer
    greet(partners(outer))
    other_n = (c, me, 1 - n)
    other_y = (c, wide_of(z, 1 - y), n)
    other_c = (1 - c, me, n)
    earlier = (c, wide_of(lax.rem(z + outer - 1, outer), y), n)
    sent = []
    main = pa.shape[4]
    rows = dq.shape[0]
    span = dk.shape[0]
    cols = 2 * hc
    padded = dq.shape[1]
    block_rows = edge.shape[2]
    extra = pa.shape[3] - block_rows

    def go(copy):
        copy.start()
        sent.append(copy)

    def arrived(dst, recv):
        remote(dst, dst, recv, recv, other_c).wait_recv()

    def products(s, left, right):
        size = 256
        for begin in range(0, padded, size):
            stop = min(begin + size, padded)
            full[s, begin:stop, :] = dot(left[:, begin:stop], right, TN).astype(BF)

    go(remote(pg.at[1 - n], got_x, xs.at[0], xr.at[0], other_n))
    vx[0] = sums[...]
    go(remote(vx.at[0], vx.at[1], vs.at[0], vr.at[0], other_n))
    acc[...] = jnp.zeros_like(acc)
    for j in range(5):
        acc[n + j] = pg[n, j].astype(F32)
    products(3, mixed, branch[...])
    products(0, dq, low1[span - rows :, :])
    vx_sum = sums[...]
    arrived(vx.at[1], vr.at[0])
    vx_sum = vx_sum + vx[1]
    vx[2] = vx_sum
    go(remote(vx.at[2], vx.at[3], vs.at[1], vr.at[1], other_y))
    products(1, dk, low1[...])
    arrived(vx.at[3], vr.at[1])
    vx_sum = vx[2] + vx[3]
    vx[4] = vx_sum
    go(remote(vx.at[4], vx.at[5], vs.at[2], vr.at[2], other_c))
    arrived(got_x, xr.at[0])
    for j in range(5):
        acc[1 - n + j] = acc[1 - n + j] + got_x[j].astype(F32)
    got_x[pl.ds(0, 2)] = acc[pl.ds(2, 2)].astype(BF)
    go(remote(got_x.at[pl.ds(0, 2)], got_y, xs.at[1], xr.at[1], other_y))
    products(2, dv, low1[...])
    arrived(vx.at[5], vr.at[2])
    vz[z] = vx[4] + vx[5]
    for d in range(1, outer):
        device = (c, wide_of(lax.rem(z + d, outer), y), n)
        go(remote(vz.at[z], vz.at[z], vs.at[2 + d], vr.at[2 + d], device))

    def place_rows(half):
        for i in range(wide):
            for s in range(4):
                to = slice(s * hc, (s + 1) * hc)
                src = slice(i * cols, i * cols + hc)
                src = pl.ds(i * cols + half * hc, hc)
                for h in range(2):
                    pa[half, i, h, to, :] = full[s, src, h * main : (h + 1) * main]
                edge[half, i, to, :] = full[s, src, 2 * main :]
            if block_rows > 4 * hc:
                gap = slice(4 * hc, block_rows)
                for h in range(2):
                    pa[half, i, h, gap, :] = jnp.zeros((block_rows - 4 * hc, main), BF)
                edge[half, i, gap, :] = jnp.zeros((block_rows - 4 * hc, LANES), BF)
            low = edge[half, i].astype(F32)
            for h in range(2):
                pa[half, i, h, block_rows:, :] = squeezed(
                    low[:, h * rem : (h + 1) * rem], extra, main, low[:, 2 * rem : 2 * rem + 1]
                ).astype(BF)

    core_copies = [remote(pa.at[1 - c], pcore, ccs, ccr, other_c)]
    place_rows(0)
    place_rows(1)
    core_copies[0].start()
    arrived(got_y, xr.at[1])
    spot = pl.ds(4 * (1 - y), 2)
    acc[spot] = acc[spot] + got_y[...].astype(F32)
    got_x[pl.ds(2, 2)] = acc[pl.ds(0, 2)].astype(BF)
    go(remote(got_x.at[pl.ds(2, 2)], got_z, xs.at[2], xr.at[2], earlier))
    core_copies[0].wait_recv()

    @pl.loop(0, wide)
    def _(i):
        for h in range(2):
            pcore[i, h] = (pcore[i, h].astype(F32) + pa[c, i, h].astype(F32)).astype(BF)

    ref = lambda z, y, n: pcore.at[wide_of(z, y), n]
    heads = Scatter(outer, ref, lambda z, y, n: pcore[wide_of(z, y), n], a1, a2, a3, ao, sems)
    heads.start()
    go(remote(lo.at[1 - n], lo_out.at[n], xs.at[3], xr.at[3], other_n))
    lo_out[n] = lo[n]
    for d in heads.order():
        heads.to_first(d)
    for d in heads.order():
        heads.to_z(d)
    arrived(got_z, xr.at[2])
    xg[...] = (acc[pl.ds(4, 2)] + got_z[...].astype(F32)).astype(BF)
    for d in range(1, outer):
        arrived(vz.at[lax.rem(z + outer - d, outer)], vr.at[2 + d])
    total = vz[0]
    for i in range(1, outer):
        total = total + vz[i]
    vec_out[...] = total
    heads.close()
    arrived(lo_out.at[1 - n], xr.at[3])
    core_copies[0].wait_send()
    for copy in sent:
        copy.wait_send()
    heads.finish()


def leave(dq, dk, dv, low1, mixed, branch, sums, pg, lo, hc, rem):
    wide = lax.axis_size("wide")
    outer = wide // 2
    main = lo.shape[2]
    bx = lo.shape[1:]
    block_rows = up16(4 * hc)
    ba = (block_rows + rem_rows(block_rows, main + rem), main)
    padded = dq.shape[1]
    vmem = pl.BlockSpec(memory_space=pltpu.VMEM)
    return pl.pallas_call(
        functools.partial(leave_kernel, outer, hc, rem),
        out_shape=(
            jax.ShapeDtypeStruct((2,) + ba, F32),
            jax.ShapeDtypeStruct((2,) + bx, BF),
            jax.ShapeDtypeStruct((2,) + bx, BF),
            jax.ShapeDtypeStruct(sums.shape, F32),
        ),
        in_specs=[vmem] * 9,
        out_specs=(vmem,) * 4,
        scratch_shapes=[
            pltpu.VMEM((2, wide, 2) + ba, BF),
            pltpu.VMEM((wide, 2) + ba, BF),
            pltpu.VMEM((4, padded, padded), BF),
            pltpu.VMEM((2, wide, block_rows, LANES), BF),
            pltpu.VMEM((6,) + bx, F32),
            pltpu.VMEM((5,) + bx, BF),
            pltpu.VMEM((2,) + bx, BF),
            pltpu.VMEM((2,) + bx, BF),
        ]
        + scatter_scratch(outer, ba)
        + [pltpu.VMEM((6,) + sums.shape, F32), pltpu.VMEM((outer,) + sums.shape, F32)]
        + [DMA((4,)), DMA((4,)), DMA, DMA, DMA((2 + outer,)), DMA((2 + outer,))]
        + scatter_sems(outer),
        compiler_params=pltpu.CompilerParams(
            collective_id=1, has_side_effects=True, vmem_limit_bytes=LIMIT
        ),
    )(dq, dk, dv, low1, mixed, branch, sums, pg, lo)


def dot(left, right, dims):
    return lax.dot_general(left, right, ((dims[0], dims[1]), ((), ())), preferred_element_type=F32)


NN = ((1,), (0,))
NT = ((1,), (1,))
TN = ((0,), (0,))


def spread(tail, rows, rem):
    extra = tail.shape[0]
    count = -(-rows // extra)
    return jnp.concatenate([tail[:, k * rem : (k + 1) * rem] for k in range(count)], 0)[:rows]


def squeezed(block, extra, main, column=None):
    parts = []
    for piece in (block,) if column is None else (block, column):
        rows, each = piece.shape
        count = -(-rows // extra)
        short = count * extra - rows
        if short:
            piece = jnp.concatenate([piece, jnp.zeros((short, each), piece.dtype)], 0)
        parts += [piece[k * extra : (k + 1) * extra] for k in range(count)]
    used = sum(p.shape[1] for p in parts)
    if used < main:
        parts.append(jnp.zeros((extra, main - used), block.dtype))
    return jnp.concatenate(parts, 1)


def store_packed(ref, index, value, main, rem):
    rows = value.shape[0]
    for h in range(2):
        at = ref.at[(h,) + index]
        at[0:rows, :] = value[:, h * main : (h + 1) * main].astype(ref.dtype)
        low = value[:, 2 * main + h * rem : 2 * main + (h + 1) * rem]
        at[rows:, :] = squeezed(low, at.shape[0] - rows, main).astype(ref.dtype)


def gelu_and_slope(u):
    share = 0.5 * (1.0 + lax.erf(u * 0.7071067811865476))
    return u * share, share + u * (jnp.exp(-0.5 * u * u) * 0.3989422804014327)


def mlp_kernel(
    wide, fc, rem, low2, cot_in, gm, residual, vec,
    pm, lo, grad_res, sums,
    weights, grads, tails, cot, low2_all, acc, got, wsem, tsem, psem, qsem, xs, xr
):
    c, w, n = lax.axis_index("dp"), lax.axis_index("wide"), lax.axis_index("narrow")
    other = (1 - c, w, n)
    rows, padded = low2.shape
    main = gm.shape[3]
    width = 2 * (main + rem)
    extra = gm.shape[2] - 2 * fc
    nf = wide * fc
    base = -(-2 * fc // extra) * rem
    greet([other])
    mine, theirs = pl.ds(c * rows, rows), pl.ds((1 - c) * rows, rows)
    swap_low = remote(low2, low2_all.at[mine], xs.at[0], xr.at[0], other)
    swap_low.start()

    def weight_copies(i):
        out = []
        for h in range(2):
            for k in range(2):
                out.append(
                    pltpu.make_async_copy(
                        gm.at[i, h, pl.ds(k * fc, fc)],
                        weights.at[k, pl.ds(i * fc, fc), pl.ds(h * main, main)],
                        wsem.at[i, h, k],
                    )
                )
            out.append(pltpu.make_async_copy(gm.at[i, h, pl.ds(2 * fc, extra)], tails.at[i, h], tsem.at[i, h]))
        return out

    @pl.loop(0, wide)
    def _(i):
        for copy in weight_copies(i):
            copy.start()

    low2_all[mine] = low2[...]
    for k in range(2):
        span = slice(k * rows, (k + 1) * rows)
        for h in range(2):
            cot[span, h * main : (h + 1) * main] = cot_in[k, h, 0:rows, :]
        cot[span, 2 * main :] = edge_tile([cot_in[k, h, rows:, :] for h in range(2)], rows, rem)

    @pl.loop(0, wide)
    def _(i):
        for copy in weight_copies(i):
            copy.wait()
        both = edge_tile([tails[i, h] for h in range(2)], 2 * fc, rem, base)
        for k in range(2):
            weights[k, pl.ds(i * fc, fc), 2 * main :] = both[k * fc : (k + 1) * fc]

    acc[...] = jnp.zeros_like(acc)
    swap_low.wait_recv()

    def step(start, size):
        at = pl.ds(start, size)
        before = dot(low2_all[...], weights[0, at, :], NT)
        hidden, slope = gelu_and_slope(before)
        hidden = hidden.astype(BF)
        acc[0] += dot(hidden, weights[1, at, :], NN)
        grads[1, at, :] = dot(hidden, cot[...], TN).astype(BF)
        grad = dot(cot[...], weights[1, at, :], NT) * slope
        grad = grad.astype(BF)
        acc[1] += dot(grad, weights[0, at, :], NN)
        grads[0, at, :] = dot(grad, low2_all[...], TN).astype(BF)

    size = 256
    full = nf // size

    @pl.loop(0, full)
    def _(j):
        step(pl.multiple_of(j * size, size), size)

    if nf % size:
        step(full * size, nf % size)

    swap_acc = remote(acc.at[:, theirs], got, xs.at[1], xr.at[1], other)
    swap_acc.start()

    def grad_copies(i):
        out = []
        for h in range(2):
            for k in range(2):
                out.append(
                    pltpu.make_async_copy(
                        grads.at[k, pl.ds(i * fc, fc), pl.ds(h * main, main)],
                        pm.at[i, h, pl.ds(k * fc, fc)],
                        psem.at[i, h, k],
                    )
                )
        return out

    def tail_copies(i):
        return [
            pltpu.make_async_copy(tails.at[i, h], pm.at[i, h, pl.ds(2 * fc, extra)], qsem.at[i, h])
            for h in range(2)
        ]

    @pl.loop(0, wide)
    def _(i):
        for copy in grad_copies(i):
            copy.start()
        low = jnp.concatenate([grads[k, pl.ds(i * fc, fc), 2 * main :] for k in range(2)], 0).astype(F32)
        for h in range(2):
            tails[i, h] = squeezed(low[:, h * rem : (h + 1) * rem], extra, main, low[:, 2 * rem : 2 * rem + 1]).astype(BF)
        for copy in tail_copies(i):
            copy.start()

    swap_acc.wait_recv()
    result = residual[...] + (acc[0, mine] + got[0]) + vec[5:6]
    store_packed(lo, (), result, main, rem)
    normed2, scale2 = normed_rows(residual[...], width)
    grad_low2 = acc[1, mine] + got[1]
    grad_out = cot[mine].astype(F32)
    lane = lax.broadcasted_iota(jnp.int32, grad_out.shape, 1)
    total = jnp.where(lane < width, grad_out + norm_back(grad_low2, normed2, scale2, vec[3:4], width), 0.0)
    grad_res[...] = total
    sums[...] = jnp.zeros_like(sums)
    sums[2:3] = jnp.sum(total.astype(BF).astype(F32), 0, keepdims=True)
    sums[3:4] = jnp.sum(grad_low2 * normed2, 0, keepdims=True)
    sums[4:5] = jnp.sum(grad_low2, 0, keepdims=True)
    sums[5:6] = jnp.sum(grad_out, 0, keepdims=True)

    @pl.loop(0, wide)
    def _(i):
        for copy in grad_copies(i) + tail_copies(i):
            copy.wait()

    swap_low.wait_send()
    swap_acc.wait_send()


def mlp(low2, cot_in, gm, residual, vec, fc, rem):
    wide = gm.shape[0]
    rows, padded = low2.shape
    nf = wide * fc
    main = gm.shape[3]
    extra = gm.shape[2] - 2 * fc
    vmem = pl.BlockSpec(memory_space=pltpu.VMEM)
    return pl.pallas_call(
        functools.partial(mlp_kernel, wide, fc, rem),
        out_shape=(
            jax.ShapeDtypeStruct(gm.shape, BF),
            jax.ShapeDtypeStruct((2,) + cot_in.shape[2:], BF),
            jax.ShapeDtypeStruct((rows, padded), F32),
            jax.ShapeDtypeStruct((16, padded), F32),
        ),
        in_specs=[vmem, vmem, ANY, vmem, vmem],
        out_specs=(ANY, vmem, vmem, vmem),
        scratch_shapes=[
            pltpu.VMEM((2, nf, padded), BF),
            pltpu.VMEM((2, nf, padded), BF),
            pltpu.VMEM((wide, 2, extra, main), BF),
            pltpu.VMEM((2 * rows, padded), BF),
            pltpu.VMEM((2 * rows, padded), BF),
            pltpu.VMEM((2, 2 * rows, padded), F32),
            pltpu.VMEM((2, rows, padded), F32),
            DMA((wide, 2, 2)),
            DMA((wide, 2)),
            DMA((wide, 2, 2)),
            DMA((wide, 2)),
            DMA((2,)),
            DMA((2,)),
        ],
        compiler_params=pltpu.CompilerParams(
            collective_id=2, has_side_effects=True, vmem_limit_bytes=LIMIT
        ),
    )(low2, cot_in, gm, residual, vec)


def fill_mask(q_seg, k_seg, mask):
    keys, queries = mask.shape
    key = lax.broadcasted_iota(jnp.int32, (keys, queries), 0)
    query = lax.broadcasted_iota(jnp.int32, (keys, queries), 1) + (keys - queries)
    allowed = (k_seg[...] == q_seg[...]) & (key <= query)
    mask[...] = jnp.where(allowed, 0.0, NEGATIVE)


def turned(block):
    return block.astype(F32).T


def attend_pair(q, k, v, mask):
    q_t = turned(q) * SCALE
    row = lax.broadcasted_iota(jnp.int32, q_t.shape, 0)
    parts, logs = [], []
    for h in range(2):
        mine = (row >= h * HEAD) & (row < (h + 1) * HEAD)
        s = dot(k, jnp.where(mine, q_t, 0.0).astype(BF), NN) + mask[...]
        top = jnp.max(s, 0, keepdims=True)
        p = jnp.exp(s - top)
        total = jnp.sum(p, 0, keepdims=True)
        p = (p * (1.0 / total)).astype(BF)
        parts.append(dot(v, p, TN)[h * HEAD : (h + 1) * HEAD])
        logs.append(top + jnp.log(total))
    return jnp.concatenate(parts, 0).T.astype(BF), logs


def normed_rows(values, width):
    lane = lax.broadcasted_iota(jnp.int32, values.shape, 1)
    mean = jnp.sum(values, 1, keepdims=True) * (1.0 / width)
    centred = jnp.where(lane < width, values - mean, 0.0)
    scale = lax.rsqrt(jnp.sum(centred * centred, 1, keepdims=True) * (1.0 / width) + EPS)
    return centred * scale, scale


def norm_back(grad, normed, scale, gain, width):
    lane = lax.broadcasted_iota(jnp.int32, grad.shape, 1)
    scaled = jnp.where(lane < width, grad * gain, 0.0)
    first = jnp.sum(scaled, 1, keepdims=True) * (1.0 / width)
    second = jnp.sum(scaled * normed, 1, keepdims=True) * (1.0 / width)
    return scale * (scaled - first - normed * second)


def edge_tile(tails, rows, rem, base=None):
    tails = [t.astype(F32) for t in tails]
    parts = [spread(t, rows, rem) for t in tails]
    used = 2 * rem
    if base is not None:
        parts.append(spread(tails[0][:, base:], rows, 1))
        used += 1
    parts.append(jnp.zeros((rows, LANES - used), F32))
    return jnp.concatenate(parts, 1).astype(BF)


def forward_kernel(
    outer, hc, rem, xin, cot, sa, sm, q_seg, k_seg,
    cot_out, gm, wa_out, x_out, low1_out, k_out, v_out, q, mixed, lse, residual, low2, vec,
    ga, xs6, wa, x5, low1, k, v, mask, xs, xr, hs, hr, ks, kr, ls, os, *sems
):
    c, z, y, n, first, second = place()
    me = wide_of(z, y)
    wide = 2 * outer
    greet(partners(outer))
    other_n = (c, me, 1 - n)
    other_y = (c, wide_of(z, 1 - y), n)
    other_c = (1 - c, me, n)
    later = (c, wide_of(lax.rem(z + 1, outer), y), n)
    main = sa.shape[1]
    width = 2 * (main + rem)
    rows = q.shape[0]
    span = x5.shape[0]
    cols = 2 * hc
    sent = []

    def go(copy):
        copy.start()
        sent.append(copy)

    def arrived(dst, recv):
        remote(dst, dst, recv, recv, other_c).wait_recv()

    def x_send(j):
        src = xs6.at[n, j + 1 - n] if j < 4 else xin.at[1 - n]
        go(remote(src, xs6.at[n, j + 1 - n], hs.at[j], hr.at[j], other_n))

    own = xs6.at[n, pl.ds(4, 2)]
    keep = pltpu.make_async_copy(xin, own, ls.at[0])
    keep.start()
    keep_cot = pltpu.make_async_copy(cot.at[n], cot_out.at[c, n], ls.at[1])
    keep_cot.start()
    go(remote(xin, xs6.at[n, pl.ds(0, 2)], xs.at[0], xr.at[0], later))
    x_send(4)
    heads = Gather(outer, sa, ga, True, (y, 1 - n), (1 - y, n), sems[:9])
    heads.start()
    heads.start_rest()
    fill_mask(q_seg, k_seg, mask)
    wa[:, width:, :] = jnp.zeros((4, wa.shape[1] - width, wa.shape[2]), BF)
    arrived(xs6.at[n, pl.ds(0, 2)], xr.at[0])
    keep.wait()
    x_send(0)
    go(remote(xs6.at[n, pl.ds(4 * (1 - y), 2)], xs6.at[n, pl.ds(2, 2)], xs.at[1], xr.at[1], other_y))
    for d in range(1, outer):
        heads.along_z(d)
    feed = Gather(outer, sm, gm, False, first, second, sems[9:])
    feed.start()
    arrived(xs6.at[n, pl.ds(2, 2)], xr.at[1])
    for j in (1, 2, 3):
        x_send(j)
    for d in range(outer):
        heads.along_first(d)
    go(remote(cot.at[1 - n], cot_out.at[c, n], ks.at[0], kr.at[0], other_n))
    go(remote(cot.at[n], cot_out.at[c, n], ks.at[1], kr.at[1], other_c))
    feed.start_rest()

    for j in range(5):
        arrived(xs6.at[1 - n, j + n], hr.at[j])
    for j in range(5):
        at = slice(j * rows, (j + 1) * rows)
        for h in range(2):
            x5[at, h * main : (h + 1) * main] = xs6[h, n + j, 0:rows, :]
        x5[at, 2 * main :] = edge_tile([xs6[h, n + j, rows:, :] for h in range(2)], rows, rem)
    outs = [pltpu.make_async_copy(x5, x_out, os.at[0])]
    outs[0].start()
    for kk in range(2):
        for d in range(outer):
            heads.along_second(d, kk)
    heads.finish()
    for d in range(1, outer):
        feed.along_z(d)

    block_rows = 16 + up16(4 * hc)
    extra = ga.shape[3] - block_rows
    base = -(-block_rows // extra) * rem
    for i in range(wide):
        for half in range(2):
            edge = edge_tile([ga[half, i, h, block_rows:, :] for h in range(2)], block_rows, rem, base)
            for s in range(4):
                src = slice(s * hc, (s + 1) * hc)
                to = slice(i * cols + half * hc, i * cols + (half + 1) * hc)
                for h in range(2):
                    wa[s, to, h * main : (h + 1) * main] = ga[half, i, h, src, :]
                wa[s, to, 2 * main :] = edge[src]
            if i == 0 and half == 0:
                at = slice(block_rows - 16, block_rows)
                for h in range(2):
                    vec[:, h * main : (h + 1) * main] = ga[0, 0, h, at, :].astype(F32)
                vec[:, 2 * main :] = edge[at].astype(F32)
    outs.append(pltpu.make_async_copy(wa, wa_out, os.at[1]))
    outs[1].start()

    @pl.loop(0, span // rows)
    def _(j):
        at = pl.ds(pl.multiple_of(j * rows, rows), rows)
        normed, _ = normed_rows(x5[at, :].astype(F32), width)
        low1[at, :] = (normed * vec[0:1] + vec[1:2]).astype(BF)
        k[at, :] = dot(low1[at, :], wa[1], NT).astype(BF)
        v[at, :] = dot(low1[at, :], wa[2], NT).astype(BF)

    q[...] = dot(low1[span - rows :, :], wa[0], NT).astype(BF)
    for src, dst in ((low1, low1_out), (k, k_out), (v, v_out)):
        outs.append(pltpu.make_async_copy(src, dst, os.at[len(outs)]))
        outs[-1].start()

    pairs = q.shape[1] // LANES
    lse[...] = jnp.zeros_like(lse)

    def some(begin, end):
        @pl.loop(begin, end)
        def _(i):
            at = pl.ds(pl.multiple_of(i * LANES, LANES), LANES)
            out, logs = attend_pair(q[:, at], k[:, at], v[:, at], mask)
            mixed[:, at] = out
            for h in range(2):
                lse[i, pl.ds(h, 1), :] = logs[h]

    cut = pairs // 2
    some(0, cut)
    for d in range(outer):
        feed.along_first(d)
    arrived(cot_out.at[c, 1 - n], kr.at[0])
    go(remote(cot_out.at[c, 1 - n], cot_out.at[c, 1 - n], ks.at[2], kr.at[2], other_c))
    some(cut, pairs)
    value = x5[span - rows :, :].astype(F32) + dot(mixed[...], wa[3], NN) + vec[2:3]
    residual[...] = value
    normed, _ = normed_rows(value, width)
    low2[...] = (normed * vec[3:4] + vec[4:5]).astype(BF)

    for kk in range(2):
        for d in range(outer):
            feed.along_second(d, kk)
    arrived(cot_out.at[1 - c, n], kr.at[1])
    arrived(cot_out.at[1 - c, 1 - n], kr.at[2])
    keep_cot.wait()
    for copy in outs:
        copy.wait()
    for copy in sent:
        copy.wait_send()
    feed.finish()


def forward(xin, cot, sa, sm, q_seg, k_seg, hc, rem):
    wide = lax.axis_size("wide")
    outer = wide // 2
    main = sa.shape[1]
    width = 2 * (main + rem)
    padded = -(-(width + 1) // LANES) * LANES
    rows = q_seg.shape[1]
    span = k_seg.shape[0]
    pairs = padded // LANES
    vmem = pl.BlockSpec(memory_space=pltpu.VMEM)
    shape = jax.ShapeDtypeStruct
    return pl.pallas_call(
        functools.partial(forward_kernel, outer, hc, rem),
        out_shape=(
            shape((2,) + cot.shape, BF),
            shape((wide, 2) + sm.shape, BF),
            shape((4, padded, padded), BF),
            shape((span, padded), BF),
            shape((span, padded), BF),
            shape((span, padded), BF),
            shape((span, padded), BF),
            shape((rows, padded), BF),
            shape((rows, padded), BF),
            shape((pairs, 8, rows), F32),
            shape((rows, padded), F32),
            shape((rows, padded), BF),
            shape((16, padded), F32),
        ),
        in_specs=[ANY] * 4 + [vmem] * 2,
        out_specs=(ANY,) * 7 + (vmem,) * 6,
        scratch_shapes=[
            pltpu.VMEM((2, wide, 2) + sa.shape, BF),
            pltpu.VMEM((2, 6) + xin.shape[1:], BF),
            pltpu.VMEM((4, padded, padded), BF),
            pltpu.VMEM((span, padded), BF),
            pltpu.VMEM((span, padded), BF),
            pltpu.VMEM((span, padded), BF),
            pltpu.VMEM((span, padded), BF),
            pltpu.VMEM((span, rows), F32),
        ]
        + [DMA((2,)), DMA((2,)), DMA((5,)), DMA((5,)), DMA((3,)), DMA((3,)), DMA((2,)), DMA((5,))]
        + gather_sems(outer)
        + gather_sems(outer),
        compiler_params=pltpu.CompilerParams(
            collective_id=0, has_side_effects=True, vmem_limit_bytes=LIMIT
        ),
    )(xin, cot, sa, sm, q_seg, k_seg)


def attend_back_pair(q, k, v, g, lse, mask):
    q_n = q.astype(F32) * SCALE
    g_n = g.astype(F32)
    q_t, g_t = q_n.T, g_n.T
    row = lax.broadcasted_iota(jnp.int32, q_t.shape, 0)
    lane = lax.broadcasted_iota(jnp.int32, q_n.shape, 1)
    parts = []
    dk_sum = dv_sum = None
    for h in range(2):
        in_row = (row >= h * HEAD) & (row < (h + 1) * HEAD)
        in_lane = (lane >= h * HEAD) & (lane < (h + 1) * HEAD)
        s = dot(k, jnp.where(in_row, q_t, 0.0).astype(BF), NN) + mask[...]
        p = jnp.exp(s - lse[h : h + 1])
        dp = dot(v, jnp.where(in_row, g_t, 0.0).astype(BF), NN)
        delta = jnp.sum(p * dp, 0, keepdims=True)
        ds = (p * (dp - delta)).astype(BF)
        one = dot(ds, jnp.where(in_lane, q_n, 0.0).astype(BF), NN)
        two = dot(p.astype(BF), jnp.where(in_lane, g_n, 0.0).astype(BF), NN)
        dk_sum = one if dk_sum is None else dk_sum + one
        dv_sum = two if dv_sum is None else dv_sum + two
        parts.append(dot(k, ds, TN)[h * HEAD : (h + 1) * HEAD] * SCALE)
    return jnp.concatenate(parts, 0).T.astype(BF), dk_sum.astype(BF), dv_sum.astype(BF)


def backward_kernel(
    outer, rem, grad_res, q, lse, q_seg, k_seg, vec, sums_in, k_in, v_in, wa_in, x_in, pm,
    mo, dq, dk, dv, pg, branch, sums,
    w, k, v, x5, g, mask, stage, m1, m2, m3, ls, st, *sems
):
    greet(partners(outer))
    main = pm.shape[3]
    width = 2 * (main + rem)
    rows, padded = q.shape
    span = k.shape[0]

    def value(z, y, n):
        copy = pltpu.make_async_copy(pm.at[wide_of(z, y), n], stage, st)
        copy.start()
        copy.wait()
        return stage[...]

    feed = Scatter(outer, lambda z, y, n: pm.at[wide_of(z, y), n], value, m1, m2, m3, mo, sems)
    loads = [
        pltpu.make_async_copy(src, dst, ls.at[i])
        for i, (src, dst) in enumerate(
            (
                (wa_in.at[3], w.at[0]),
                (k_in, k),
                (v_in, v),
                (x_in, x5),
                (wa_in.at[1], w.at[1]),
                (wa_in.at[2], w.at[2]),
                (wa_in.at[0], w.at[0]),
            )
        )
    ]
    for copy in loads[:-1]:
        copy.start()
    feed.start()
    fill_mask(q_seg, k_seg, mask)
    branch[...] = grad_res[...].astype(BF)
    loads[0].wait()
    g[...] = dot(branch[...], w[0], NT).astype(BF)
    loads[-1].start()
    loads[1].wait()
    loads[2].wait()
    pairs = padded // LANES

    def some(begin, end):
        @pl.loop(begin, end)
        def _(i):
            at = pl.ds(pl.multiple_of(i * LANES, LANES), LANES)
            one, two, three = attend_back_pair(q[:, at], k[:, at], v[:, at], g[:, at], lse[i], mask)
            dq[:, at] = one
            dk[:, at] = two
            dv[:, at] = three

    order = feed.order()
    third, most = pairs // 3, len(order)
    some(0, third)
    for d in order[: most // 2]:
        feed.to_first(d)
    some(third, 2 * third)
    for d in order[most // 2 : most - 1]:
        feed.to_first(d)
    some(2 * third, pairs)
    for d in order[most - 1 :]:
        feed.to_first(d)
    for copy in loads[3:]:
        copy.wait()
    sums[...] = sums_in[...]

    def input_part(j, extra_part):
        at = pl.ds(j * rows, rows)
        grad = dot(dk[at, :], w[1], NN) + dot(dv[at, :], w[2], NN)
        if extra_part:
            grad = grad + dot(dq[...], w[0], NN)
        normed, scale = normed_rows(x5[at, :].astype(F32), width)
        sums[0:1] += jnp.sum(grad * normed, 0, keepdims=True)
        sums[1:2] += jnp.sum(grad, 0, keepdims=True)
        back = norm_back(grad, normed, scale, vec[0:1], width)
        if extra_part:
            back = back + grad_res[...]
        store_packed(pg, (j,), back, main, rem)

    @pl.loop(0, span // rows - 1)
    def _(j):
        input_part(j, False)

    input_part(span // rows - 1, True)
    for d in order:
        feed.to_z(d)
    feed.close()
    feed.finish()


def backward(grad_res, q, lse, q_seg, k_seg, vec, sums, k, v, wa, x5, pm, rem):
    wide = pm.shape[0]
    outer = wide // 2
    rows, padded = q.shape
    span = k.shape[0]
    main = pm.shape[3]
    block = pm.shape[2:]
    vmem = pl.BlockSpec(memory_space=pltpu.VMEM)
    shape = jax.ShapeDtypeStruct
    tokens = (rows + rem_rows(rows, main + rem), main)
    return pl.pallas_call(
        functools.partial(backward_kernel, outer, rem),
        out_shape=(
            shape((2,) + block, F32),
            shape((rows, padded), BF),
            shape((span, padded), BF),
            shape((span, padded), BF),
            shape((2, span // rows) + tokens, BF),
            shape((rows, padded), BF),
            shape(sums.shape, F32),
        ),
        in_specs=[vmem] * 7 + [ANY] * 5,
        out_specs=(vmem,) * 7,
        scratch_shapes=[
            pltpu.VMEM((3, padded, padded), BF),
            pltpu.VMEM((span, padded), BF),
            pltpu.VMEM((span, padded), BF),
            pltpu.VMEM((span, padded), BF),
            pltpu.VMEM((rows, padded), BF),
            pltpu.VMEM((span, rows), F32),
            pltpu.VMEM(block, BF),
        ]
        + scatter_scratch(outer, block)
        + [DMA((7,)), DMA]
        + scatter_sems(outer),
        compiler_params=pltpu.CompilerParams(
            collective_id=3, has_side_effects=True, vmem_limit_bytes=LIMIT
        ),
    )(grad_res, q, lse, q_seg, k_seg, vec, sums, k, v, wa, x5, pm)


def shards(
    layer_input,
    doc_segments,
    first_gain,
    first_shift,
    heads_weight,
    query_bias,
    value_bias,
    merge_weight,
    merge_bias,
    second_gain,
    second_shift,
    up_weight,
    up_bias,
    down_weight,
    down_bias,
    out_cotangent,
):
    parts = lax.axis_size("narrow")
    wide = lax.axis_size("wide")
    c, w, n = lax.axis_index("dp"), lax.axis_index("wide"), lax.axis_index("narrow")
    half = heads_weight.shape[0]
    width = half * parts
    padded = -(-width // LANES) * LANES
    cols = heads_weight.shape[2]
    units = up_weight.shape[1]
    hc, fc = cols // 2, up16(units // 2)
    short = fc - units // 2
    rows = layer_input.shape[0] // parts
    span = (REACH + 1) * rows

    by_half = heads_weight.transpose(1, 2, 0).reshape(3, 2, hc, half)
    heads_rows = lax.dynamic_index_in_dim(by_half, c, 1, False).reshape(3 * hc, half)
    merge_rows = lax.dynamic_slice_in_dim(merge_weight, c * hc, hc, 0)
    up_rows = lax.dynamic_slice_in_dim(up_weight, c * (units // 2), units // 2, 1).T
    down_rows = lax.dynamic_slice_in_dim(down_weight, c * (units // 2), units // 2, 0)
    up_rows = jnp.pad(up_rows, ((0, short), (0, 0)))
    down_rows = jnp.pad(down_rows, ((0, short), (0, 0)))
    line = lambda *v: jnp.pad(jnp.concatenate(v), (0, half - sum(e.shape[0] for e in v)))
    vectors = jnp.stack([first_gain, first_shift, merge_bias, second_gain, second_shift, down_bias])
    gap = up16(4 * hc) - 4 * hc
    sa = jnp.concatenate([heads_rows, merge_rows, jnp.zeros((gap, half), BF), vectors, jnp.zeros((10, half), BF)], 0)
    part = lambda v, size: lax.dynamic_slice_in_dim(v, c * size, size, 0)
    zero = lambda size: jnp.zeros((size,), BF)
    unit = jnp.array([0, 1, 0, 0, 1, 0], BF)
    column_a = jnp.concatenate(
        [part(query_bias, hc), zero(hc), part(value_bias, hc), zero(hc + gap), unit, zero(10)]
    )
    sm = jnp.concatenate([up_rows, down_rows], 0)
    column_m = jnp.concatenate([part(up_bias, units // 2), zero(short + fc)])
    xin = pack(layer_input.reshape(2, rows, half))
    cot_in = pack(out_cotangent.reshape(2, rows, half))
    seg_row = lax.dynamic_index_in_dim(doc_segments, c, 0, keepdims=False)
    start = (w * parts + n) * rows
    ahead = jnp.concatenate([jnp.full((REACH * rows,), -1, jnp.int32), seg_row])
    k_seg = lax.dynamic_slice_in_dim(ahead, start, span, 0)[:, None]
    q_seg = lax.dynamic_slice_in_dim(seg_row, start, rows, 0)[None]

    rem = widths(half)[1]
    cot_all, gm, wa, x5, low1, key, value, query, mixed, lse, residual, low2, vec = forward(
        xin, cot_in, pack(sa, column_a), pack(sm, column_m), q_seg, k_seg, hc, rem
    )
    pm, lo, grad_residual, sums = mlp(low2, cot_all, gm, residual, vec, fc, rem)

    mo, dq, dk, dv, pg, branch, sums = backward(
        grad_residual, query, lse, q_seg, k_seg, vec, sums, key, value, wa, x5, pm, rem
    )
    ao, xg, lo_out, sums = leave(dq, dk, dv, low1, mixed, branch, sums, pg, lo, hc, rem)

    layer_output = unpack_half(lo_out, rows, half).reshape(2 * rows, half)
    input_grad = unpack_half(xg, rows, half).reshape(2 * rows, half)
    biases = column_of(ao, up16(4 * hc), half)
    ao = unpack_half(ao, up16(4 * hc), half)
    heads_total = ao[:, : 3 * hc].reshape(2, 3, hc, half).transpose(3, 1, 0, 2).reshape(half, 3, cols)
    merge_total = ao[:, 3 * hc : 4 * hc].reshape(cols, half)
    up_bias_total = column_of(mo, 2 * fc, half)[:, : units // 2].reshape(units)
    mo = unpack_half(mo, 2 * fc, half)
    up_total = mo[:, : units // 2].reshape(units, half).T
    down_total = mo[:, fc : fc + units // 2].reshape(units, half)

    lines = lax.dynamic_index_in_dim(halves(sums[:6, :width]), n, 0, False)
    query_total = biases[:, :hc].reshape(cols)
    value_total = biases[:, 2 * hc : 3 * hc].reshape(cols)
    return (
        layer_output,
        input_grad,
        lines[0],
        lines[1],
        heads_total,
        query_total,
        value_total,
        merge_total,
        lines[2],
        lines[3],
        lines[4],
        up_total,
        up_bias_total,
        down_total,
        lines[5],
    )


def solution(mesh):
    return jax.shard_map(
        shards,
        mesh=mesh,
        in_specs=(
            P(("dp", "wide"), "narrow"),
            P(),
            P("narrow"),
            P("narrow"),
            P("narrow", None, "wide"),
            P("wide"),
            P("wide"),
            P("wide", "narrow"),
            P("narrow"),
            P("narrow"),
            P("narrow"),
            P("narrow", "wide"),
            P("wide"),
            P("wide", "narrow"),
            P("narrow"),
            P(("dp", "wide"), "narrow"),
        ),
        out_specs=(
            P(("dp", "wide"), "narrow"),
            P(("dp", "wide"), "narrow"),
            P("narrow"),
            P("narrow"),
            P("narrow", None, "wide"),
            P("wide"),
            P("wide"),
            P("wide", "narrow"),
            P("narrow"),
            P("narrow"),
            P("narrow"),
            P("narrow", "wide"),
            P("wide"),
            P("wide", "narrow"),
            P("narrow"),
        ),
        check_vma=False,
    )
```

```python
import functools

import jax
import jax.numpy as jnp
from jax import lax
from jax.experimental import pallas as pl
from jax.experimental.pallas import tpu as pltpu
from jax.sharding import PartitionSpec as P

HEAD = 64
REACH = 4
EPS = 1e-05
NEGATIVE = -1e30
LANES = 128
BF = jnp.bfloat16
F32 = jnp.float32
MESH = pl.DeviceIdType.MESH
ANY = pl.BlockSpec(memory_space=pl.ANY)
DMA = pltpu.SemaphoreType.DMA
SCALE = HEAD ** (-0.5)
LIMIT = 62 * 1024 * 1024


def widths(half):
    main = half // LANES * LANES
    return main, half - main


def rem_rows(rows, half):
    main, rem = widths(half)
    return up16(-(-rows // (main // rem)))


def up16(rows):
    return -(-rows // 16) * 16


def pack(block, column=None):
    rows, half = block.shape[-2:]
    main, rem = widths(half)
    count = main // rem
    extra = rem_rows(rows, half)
    lead = block.shape[:-2]
    none = [(0, 0)] * len(lead)
    tail = jnp.pad(block[..., main:], none + [(0, count * extra - rows), (0, 0)])
    tail = jnp.swapaxes(tail.reshape(lead + (count, extra, rem)), -2, -3).reshape(lead + (extra, main))
    if column is not None:
        base, groups = column_base(rows, half), -(-rows // extra)
        column = jnp.pad(column, (0, groups * extra - rows)).reshape(groups, extra).T
        tail = jnp.concatenate([tail[:, :base], column, tail[:, base + groups :]], 1)
    return jnp.concatenate([block[..., :main], tail], -2)


def column_base(rows, half):
    return -(-rows // rem_rows(rows, half)) * widths(half)[1]


def column_of(block, rows, half):
    base, extra = column_base(rows, half), rem_rows(rows, half)
    groups = -(-rows // extra)
    tail = block[..., rows : rows + extra, base : base + groups]
    return jnp.swapaxes(tail, -1, -2).reshape(block.shape[:-2] + (groups * extra,))[..., :rows]


def unpack(block, rows, half):
    main, rem = widths(half)
    count = main // rem
    extra = rem_rows(rows, half)
    lead = block.shape[:-2]
    tail = block[..., rows : rows + extra, :].reshape(lead + (extra, count, rem))
    tail = jnp.swapaxes(tail, -2, -3).reshape(lead + (count * extra, rem))[..., :rows, :]
    return block[..., :rows, :], tail


def unpack_half(block, rows, half):
    return jnp.concatenate(unpack(block, rows, half), -1)


def join(blocks, rows, half):
    body, tail = unpack(blocks, rows, half)
    return jnp.concatenate([body[0], body[1], tail[0], tail[1]], -1)


def halves(full):
    half = full.shape[-1] // 2
    main, rem = widths(half)
    edge = 2 * main
    return jnp.stack(
        [
            jnp.concatenate([full[..., :main], full[..., edge : edge + rem]], -1),
            jnp.concatenate([full[..., main:edge], full[..., edge + rem :]], -1),
        ]
    )


def place():
    c, w, n = lax.axis_index("dp"), lax.axis_index("wide"), lax.axis_index("narrow")
    z, y = lax.div(w, 2), lax.rem(w, 2)
    first = (y + c * (1 - 2 * y), n + (1 - c) * (1 - 2 * n))
    second = (y + (1 - c) * (1 - 2 * y), n + c * (1 - 2 * n))
    return c, z, y, n, first, second


def wide_of(z, y):
    return z * 2 + y


def remote(src, dst, send, recv, device):
    return pltpu.make_async_remote_copy(
        src_ref=src, dst_ref=dst, send_sem=send, recv_sem=recv, device_id=device, device_id_type=MESH
    )


def greet(devices):
    barrier = pltpu.get_barrier_semaphore()
    for device in devices:
        pl.semaphore_signal(barrier, inc=1, device_id=device, device_id_type=MESH)
    pl.semaphore_wait(barrier, len(devices))


def partners(outer):
    c, z, y, n, _, _ = place()
    out = [(c, wide_of(lax.rem(z + d, outer), y), n) for d in range(1, outer)]
    out.append((c, wide_of(z, 1 - y), n))
    out.append((c, wide_of(z, y), 1 - n))
    out.append((1 - c, wide_of(z, y), n))
    return out


class Gather:
    def __init__(self, outer, src, out, both, first, second, sems):
        self.outer, self.src, self.out, self.both = outer, src, out, both
        self.first, self.second = first, second
        self.zs, self.zr, self.fs, self.fr, self.ss, self.sr, self.cs, self.cr, self.local = sems
        self.sent = []

    def block(self, z, y, n):
        c = lax.axis_index("dp")
        return self.out.at[c, wide_of(z, y), n] if self.both else self.out.at[wide_of(z, y), n]

    def go(self, copy):
        copy.start()
        self.sent.append(copy)

    def z_at(self, d):
        return lax.rem(place()[1] + self.outer - d, self.outer)

    def to_first(self, d, src):
        c, z, y, n, _, _ = place()
        first, second = self.first, self.second
        device = (c, wide_of(z, first[0]), first[1])
        self.go(remote(src, self.block(self.z_at(d), y, n), self.fs.at[d], self.fr.at[d], device))

    def to_second(self, d, src, k):
        c, z, y, n, _, _ = place()
        first, second = self.first, self.second
        device = (c, wide_of(z, second[0]), second[1])
        dst = self.block(self.z_at(d), y, n) if k == 0 else self.block(self.z_at(d), *first)
        i = k * self.outer + d
        self.go(remote(src, dst, self.ss.at[i], self.sr.at[i], device))

    def to_core(self, i, src, dst):
        if self.both:
            c, z, y, n, _, _ = place()
            self.go(remote(src, dst, self.cs.at[i], self.cr.at[i], (1 - c, wide_of(z, y), n)))

    def start(self):
        c, z, y, n, _, _ = place()
        first, second = self.first, self.second
        own = self.block(z, y, n)
        self.keep = pltpu.make_async_copy(self.src, own, self.local)
        self.keep.start()
        for d in range(1, self.outer):
            device = (c, wide_of(lax.rem(z + d, self.outer), y), n)
            self.go(remote(self.src, own, self.zs.at[d - 1], self.zr.at[d - 1], device))

    def start_rest(self):
        c, z, y, n, _, _ = place()
        own = self.block(z, y, n)
        self.to_first(0, self.src)
        self.to_second(0, self.src, 0)
        self.to_core(0, self.src, own)

    def arrived(self, dst, recv):
        c, z, y, n, _, _ = place()
        remote(dst, dst, recv, recv, (1 - c, wide_of(z, y), n)).wait_recv()

    def along_z(self, d):
        c, z, y, n, _, _ = place()
        first, second = self.first, self.second
        got = self.block(self.z_at(d), y, n)
        self.arrived(got, self.zr.at[d - 1])
        self.to_first(d, got)
        self.to_second(d, got, 0)
        self.to_core(d, got, got)

    def along_first(self, d):
        c, z, y, n, _, _ = place()
        first, second = self.first, self.second
        got = self.block(self.z_at(d), *first)
        self.arrived(got, self.fr.at[d])
        self.to_second(d, got, 1)
        self.to_core(self.outer + d, got, got)

    def along_second(self, d, k):
        c, z, y, n, _, _ = place()
        first, second = self.first, self.second
        got = self.block(self.z_at(d), *second) if k == 0 else self.block(self.z_at(d), 1 - y, 1 - n)
        i = k * self.outer + d
        self.arrived(got, self.sr.at[i])
        self.to_core(2 * self.outer + i, got, got)

    def finish(self):
        c, z, y, n, _, _ = place()
        first, second = self.first, self.second
        if self.both:
            spots = [(y, n), first, second, (1 - y, 1 - n)]
            for k, spot in enumerate(spots):
                for d in range(self.outer):
                    got = self.out.at[1 - c, wide_of(self.z_at(d), spot[0]), spot[1]]
                    self.arrived(got, self.cr.at[k * self.outer + d])
        self.keep.wait()
        for copy in self.sent:
            copy.wait_send()


def gather_sems(outer):
    return [
        DMA((outer,)),
        DMA((outer,)),
        DMA((outer,)),
        DMA((outer,)),
        DMA((2 * outer,)),
        DMA((2 * outer,)),
        DMA((4 * outer,)),
        DMA((4 * outer,)),
        DMA,
    ]


class Scatter:
    def __init__(self, outer, first, second, part, one, two, three, fin, sems):
        self.outer, self.part, self.first, self.second = outer, part, first, second
        self.one, self.two, self.three, self.fin = one, two, three, fin
        self.ss, self.sr, self.fs, self.fr, self.zs, self.zr, self.cs, self.cr = sems
        self.sent, self.along_first = [], {}

    def go(self, copy):
        copy.start()
        self.sent.append(copy)

    def arrived(self, dst, recv):
        c, z, y, n, _, _ = place()
        remote(dst, dst, recv, recv, (1 - c, wide_of(z, y), n)).wait_recv()

    def z_at(self, d):
        return lax.rem(place()[1] + d, self.outer)

    def order(self):
        return [d for d in range(1, self.outer)] + [0]

    def start(self, begin=0, end=None):
        c, z, y, n, _, _ = place()
        first, second = self.first, self.second
        device = (c, wide_of(z, second[0]), second[1])
        for d in self.order()[begin:end]:
            for k, spot in ((1, (1 - y, 1 - n)), (0, second)):
                i = k * self.outer + d
                self.go(
                    remote(self.part(self.z_at(d), *spot), self.one.at[i], self.ss.at[i], self.sr.at[i], device)
                )

    def steps(self):
        order = self.order()
        out = [functools.partial(self.to_first, order[0])]
        for here, there in zip(order[1:], order):
            out.append(functools.partial(self.to_first, here))
            out.append(functools.partial(self.to_z, there))
        return out + [functools.partial(self.to_z, order[-1])]

    def read(self, *refs):
        return [ref[...].astype(F32) for ref in refs]

    def to_first(self, d):
        c, z, y, n, _, _ = place()
        first, second = self.first, self.second
        device = (c, wide_of(z, first[0]), first[1])
        i = self.outer + d
        self.arrived(self.one.at[i], self.sr.at[i])
        own, got = self.read(self.part(self.z_at(d), *first), self.one.at[i])
        src = self.for_first(d)
        src[...] = (got + own).astype(BF)
        self.along_first[d] = remote(src, self.two.at[d], self.fs.at[d], self.fr.at[d], device)
        self.go(self.along_first[d])

    def for_first(self, d):
        return self.one.at[self.outer + d]

    def for_z(self, d):
        return self.one.at[d]

    def to_z(self, d):
        c, z, y, n, _, _ = place()
        self.arrived(self.one.at[d], self.sr.at[d])
        self.arrived(self.two.at[d], self.fr.at[d])
        own, one, two = self.read(self.part(self.z_at(d), y, n), self.one.at[d], self.two.at[d])
        value = (one + own).astype(BF).astype(F32) + two
        if d == 0:
            self.fin[c] = value
        else:
            src = self.for_z(d)
            src[...] = value.astype(BF)
            device = (c, wide_of(self.z_at(d), y), n)
            self.go(remote(src, self.three.at[d - 1], self.zs.at[d - 1], self.zr.at[d - 1], device))

    def close(self):
        c, z, y, n, _, _ = place()
        for d in range(1, self.outer):
            self.arrived(self.three.at[d - 1], self.zr.at[d - 1])
        value = self.fin[c]
        for d in range(1, self.outer):
            value = value + self.read(self.three.at[d - 1])[0]
        self.fin[c] = value
        self.go(remote(self.fin.at[c], self.fin.at[c], self.cs, self.cr, (1 - c, wide_of(z, y), n)))

    def finish(self):
        c = lax.axis_index("dp")
        self.arrived(self.fin.at[1 - c], self.cr)
        for copy in self.sent:
            copy.wait_send()


class StagedScatter(Scatter):
    def stage(self, buffers, sems, firsts):
        self.buffers, self.load_sems, self.firsts = buffers, sems, firsts

    def read(self, *refs):
        copies = [
            pltpu.make_async_copy(ref, self.buffers.at[i], self.load_sems.at[i]) for i, ref in enumerate(refs)
        ]
        for copy in copies:
            copy.start()
        for copy in copies:
            copy.wait()
        return [self.buffers[i].astype(F32) for i in range(len(refs))]

    def for_first(self, d):
        return self.firsts.at[d]

    def for_z(self, d):
        slot = self.firsts.at[d]
        copy = self.along_first.pop(d)
        copy.wait_send()
        self.sent = [e for e in self.sent if e is not copy]
        return slot


def scatter_scratch(outer, block):
    return [
        pltpu.VMEM((2 * outer,) + block, BF),
        pltpu.VMEM((outer,) + block, BF),
        pltpu.VMEM((max(outer - 1, 1),) + block, BF),
    ]


def scatter_sems(outer):
    return [
        DMA((2 * outer,)),
        DMA((2 * outer,)),
        DMA((outer,)),
        DMA((outer,)),
        DMA((outer,)),
        DMA((outer,)),
        DMA,
        DMA,
    ]


def dot(left, right, dims):
    return lax.dot_general(left, right, ((dims[0], dims[1]), ((), ())), preferred_element_type=F32)


NN = ((1,), (0,))
NT = ((1,), (1,))
TN = ((0,), (0,))


def spread(tail, rows, rem):
    extra = tail.shape[0]
    count = -(-rows // extra)
    return jnp.concatenate([tail[:, k * rem : (k + 1) * rem] for k in range(count)], 0)[:rows]


def squeezed(block, extra, main, column=None):
    parts = []
    for piece in (block,) if column is None else (block, column):
        rows, each = piece.shape
        count = -(-rows // extra)
        short = count * extra - rows
        if short:
            piece = jnp.concatenate([piece, jnp.zeros((short, each), piece.dtype)], 0)
        parts += [piece[k * extra : (k + 1) * extra] for k in range(count)]
    used = sum(p.shape[1] for p in parts)
    if used < main:
        parts.append(jnp.zeros((extra, main - used), block.dtype))
    return jnp.concatenate(parts, 1)


def store_packed(ref, index, value, main, rem):
    rows = value.shape[0]
    for h in range(2):
        at = ref.at[(h,) + index]
        at[0:rows, :] = value[:, h * main : (h + 1) * main].astype(ref.dtype)
        low = value[:, 2 * main + h * rem : 2 * main + (h + 1) * rem]
        at[rows:, :] = squeezed(low, at.shape[0] - rows, main).astype(ref.dtype)


def gelu_and_slope(u):
    share = 0.5 * (1.0 + lax.erf(u * 0.7071067811865476))
    return u * share, share + u * (jnp.exp(-0.5 * u * u) * 0.3989422804014327)


def mlp_kernel(
    wide, fc, rem, low2, cot_in, gm, residual, vec,
    pm, lo, grad_res, sums,
    weights, grads, tails, cot, low2_all, acc, got, wsem, tsem, psem, qsem, xs, xr
):
    c, w, n = lax.axis_index("dp"), lax.axis_index("wide"), lax.axis_index("narrow")
    other = (1 - c, w, n)
    rows, padded = low2.shape
    main = gm.shape[3]
    width = 2 * (main + rem)
    extra = gm.shape[2] - 2 * fc
    nf = wide * fc
    base = -(-2 * fc // extra) * rem
    greet([other])
    mine, theirs = pl.ds(c * rows, rows), pl.ds((1 - c) * rows, rows)
    swap_low = remote(low2, low2_all.at[mine], xs.at[0], xr.at[0], other)
    swap_low.start()

    def weight_copies(i):
        out = []
        for h in range(2):
            for k in range(2):
                out.append(
                    pltpu.make_async_copy(
                        gm.at[i, h, pl.ds(k * fc, fc)],
                        weights.at[k, pl.ds(i * fc, fc), pl.ds(h * main, main)],
                        wsem.at[i, h, k],
                    )
                )
            out.append(pltpu.make_async_copy(gm.at[i, h, pl.ds(2 * fc, extra)], tails.at[i, h], tsem.at[i, h]))
        return out

    @pl.loop(0, wide)
    def _(i):
        for copy in weight_copies(i):
            copy.start()

    low2_all[mine] = low2[...]
    for k in range(2):
        span = slice(k * rows, (k + 1) * rows)
        for h in range(2):
            cot[span, h * main : (h + 1) * main] = cot_in[k, h, 0:rows, :]
        cot[span, 2 * main :] = edge_tile([cot_in[k, h, rows:, :] for h in range(2)], rows, rem)

    @pl.loop(0, wide)
    def _(i):
        for copy in weight_copies(i):
            copy.wait()
        both = edge_tile([tails[i, h] for h in range(2)], 2 * fc, rem, base)
        for k in range(2):
            weights[k, pl.ds(i * fc, fc), 2 * main :] = both[k * fc : (k + 1) * fc]

    acc[...] = jnp.zeros_like(acc)
    swap_low.wait_recv()

    def step(start, size):
        at = pl.ds(start, size)
        before = dot(low2_all[...], weights[0, at, :], NT)
        hidden, slope = gelu_and_slope(before)
        hidden = hidden.astype(BF)
        acc[0] += dot(hidden, weights[1, at, :], NN)
        grads[1, at, :] = dot(hidden, cot[...], TN).astype(BF)
        grad = dot(cot[...], weights[1, at, :], NT) * slope
        grad = grad.astype(BF)
        acc[1] += dot(grad, weights[0, at, :], NN)
        grads[0, at, :] = dot(grad, low2_all[...], TN).astype(BF)

    size = 256
    full = nf // size

    @pl.loop(0, full)
    def _(j):
        step(pl.multiple_of(j * size, size), size)

    if nf % size:
        step(full * size, nf % size)

    swap_acc = remote(acc.at[:, theirs], got, xs.at[1], xr.at[1], other)
    swap_acc.start()

    def grad_copies(i):
        out = []
        for h in range(2):
            for k in range(2):
                out.append(
                    pltpu.make_async_copy(
                        grads.at[k, pl.ds(i * fc, fc), pl.ds(h * main, main)],
                        pm.at[i, h, pl.ds(k * fc, fc)],
                        psem.at[i, h, k],
                    )
                )
        return out

    def tail_copies(i):
        return [
            pltpu.make_async_copy(tails.at[i, h], pm.at[i, h, pl.ds(2 * fc, extra)], qsem.at[i, h])
            for h in range(2)
        ]

    @pl.loop(0, wide)
    def _(i):
        for copy in grad_copies(i):
            copy.start()
        low = jnp.concatenate([grads[k, pl.ds(i * fc, fc), 2 * main :] for k in range(2)], 0).astype(F32)
        for h in range(2):
            tails[i, h] = squeezed(low[:, h * rem : (h + 1) * rem], extra, main, low[:, 2 * rem : 2 * rem + 1]).astype(BF)
        for copy in tail_copies(i):
            copy.start()

    swap_acc.wait_recv()
    result = residual[...] + (acc[0, mine] + got[0]) + vec[5:6]
    store_packed(lo, (), result, main, rem)
    normed2, scale2 = normed_rows(residual[...], width)
    grad_low2 = acc[1, mine] + got[1]
    grad_out = cot[mine].astype(F32)
    lane = lax.broadcasted_iota(jnp.int32, grad_out.shape, 1)
    total = jnp.where(lane < width, grad_out + norm_back(grad_low2, normed2, scale2, vec[3:4], width), 0.0)
    grad_res[...] = total
    sums[...] = jnp.zeros_like(sums)
    sums[2:3] = jnp.sum(total.astype(BF).astype(F32), 0, keepdims=True)
    sums[3:4] = jnp.sum(grad_low2 * normed2, 0, keepdims=True)
    sums[4:5] = jnp.sum(grad_low2, 0, keepdims=True)
    sums[5:6] = jnp.sum(grad_out, 0, keepdims=True)

    @pl.loop(0, wide)
    def _(i):
        for copy in grad_copies(i) + tail_copies(i):
            copy.wait()

    swap_low.wait_send()
    swap_acc.wait_send()


def mlp(low2, cot_in, gm, residual, vec, fc, rem):
    wide = gm.shape[0]
    rows, padded = low2.shape
    nf = wide * fc
    main = gm.shape[3]
    extra = gm.shape[2] - 2 * fc
    vmem = pl.BlockSpec(memory_space=pltpu.VMEM)
    return pl.pallas_call(
        functools.partial(mlp_kernel, wide, fc, rem),
        out_shape=(
            jax.ShapeDtypeStruct(gm.shape, BF),
            jax.ShapeDtypeStruct((2,) + cot_in.shape[2:], BF),
            jax.ShapeDtypeStruct((rows, padded), F32),
            jax.ShapeDtypeStruct((16, padded), F32),
        ),
        in_specs=[vmem, vmem, ANY, vmem, vmem],
        out_specs=(ANY, vmem, vmem, vmem),
        scratch_shapes=[
            pltpu.VMEM((2, nf, padded), BF),
            pltpu.VMEM((2, nf, padded), BF),
            pltpu.VMEM((wide, 2, extra, main), BF),
            pltpu.VMEM((2 * rows, padded), BF),
            pltpu.VMEM((2 * rows, padded), BF),
            pltpu.VMEM((2, 2 * rows, padded), F32),
            pltpu.VMEM((2, rows, padded), F32),
            DMA((wide, 2, 2)),
            DMA((wide, 2)),
            DMA((wide, 2, 2)),
            DMA((wide, 2)),
            DMA((2,)),
            DMA((2,)),
        ],
        compiler_params=pltpu.CompilerParams(
            collective_id=2, has_side_effects=True, vmem_limit_bytes=LIMIT
        ),
    )(low2, cot_in, gm, residual, vec)


def fill_mask(q_seg, k_seg, mask):
    keys, queries = mask.shape
    key = lax.broadcasted_iota(jnp.int32, (keys, queries), 0)
    query = lax.broadcasted_iota(jnp.int32, (keys, queries), 1) + (keys - queries)
    allowed = (k_seg[...] == q_seg[...]) & (key <= query)
    mask[...] = jnp.where(allowed, 0.0, NEGATIVE)


def turned(block):
    return block.astype(F32).T


def attend_pair(q, k, v, mask):
    q_t = turned(q) * SCALE
    row = lax.broadcasted_iota(jnp.int32, q_t.shape, 0)
    parts, logs = [], []
    for h in range(2):
        mine = (row >= h * HEAD) & (row < (h + 1) * HEAD)
        s = dot(k, jnp.where(mine, q_t, 0.0).astype(BF), NN) + mask[...]
        top = jnp.max(s, 0, keepdims=True)
        p = jnp.exp(s - top)
        total = jnp.sum(p, 0, keepdims=True)
        p = (p * (1.0 / total)).astype(BF)
        parts.append(dot(v, p, TN)[h * HEAD : (h + 1) * HEAD])
        logs.append(top + jnp.log(total))
    return jnp.concatenate(parts, 0).T.astype(BF), logs


def normed_rows(values, width):
    lane = lax.broadcasted_iota(jnp.int32, values.shape, 1)
    mean = jnp.sum(values, 1, keepdims=True) * (1.0 / width)
    centred = jnp.where(lane < width, values - mean, 0.0)
    scale = lax.rsqrt(jnp.sum(centred * centred, 1, keepdims=True) * (1.0 / width) + EPS)
    return centred * scale, scale


def norm_back(grad, normed, scale, gain, width):
    lane = lax.broadcasted_iota(jnp.int32, grad.shape, 1)
    scaled = jnp.where(lane < width, grad * gain, 0.0)
    first = jnp.sum(scaled, 1, keepdims=True) * (1.0 / width)
    second = jnp.sum(scaled * normed, 1, keepdims=True) * (1.0 / width)
    return scale * (scaled - first - normed * second)


def edge_tile(tails, rows, rem, base=None):
    tails = [t.astype(F32) for t in tails]
    parts = [spread(t, rows, rem) for t in tails]
    used = 2 * rem
    if base is not None:
        parts.append(spread(tails[0][:, base:], rows, 1))
        used += 1
    parts.append(jnp.zeros((rows, LANES - used), F32))
    return jnp.concatenate(parts, 1).astype(BF)


def forward_kernel(
    outer, hc, rem, xin, cot, sa, sm, q_seg, k_seg,
    cot_out, gm, wa_out, x_out, low1_out, k_out, v_out, q, mixed, lse, residual, low2, vec,
    ga, xs6, wa, x5, low1, k, v, mask, xs, xr, hs, hr, ks, kr, ls, os, *sems
):
    c, z, y, n, first, second = place()
    me = wide_of(z, y)
    wide = 2 * outer
    greet(partners(outer))
    other_n = (c, me, 1 - n)
    other_y = (c, wide_of(z, 1 - y), n)
    other_c = (1 - c, me, n)
    later = (c, wide_of(lax.rem(z + 1, outer), y), n)
    main = sa.shape[1]
    width = 2 * (main + rem)
    rows = q.shape[0]
    span = x5.shape[0]
    cols = 2 * hc
    sent = []

    def go(copy):
        copy.start()
        sent.append(copy)

    def arrived(dst, recv):
        remote(dst, dst, recv, recv, other_c).wait_recv()

    def x_send(j):
        src = xs6.at[n, j + 1 - n] if j < 4 else xin.at[1 - n]
        go(remote(src, xs6.at[n, j + 1 - n], hs.at[j], hr.at[j], other_n))

    own = xs6.at[n, pl.ds(4, 2)]
    keep = pltpu.make_async_copy(xin, own, ls.at[0])
    keep.start()
    keep_cot = pltpu.make_async_copy(cot.at[n], cot_out.at[c, n], ls.at[1])
    keep_cot.start()
    go(remote(xin, xs6.at[n, pl.ds(0, 2)], xs.at[0], xr.at[0], later))
    x_send(4)
    heads = Gather(outer, sa, ga, True, (y, 1 - n), (1 - y, n), sems[:9])
    heads.start()
    heads.start_rest()
    fill_mask(q_seg, k_seg, mask)
    wa[:, width:, :] = jnp.zeros((4, wa.shape[1] - width, wa.shape[2]), BF)
    arrived(xs6.at[n, pl.ds(0, 2)], xr.at[0])
    keep.wait()
    x_send(0)
    go(remote(xs6.at[n, pl.ds(4 * (1 - y), 2)], xs6.at[n, pl.ds(2, 2)], xs.at[1], xr.at[1], other_y))
    for d in range(1, outer):
        heads.along_z(d)
    feed = Gather(outer, sm, gm, False, first, second, sems[9:])
    feed.start()
    arrived(xs6.at[n, pl.ds(2, 2)], xr.at[1])
    for j in (1, 2, 3):
        x_send(j)
    for d in range(outer):
        heads.along_first(d)
    go(remote(cot.at[1 - n], cot_out.at[c, n], ks.at[0], kr.at[0], other_n))
    go(remote(cot.at[n], cot_out.at[c, n], ks.at[1], kr.at[1], other_c))
    feed.start_rest()

    for j in range(5):
        arrived(xs6.at[1 - n, j + n], hr.at[j])
    for j in range(5):
        at = slice(j * rows, (j + 1) * rows)
        for h in range(2):
            x5[at, h * main : (h + 1) * main] = xs6[h, n + j, 0:rows, :]
        x5[at, 2 * main :] = edge_tile([xs6[h, n + j, rows:, :] for h in range(2)], rows, rem)
    outs = [pltpu.make_async_copy(x5, x_out, os.at[0])]
    outs[0].start()
    for kk in range(2):
        for d in range(outer):
            heads.along_second(d, kk)
    heads.finish()
    for d in range(1, outer):
        feed.along_z(d)

    block_rows = 16 + up16(4 * hc)
    extra = ga.shape[3] - block_rows
    base = -(-block_rows // extra) * rem
    for i in range(wide):
        for half in range(2):
            edge = edge_tile([ga[half, i, h, block_rows:, :] for h in range(2)], block_rows, rem, base)
            for s in range(4):
                src = slice(s * hc, (s + 1) * hc)
                to = slice(i * cols + half * hc, i * cols + (half + 1) * hc)
                for h in range(2):
                    wa[s, to, h * main : (h + 1) * main] = ga[half, i, h, src, :]
                wa[s, to, 2 * main :] = edge[src]
            if i == 0 and half == 0:
                at = slice(block_rows - 16, block_rows)
                for h in range(2):
                    vec[:, h * main : (h + 1) * main] = ga[0, 0, h, at, :].astype(F32)
                vec[:, 2 * main :] = edge[at].astype(F32)
    outs.append(pltpu.make_async_copy(wa, wa_out, os.at[1]))
    outs[1].start()

    @pl.loop(0, span // rows)
    def _(j):
        at = pl.ds(pl.multiple_of(j * rows, rows), rows)
        normed, _ = normed_rows(x5[at, :].astype(F32), width)
        low1[at, :] = (normed * vec[0:1] + vec[1:2]).astype(BF)
        k[at, :] = dot(low1[at, :], wa[1], NT).astype(BF)
        v[at, :] = dot(low1[at, :], wa[2], NT).astype(BF)

    q[...] = dot(low1[span - rows :, :], wa[0], NT).astype(BF)
    for src, dst in ((low1, low1_out), (k, k_out), (v, v_out)):
        outs.append(pltpu.make_async_copy(src, dst, os.at[len(outs)]))
        outs[-1].start()

    pairs = q.shape[1] // LANES
    lse[...] = jnp.zeros_like(lse)

    def some(begin, end):
        @pl.loop(begin, end)
        def _(i):
            at = pl.ds(pl.multiple_of(i * LANES, LANES), LANES)
            out, logs = attend_pair(q[:, at], k[:, at], v[:, at], mask)
            mixed[:, at] = out
            for h in range(2):
                lse[i, pl.ds(h, 1), :] = logs[h]

    cut = pairs // 2
    some(0, cut)
    for d in range(outer):
        feed.along_first(d)
    arrived(cot_out.at[c, 1 - n], kr.at[0])
    go(remote(cot_out.at[c, 1 - n], cot_out.at[c, 1 - n], ks.at[2], kr.at[2], other_c))
    some(cut, pairs)
    value = x5[span - rows :, :].astype(F32) + dot(mixed[...], wa[3], NN) + vec[2:3]
    residual[...] = value
    normed, _ = normed_rows(value, width)
    low2[...] = (normed * vec[3:4] + vec[4:5]).astype(BF)

    for kk in range(2):
        for d in range(outer):
            feed.along_second(d, kk)
    arrived(cot_out.at[1 - c, n], kr.at[1])
    arrived(cot_out.at[1 - c, 1 - n], kr.at[2])
    keep_cot.wait()
    for copy in outs:
        copy.wait()
    for copy in sent:
        copy.wait_send()
    feed.finish()


def forward(xin, cot, sa, sm, q_seg, k_seg, hc, rem):
    wide = lax.axis_size("wide")
    outer = wide // 2
    main = sa.shape[1]
    width = 2 * (main + rem)
    padded = -(-(width + 1) // LANES) * LANES
    rows = q_seg.shape[1]
    span = k_seg.shape[0]
    pairs = padded // LANES
    vmem = pl.BlockSpec(memory_space=pltpu.VMEM)
    shape = jax.ShapeDtypeStruct
    return pl.pallas_call(
        functools.partial(forward_kernel, outer, hc, rem),
        out_shape=(
            shape((2,) + cot.shape, BF),
            shape((wide, 2) + sm.shape, BF),
            shape((4, padded, padded), BF),
            shape((span, padded), BF),
            shape((span, padded), BF),
            shape((span, padded), BF),
            shape((span, padded), BF),
            shape((rows, padded), BF),
            shape((rows, padded), BF),
            shape((pairs, 8, rows), F32),
            shape((rows, padded), F32),
            shape((rows, padded), BF),
            shape((16, padded), F32),
        ),
        in_specs=[ANY] * 4 + [vmem] * 2,
        out_specs=(ANY,) * 7 + (vmem,) * 6,
        scratch_shapes=[
            pltpu.VMEM((2, wide, 2) + sa.shape, BF),
            pltpu.VMEM((2, 6) + xin.shape[1:], BF),
            pltpu.VMEM((4, padded, padded), BF),
            pltpu.VMEM((span, padded), BF),
            pltpu.VMEM((span, padded), BF),
            pltpu.VMEM((span, padded), BF),
            pltpu.VMEM((span, padded), BF),
            pltpu.VMEM((span, rows), F32),
        ]
        + [DMA((2,)), DMA((2,)), DMA((5,)), DMA((5,)), DMA((3,)), DMA((3,)), DMA((2,)), DMA((5,))]
        + gather_sems(outer)
        + gather_sems(outer),
        compiler_params=pltpu.CompilerParams(
            collective_id=0, has_side_effects=True, vmem_limit_bytes=LIMIT
        ),
    )(xin, cot, sa, sm, q_seg, k_seg)


def attend_back_pair(q, k, v, g, lse, mask):
    q_n = q.astype(F32) * SCALE
    g_n = g.astype(F32)
    q_t, g_t = q_n.T, g_n.T
    row = lax.broadcasted_iota(jnp.int32, q_t.shape, 0)
    lane = lax.broadcasted_iota(jnp.int32, q_n.shape, 1)
    parts = []
    dk_sum = dv_sum = None
    for h in range(2):
        in_row = (row >= h * HEAD) & (row < (h + 1) * HEAD)
        in_lane = (lane >= h * HEAD) & (lane < (h + 1) * HEAD)
        s = dot(k, jnp.where(in_row, q_t, 0.0).astype(BF), NN) + mask[...]
        p = jnp.exp(s - lse[h : h + 1])
        dp = dot(v, jnp.where(in_row, g_t, 0.0).astype(BF), NN)
        delta = jnp.sum(p * dp, 0, keepdims=True)
        ds = (p * (dp - delta)).astype(BF)
        one = dot(ds, jnp.where(in_lane, q_n, 0.0).astype(BF), NN)
        two = dot(p.astype(BF), jnp.where(in_lane, g_n, 0.0).astype(BF), NN)
        dk_sum = one if dk_sum is None else dk_sum + one
        dv_sum = two if dv_sum is None else dv_sum + two
        parts.append(dot(k, ds, TN)[h * HEAD : (h + 1) * HEAD] * SCALE)
    return jnp.concatenate(parts, 0).T.astype(BF), dk_sum.astype(BF), dv_sum.astype(BF)


def backward_kernel(
    outer, hc, rem, grad_res, q, lse, q_seg, k_seg, vec, sums_in, k_in, v_in, wa_in, x_in, low1_in, mixed_in, pm, lo,
    mo, ao, xg, vec_out, lo_out, m1, m2, m3, pcore,
    pool, k, v, dk, dv, dq, g, branch, mask, stage, firsts, a1, a2, a3, pa, po, pin, edge,
    pg, got_x, got_y, got_z, out_y, out_z, sums, vx, vz,
    ls, xs, xr, hs, hr, cs, cr, vs, vr, ps, ms, *sems
):
    c, z, y, n, first, second = place()
    me = wide_of(z, y)
    wide = 2 * outer
    greet(partners(outer))
    other_n = (c, me, 1 - n)
    other_y = (c, wide_of(z, 1 - y), n)
    other_c = (1 - c, me, n)
    earlier = (c, wide_of(lax.rem(z + outer - 1, outer), y), n)
    main = pm.shape[3]
    width = 2 * (main + rem)
    rows, padded = q.shape
    span = k.shape[0]
    blocks = span // rows
    cols = 2 * hc
    block_rows = edge.shape[0]
    extra = pa.shape[2] - block_rows
    sent = []

    def go(copy):
        copy.start()
        sent.append(copy)

    def arrived(dst, recv):
        remote(dst, dst, recv, recv, other_c).wait_recv()

    feed = StagedScatter(
        outer, first, second, lambda z, y, n: pm.at[wide_of(z, y), n], m1, m2, m3, mo, sems[:8]
    )
    feed.stage(stage, ms, firsts)
    loads = [
        pltpu.make_async_copy(src, dst, ls.at[i])
        for i, (src, dst) in enumerate(
            (
                (wa_in.at[3], pool.at[0]),
                (k_in, k),
                (v_in, v),
                (wa_in.at[1], pool.at[1]),
                (wa_in.at[2], pool.at[2]),
                (wa_in.at[0], pool.at[0]),
                (x_in, v),
                (low1_in, k),
                (mixed_in, g),
                (lo.at[n], lo_out.at[n]),
            )
        )
    ]
    for copy in loads[:5] + loads[9:]:
        copy.start()
    feed.start()
    go(remote(lo.at[1 - n], lo_out.at[n], xs.at[2], xr.at[2], other_n))
    fill_mask(q_seg, k_seg, mask)
    branch[...] = grad_res[...].astype(BF)
    loads[0].wait()
    g[...] = dot(branch[...], pool[0], NT).astype(BF)
    loads[5].start()
    loads[1].wait()
    loads[2].wait()
    pairs = padded // LANES

    def some(begin, end):
        @pl.loop(begin, end)
        def _(i):
            at = pl.ds(pl.multiple_of(i * LANES, LANES), LANES)
            one, two, three = attend_back_pair(q[:, at], k[:, at], v[:, at], g[:, at], lse[i], mask)
            dq[:, at] = one
            dk[:, at] = two
            dv[:, at] = three

    steps = feed.steps()

    def pump(count):
        for _ in range(min(count, len(steps))):
            steps.pop(0)()

    some(0, pairs // 2)
    pump(1)
    some(pairs // 2, pairs)
    for copy in loads[6:9]:
        copy.start()
    sums[...] = sums_in[...]
    for copy in loads[3:7]:
        copy.wait()

    def input_part(j, extra_part):
        at = pl.ds(j * rows, rows)
        grad = dot(dk[at, :], pool[1], NN) + dot(dv[at, :], pool[2], NN)
        if extra_part:
            grad = grad + dot(dq[...], pool[0], NN)
        normed, scale = normed_rows(v[at, :].astype(F32), width)
        sums[0:1] += jnp.sum(grad * normed, 0, keepdims=True)
        sums[1:2] += jnp.sum(grad, 0, keepdims=True)
        back = norm_back(grad, normed, scale, vec[0:1], width)
        if extra_part:
            back = back + grad_res[...]
        store_packed(pg, (j,), back, main, rem)

    def x_back(j):
        go(remote(pg.at[1 - n, j], got_x.at[j], hs.at[j], hr.at[j], other_n))

    for j in (2, 1, 3, 0):
        input_part(j, False)
        x_back(j)
        if j == 1:
            pump(1)
    input_part(blocks - 1, True)
    x_back(blocks - 1)
    vx[0] = sums[...]
    go(remote(vx.at[0], vx.at[1], vs.at[0], vr.at[0], other_c))

    def products(s, left, right):
        size = 256
        for begin in range(0, padded, size):
            stop = min(begin + size, padded)
            pool[s, begin:stop, :] = dot(left[:, begin:stop], right, TN).astype(BF)

    for copy in loads[7:9]:
        copy.wait()
    products(3, g, branch[...])
    pump(1)
    products(0, dq, k[span - rows :, :])
    arrived(vx.at[1], vr.at[0])
    vz[z] = vx[0] + vx[1]
    for d in range(1, outer):
        device = (c, wide_of(lax.rem(z + d, outer), y), n)
        go(remote(vz.at[z], vz.at[z], vs.at[2 + d], vr.at[2 + d], device))
    products(1, dk, k[...])
    pump(2)
    products(2, dv, k[...])
    pump(1)

    def place_rows(i, core, out):
        for s in range(4):
            to = slice(s * hc, (s + 1) * hc)
            src = slice(i * cols + core * hc, i * cols + (core + 1) * hc)
            for h in range(2):
                out[h, to, :] = pool[s, src, h * main : (h + 1) * main]
            edge[to, :] = pool[s, src, 2 * main :]
        if block_rows > 4 * hc:
            gap = slice(4 * hc, block_rows)
            for h in range(2):
                out[h, gap, :] = jnp.zeros((block_rows - 4 * hc, main), BF)
            edge[gap, :] = jnp.zeros((block_rows - 4 * hc, LANES), BF)
        low = edge[...].astype(F32)
        for h in range(2):
            out[h, block_rows:, :] = squeezed(
                low[:, h * rem : (h + 1) * rem], extra, main, low[:, 2 * rem : 2 * rem + 1]
            ).astype(BF)

    def to_core(i):
        return remote(po.at[i % 2], pcore.at[i], cs.at[i], cr.at[i], other_c)

    for i in range(wide):
        if i >= 2:
            to_core(i - 2).wait_send()
        for core in range(2):
            pl.when(c == core)(functools.partial(place_rows, i, 1 - core, po.at[i % 2]))
        to_core(i).start()

    for i in range(wide):
        for core in range(2):
            pl.when(c == core)(functools.partial(place_rows, i, core, pa.at[i]))
    def fetch(i):
        arrived(pcore.at[i], cr.at[i])
        copy = pltpu.make_async_copy(pcore.at[i], pin.at[i % 2], ps.at[i % 2])
        copy.start()
        return copy

    copies = [fetch(0)]
    for i in range(wide):
        if i + 1 < wide:
            copies.append(fetch(i + 1))
        copies[i].wait()
        for h in range(2):
            pa[i, h] = (pa[i, h].astype(F32) + pin[i % 2, h].astype(F32)).astype(BF)
    heads = Scatter(
        outer, (y, 1 - n), (1 - y, n), lambda z, y, n: pa.at[wide_of(z, y), n], a1, a2, a3, ao, sems[8:]
    )
    heads.start(0, 2)
    pump(len(steps))
    late = heads.steps()
    for d in range(1, outer):
        arrived(vz.at[lax.rem(z + outer - d, outer)], vr.at[2 + d])
    total = vz[0]
    for i in range(1, outer):
        total = total + vz[i]
    vx[2] = total
    go(remote(vx.at[2], vx.at[3], vs.at[1], vr.at[1], other_y))

    def summed(b):
        if b == 0:
            return jnp.where(n == 0, pg[n, 0].astype(F32), got_x[0].astype(F32))
        if b == 5:
            return jnp.where(n == 1, pg[n, 4].astype(F32), got_x[4].astype(F32))
        return pg[n, b - n].astype(F32) + got_x[b - 1 + n].astype(F32)

    for j in (2, 1, 3):
        arrived(got_x.at[j], hr.at[j])
    for b in range(2):
        out_y[b] = summed(2 + b).astype(BF)
    go(remote(out_y, got_y, xs.at[0], xr.at[0], other_y))
    heads.start(2)
    late.pop(0)()
    arrived(vx.at[3], vr.at[1])
    vx[4] = vx[2] + vx[3]
    go(remote(vx.at[4], vx.at[5], vs.at[2], vr.at[2], other_n))
    for j in (0, 4):
        arrived(got_x.at[j], hr.at[j])
    arrived(got_y, xr.at[0])
    for b in range(2):
        out_z[b] = (summed(b) + jnp.where(y == 1, got_y[b].astype(F32), 0.0)).astype(BF)
    go(remote(out_z, got_z, xs.at[1], xr.at[1], earlier))
    for _ in range(min(2, len(late))):
        late.pop(0)()
    feed.close()
    for step in late:
        step()
    arrived(got_z, xr.at[1])
    for b in range(2):
        value = summed(4 + b) + jnp.where(y == 0, got_y[b].astype(F32), 0.0)
        xg[b] = (value + got_z[b].astype(F32)).astype(BF)
    arrived(vx.at[5], vr.at[2])
    vec_out[...] = vx[4] + vx[5]
    heads.close()
    loads[9].wait()
    arrived(lo_out.at[1 - n], xr.at[2])
    for i in range(max(wide - 2, 0), wide):
        to_core(i).wait_send()
    for copy in sent:
        copy.wait_send()
    feed.finish()
    heads.finish()


def backward(grad_res, q, lse, q_seg, k_seg, vec, sums, k, v, wa, x5, low1, mixed, pm, lo, hc, rem):
    wide = pm.shape[0]
    outer = wide // 2
    rows, padded = q.shape
    span = k.shape[0]
    main = pm.shape[3]
    bm, bx = pm.shape[2:], lo.shape[1:]
    block_rows = up16(4 * hc)
    ba = (block_rows + rem_rows(block_rows, main + rem), main)
    vmem = pl.BlockSpec(memory_space=pltpu.VMEM)
    shape = jax.ShapeDtypeStruct
    few = max(outer - 1, 1)
    return pl.pallas_call(
        functools.partial(backward_kernel, outer, hc, rem),
        out_shape=(
            shape((2,) + bm, F32),
            shape((2,) + ba, F32),
            shape((2,) + bx, BF),
            shape(sums.shape, F32),
            shape((2,) + bx, BF),
            shape((2 * outer,) + bm, BF),
            shape((outer,) + bm, BF),
            shape((few,) + bm, BF),
            shape((wide, 2) + ba, BF),
        ),
        in_specs=[vmem] * 7 + [ANY] * 8,
        out_specs=(vmem,) * 4 + (ANY,) * 5,
        scratch_shapes=[
            pltpu.VMEM((4, padded, padded), BF),
            pltpu.VMEM((span, padded), BF),
            pltpu.VMEM((span, padded), BF),
            pltpu.VMEM((span, padded), BF),
            pltpu.VMEM((span, padded), BF),
            pltpu.VMEM((rows, padded), BF),
            pltpu.VMEM((rows, padded), BF),
            pltpu.VMEM((rows, padded), BF),
            pltpu.VMEM((span, rows), F32),
            pltpu.VMEM((3,) + bm, BF),
            pltpu.VMEM((outer,) + bm, BF),
        ]
        + scatter_scratch(outer, ba)
        + [
            pltpu.VMEM((wide, 2) + ba, BF),
            pltpu.VMEM((2, 2) + ba, BF),
            pltpu.VMEM((2, 2) + ba, BF),
            pltpu.VMEM((block_rows, LANES), BF),
            pltpu.VMEM((2, span // rows) + bx, BF),
            pltpu.VMEM((5,) + bx, BF),
            pltpu.VMEM((2,) + bx, BF),
            pltpu.VMEM((2,) + bx, BF),
            pltpu.VMEM((2,) + bx, BF),
            pltpu.VMEM((2,) + bx, BF),
            pltpu.VMEM(sums.shape, F32),
            pltpu.VMEM((6,) + sums.shape, F32),
            pltpu.VMEM((outer,) + sums.shape, F32),
        ]
        + [DMA((10,)), DMA((3,)), DMA((3,)), DMA((5,)), DMA((5,)), DMA((wide,)), DMA((wide,))]
        + [DMA((2 + outer,)), DMA((2 + outer,)), DMA((2,)), DMA((3,))]
        + scatter_sems(outer)
        + scatter_sems(outer),
        compiler_params=pltpu.CompilerParams(
            collective_id=1, has_side_effects=True, vmem_limit_bytes=LIMIT
        ),
    )(grad_res, q, lse, q_seg, k_seg, vec, sums, k, v, wa, x5, low1, mixed, pm, lo)


def shards(
    layer_input,
    doc_segments,
    first_gain,
    first_shift,
    heads_weight,
    query_bias,
    value_bias,
    merge_weight,
    merge_bias,
    second_gain,
    second_shift,
    up_weight,
    up_bias,
    down_weight,
    down_bias,
    out_cotangent,
):
    parts = lax.axis_size("narrow")
    wide = lax.axis_size("wide")
    c, w, n = lax.axis_index("dp"), lax.axis_index("wide"), lax.axis_index("narrow")
    half = heads_weight.shape[0]
    width = half * parts
    padded = -(-width // LANES) * LANES
    cols = heads_weight.shape[2]
    units = up_weight.shape[1]
    hc, fc = cols // 2, up16(units // 2)
    short = fc - units // 2
    rows = layer_input.shape[0] // parts
    span = (REACH + 1) * rows

    by_half = heads_weight.transpose(1, 2, 0).reshape(3, 2, hc, half)
    heads_rows = lax.dynamic_index_in_dim(by_half, c, 1, False).reshape(3 * hc, half)
    merge_rows = lax.dynamic_slice_in_dim(merge_weight, c * hc, hc, 0)
    up_rows = lax.dynamic_slice_in_dim(up_weight, c * (units // 2), units // 2, 1).T
    down_rows = lax.dynamic_slice_in_dim(down_weight, c * (units // 2), units // 2, 0)
    up_rows = jnp.pad(up_rows, ((0, short), (0, 0)))
    down_rows = jnp.pad(down_rows, ((0, short), (0, 0)))
    line = lambda *v: jnp.pad(jnp.concatenate(v), (0, half - sum(e.shape[0] for e in v)))
    vectors = jnp.stack([first_gain, first_shift, merge_bias, second_gain, second_shift, down_bias])
    gap = up16(4 * hc) - 4 * hc
    sa = jnp.concatenate([heads_rows, merge_rows, jnp.zeros((gap, half), BF), vectors, jnp.zeros((10, half), BF)], 0)
    part = lambda v, size: lax.dynamic_slice_in_dim(v, c * size, size, 0)
    zero = lambda size: jnp.zeros((size,), BF)
    unit = jnp.array([0, 1, 0, 0, 1, 0], BF)
    column_a = jnp.concatenate(
        [part(query_bias, hc), zero(hc), part(value_bias, hc), zero(hc + gap), unit, zero(10)]
    )
    sm = jnp.concatenate([up_rows, down_rows], 0)
    column_m = jnp.concatenate([part(up_bias, units // 2), zero(short + fc)])
    xin = pack(layer_input.reshape(2, rows, half))
    cot_in = pack(out_cotangent.reshape(2, rows, half))
    seg_row = lax.dynamic_index_in_dim(doc_segments, c, 0, keepdims=False)
    start = (w * parts + n) * rows
    ahead = jnp.concatenate([jnp.full((REACH * rows,), -1, jnp.int32), seg_row])
    k_seg = lax.dynamic_slice_in_dim(ahead, start, span, 0)[:, None]
    q_seg = lax.dynamic_slice_in_dim(seg_row, start, rows, 0)[None]

    rem = widths(half)[1]
    cot_all, gm, wa, x5, low1, key, value, query, mixed, lse, residual, low2, vec = forward(
        xin, cot_in, pack(sa, column_a), pack(sm, column_m), q_seg, k_seg, hc, rem
    )
    pm, lo, grad_residual, sums = mlp(low2, cot_all, gm, residual, vec, fc, rem)

    mo, ao, xg, sums, lo_out, _, _, _, _ = backward(
        grad_residual, query, lse, q_seg, k_seg, vec, sums, key, value, wa, x5, low1, mixed, pm, lo, hc, rem
    )

    layer_output = unpack_half(lo_out, rows, half).reshape(2 * rows, half)
    input_grad = unpack_half(xg, rows, half).reshape(2 * rows, half)
    biases = column_of(ao, up16(4 * hc), half)
    ao = unpack_half(ao, up16(4 * hc), half)
    heads_total = ao[:, : 3 * hc].reshape(2, 3, hc, half).transpose(3, 1, 0, 2).reshape(half, 3, cols)
    merge_total = ao[:, 3 * hc : 4 * hc].reshape(cols, half)
    up_bias_total = column_of(mo, 2 * fc, half)[:, : units // 2].reshape(units)
    mo = unpack_half(mo, 2 * fc, half)
    up_total = mo[:, : units // 2].reshape(units, half).T
    down_total = mo[:, fc : fc + units // 2].reshape(units, half)

    lines = lax.dynamic_index_in_dim(halves(sums[:6, :width]), n, 0, False)
    query_total = biases[:, :hc].reshape(cols)
    value_total = biases[:, 2 * hc : 3 * hc].reshape(cols)
    return (
        layer_output,
        input_grad,
        lines[0],
        lines[1],
        heads_total,
        query_total,
        value_total,
        merge_total,
        lines[2],
        lines[3],
        lines[4],
        up_total,
        up_bias_total,
        down_total,
        lines[5],
    )


def solution(mesh):
    return jax.shard_map(
        shards,
        mesh=mesh,
        in_specs=(
            P(("dp", "wide"), "narrow"),
            P(),
            P("narrow"),
            P("narrow"),
            P("narrow", None, "wide"),
            P("wide"),
            P("wide"),
            P("wide", "narrow"),
            P("narrow"),
            P("narrow"),
            P("narrow"),
            P("narrow", "wide"),
            P("wide"),
            P("wide", "narrow"),
            P("narrow"),
            P(("dp", "wide"), "narrow"),
        ),
        out_specs=(
            P(("dp", "wide"), "narrow"),
            P(("dp", "wide"), "narrow"),
            P("narrow"),
            P("narrow"),
            P("narrow", None, "wide"),
            P("wide"),
            P("wide"),
            P("wide", "narrow"),
            P("narrow"),
            P("narrow"),
            P("narrow"),
            P("narrow", "wide"),
            P("wide"),
            P("wide", "narrow"),
            P("narrow"),
        ),
        check_vma=False,
    )
```

```python
import functools

import jax
import jax.numpy as jnp
from jax import lax
from jax.experimental import pallas as pl
from jax.experimental.pallas import tpu as pltpu
from jax.sharding import PartitionSpec as P

HEAD = 64
REACH = 4
EPS = 1e-05
NEGATIVE = -1e30
LANES = 128
BF = jnp.bfloat16
F32 = jnp.float32
MESH = pl.DeviceIdType.MESH
ANY = pl.BlockSpec(memory_space=pl.ANY)
DMA = pltpu.SemaphoreType.DMA
SCALE = HEAD ** (-0.5)
LIMIT = 62 * 1024 * 1024


def widths(half):
    main = half // LANES * LANES
    return main, half - main


def rem_rows(rows, half):
    main, rem = widths(half)
    return up16(-(-rows // (main // rem)))


def up16(rows):
    return -(-rows // 16) * 16


def pack(block, column=None):
    rows, half = block.shape[-2:]
    main, rem = widths(half)
    count = main // rem
    extra = rem_rows(rows, half)
    lead = block.shape[:-2]
    none = [(0, 0)] * len(lead)
    tail = jnp.pad(block[..., main:], none + [(0, count * extra - rows), (0, 0)])
    tail = jnp.swapaxes(tail.reshape(lead + (count, extra, rem)), -2, -3).reshape(lead + (extra, main))
    if column is not None:
        base, groups = column_base(rows, half), -(-rows // extra)
        column = jnp.pad(column, (0, groups * extra - rows)).reshape(groups, extra).T
        tail = jnp.concatenate([tail[:, :base], column, tail[:, base + groups :]], 1)
    return jnp.concatenate([block[..., :main], tail], -2)


def column_base(rows, half):
    return -(-rows // rem_rows(rows, half)) * widths(half)[1]


def column_of(block, rows, half):
    base, extra = column_base(rows, half), rem_rows(rows, half)
    groups = -(-rows // extra)
    tail = block[..., rows : rows + extra, base : base + groups]
    return jnp.swapaxes(tail, -1, -2).reshape(block.shape[:-2] + (groups * extra,))[..., :rows]


def unpack(block, rows, half):
    main, rem = widths(half)
    count = main // rem
    extra = rem_rows(rows, half)
    lead = block.shape[:-2]
    tail = block[..., rows : rows + extra, :].reshape(lead + (extra, count, rem))
    tail = jnp.swapaxes(tail, -2, -3).reshape(lead + (count * extra, rem))[..., :rows, :]
    return block[..., :rows, :], tail


def unpack_half(block, rows, half):
    return jnp.concatenate(unpack(block, rows, half), -1)


def join(blocks, rows, half):
    body, tail = unpack(blocks, rows, half)
    return jnp.concatenate([body[0], body[1], tail[0], tail[1]], -1)


def halves(full):
    half = full.shape[-1] // 2
    main, rem = widths(half)
    edge = 2 * main
    return jnp.stack(
        [
            jnp.concatenate([full[..., :main], full[..., edge : edge + rem]], -1),
            jnp.concatenate([full[..., main:edge], full[..., edge + rem :]], -1),
        ]
    )


def place():
    c, w, n = lax.axis_index("dp"), lax.axis_index("wide"), lax.axis_index("narrow")
    z, y = lax.div(w, 2), lax.rem(w, 2)
    first = (y + c * (1 - 2 * y), n + (1 - c) * (1 - 2 * n))
    second = (y + (1 - c) * (1 - 2 * y), n + c * (1 - 2 * n))
    return c, z, y, n, first, second


def wide_of(z, y):
    return z * 2 + y


def remote(src, dst, send, recv, device):
    return pltpu.make_async_remote_copy(
        src_ref=src, dst_ref=dst, send_sem=send, recv_sem=recv, device_id=device, device_id_type=MESH
    )


def greet(devices):
    barrier = pltpu.get_barrier_semaphore()
    for device in devices:
        pl.semaphore_signal(barrier, inc=1, device_id=device, device_id_type=MESH)
    pl.semaphore_wait(barrier, len(devices))


def partners(outer):
    c, z, y, n, _, _ = place()
    out = [(c, wide_of(lax.rem(z + d, outer), y), n) for d in range(1, outer)]
    out.append((c, wide_of(z, 1 - y), n))
    out.append((c, wide_of(z, y), 1 - n))
    out.append((1 - c, wide_of(z, y), n))
    return out


class Gather:
    def __init__(self, outer, src, out, both, first, second, sems, part=None):
        self.outer, self.src, self.out, self.both = outer, src, out, both
        self.part = outer if part is None else part
        self.first, self.second = first, second
        self.zs, self.zr, self.fs, self.fr, self.ss, self.sr, self.cs, self.cr, self.local = sems
        self.sent = []

    def block(self, z, y, n):
        c = lax.axis_index("dp")
        return self.out.at[c, wide_of(z, y), n] if self.both else self.out.at[wide_of(z, y), n]

    def go(self, copy):
        copy.start()
        self.sent.append(copy)

    def z_at(self, d):
        return lax.rem(place()[1] + self.outer - d, self.outer)

    def to_first(self, d, src):
        c, z, y, n, _, _ = place()
        first, second = self.first, self.second
        device = (c, wide_of(z, first[0]), first[1])
        self.go(remote(src, self.block(self.z_at(d), y, n), self.fs.at[d], self.fr.at[d], device))

    def to_second(self, d, src, k):
        if d >= self.part:
            return
        c, z, y, n, _, _ = place()
        first, second = self.first, self.second
        device = (c, wide_of(z, second[0]), second[1])
        dst = self.block(self.z_at(d), y, n) if k == 0 else self.block(self.z_at(d), *first)
        i = k * self.outer + d
        self.go(remote(src, dst, self.ss.at[i], self.sr.at[i], device))

    def to_core(self, i, src, dst):
        if self.both:
            c, z, y, n, _, _ = place()
            self.go(remote(src, dst, self.cs.at[i], self.cr.at[i], (1 - c, wide_of(z, y), n)))

    def start(self):
        c, z, y, n, _, _ = place()
        first, second = self.first, self.second
        own = self.block(z, y, n)
        self.keep = pltpu.make_async_copy(self.src, own, self.local)
        self.keep.start()
        for d in range(1, self.outer):
            device = (c, wide_of(lax.rem(z + d, self.outer), y), n)
            self.go(remote(self.src, own, self.zs.at[d - 1], self.zr.at[d - 1], device))

    def start_rest(self):
        c, z, y, n, _, _ = place()
        own = self.block(z, y, n)
        self.to_first(0, self.src)
        self.to_second(0, self.src, 0)
        self.to_core(0, self.src, own)

    def arrived(self, dst, recv):
        c, z, y, n, _, _ = place()
        remote(dst, dst, recv, recv, (1 - c, wide_of(z, y), n)).wait_recv()

    def along_z(self, d):
        c, z, y, n, _, _ = place()
        first, second = self.first, self.second
        got = self.block(self.z_at(d), y, n)
        self.arrived(got, self.zr.at[d - 1])
        self.to_first(d, got)
        self.to_second(d, got, 0)
        self.to_core(d, got, got)

    def along_first(self, d):
        c, z, y, n, _, _ = place()
        first, second = self.first, self.second
        got = self.block(self.z_at(d), *first)
        self.arrived(got, self.fr.at[d])
        self.to_second(d, got, 1)
        self.to_core(self.outer + d, got, got)

    def along_second(self, d, k):
        if d >= self.part:
            return
        c, z, y, n, _, _ = place()
        first, second = self.first, self.second
        got = self.block(self.z_at(d), *second) if k == 0 else self.block(self.z_at(d), 1 - y, 1 - n)
        i = k * self.outer + d
        self.arrived(got, self.sr.at[i])
        self.to_core(2 * self.outer + i, got, got)

    def finish(self):
        c, z, y, n, _, _ = place()
        first, second = self.first, self.second
        if self.both:
            spots = [(y, n), first, second, (1 - y, 1 - n)]
            for k, spot in enumerate(spots):
                for d in range(self.outer):
                    got = self.out.at[1 - c, wide_of(self.z_at(d), spot[0]), spot[1]]
                    self.arrived(got, self.cr.at[k * self.outer + d])
        self.keep.wait()
        for copy in self.sent:
            copy.wait_send()


def gather_sems(outer):
    return [
        DMA((outer,)),
        DMA((outer,)),
        DMA((outer,)),
        DMA((outer,)),
        DMA((2 * outer,)),
        DMA((2 * outer,)),
        DMA((4 * outer,)),
        DMA((4 * outer,)),
        DMA,
    ]


class Scatter:
    def __init__(self, outer, first, second, part, one, two, three, fin, sems):
        self.outer, self.part, self.first, self.second = outer, part, first, second
        self.one, self.two, self.three, self.fin = one, two, three, fin
        self.ss, self.sr, self.fs, self.fr, self.zs, self.zr, self.cs, self.cr = sems
        self.sent, self.along_first = [], {}

    def go(self, copy):
        copy.start()
        self.sent.append(copy)

    def arrived(self, dst, recv):
        c, z, y, n, _, _ = place()
        remote(dst, dst, recv, recv, (1 - c, wide_of(z, y), n)).wait_recv()

    def z_at(self, d):
        return lax.rem(place()[1] + d, self.outer)

    def order(self):
        return [d for d in range(1, self.outer)] + [0]

    def start(self, begin=0, end=None):
        c, z, y, n, _, _ = place()
        first, second = self.first, self.second
        device = (c, wide_of(z, second[0]), second[1])
        for d in self.order()[begin:end]:
            for k, spot in ((1, (1 - y, 1 - n)), (0, second)):
                i = k * self.outer + d
                self.go(
                    remote(self.part(self.z_at(d), *spot), self.one.at[i], self.ss.at[i], self.sr.at[i], device)
                )

    def steps(self):
        order = self.order()
        out = [functools.partial(self.to_first, order[0])]
        for here, there in zip(order[1:], order):
            out.append(functools.partial(self.to_first, here))
            out.append(functools.partial(self.to_z, there))
        return out + [functools.partial(self.to_z, order[-1])]

    def read(self, *refs):
        return [ref[...].astype(F32) for ref in refs]

    def to_first(self, d):
        c, z, y, n, _, _ = place()
        first, second = self.first, self.second
        device = (c, wide_of(z, first[0]), first[1])
        i = self.outer + d
        self.arrived(self.one.at[i], self.sr.at[i])
        own, got = self.read(self.part(self.z_at(d), *first), self.one.at[i])
        src = self.for_first(d)
        src[...] = (got + own).astype(BF)
        self.along_first[d] = remote(src, self.two.at[d], self.fs.at[d], self.fr.at[d], device)
        self.go(self.along_first[d])

    def for_first(self, d):
        return self.one.at[self.outer + d]

    def for_z(self, d):
        return self.one.at[d]

    def to_z(self, d):
        c, z, y, n, _, _ = place()
        self.arrived(self.one.at[d], self.sr.at[d])
        self.arrived(self.two.at[d], self.fr.at[d])
        own, one, two = self.read(self.part(self.z_at(d), y, n), self.one.at[d], self.two.at[d])
        value = (one + own).astype(BF).astype(F32) + two
        if d == 0:
            self.fin[c] = value
        else:
            src = self.for_z(d)
            src[...] = value.astype(BF)
            device = (c, wide_of(self.z_at(d), y), n)
            self.go(remote(src, self.three.at[d - 1], self.zs.at[d - 1], self.zr.at[d - 1], device))

    def close(self):
        c, z, y, n, _, _ = place()
        for d in range(1, self.outer):
            self.arrived(self.three.at[d - 1], self.zr.at[d - 1])
        value = self.fin[c]
        for d in range(1, self.outer):
            value = value + self.read(self.three.at[d - 1])[0]
        self.fin[c] = value
        self.go(remote(self.fin.at[c], self.fin.at[c], self.cs, self.cr, (1 - c, wide_of(z, y), n)))

    def finish(self):
        c = lax.axis_index("dp")
        self.arrived(self.fin.at[1 - c], self.cr)
        for copy in self.sent:
            copy.wait_send()


class StagedScatter(Scatter):
    def stage(self, buffers, sems, firsts):
        self.buffers, self.load_sems, self.firsts = buffers, sems, firsts

    def read(self, *refs):
        copies = [
            pltpu.make_async_copy(ref, self.buffers.at[i], self.load_sems.at[i]) for i, ref in enumerate(refs)
        ]
        for copy in copies:
            copy.start()
        for copy in copies:
            copy.wait()
        return [self.buffers[i].astype(F32) for i in range(len(refs))]

    def for_first(self, d):
        return self.firsts.at[d]

    def for_z(self, d):
        slot = self.firsts.at[d]
        copy = self.along_first.pop(d)
        copy.wait_send()
        self.sent = [e for e in self.sent if e is not copy]
        return slot


def scatter_scratch(outer, block):
    return [
        pltpu.VMEM((2 * outer,) + block, BF),
        pltpu.VMEM((outer,) + block, BF),
        pltpu.VMEM((max(outer - 1, 1),) + block, BF),
    ]


def scatter_sems(outer):
    return [
        DMA((2 * outer,)),
        DMA((2 * outer,)),
        DMA((outer,)),
        DMA((outer,)),
        DMA((outer,)),
        DMA((outer,)),
        DMA,
        DMA,
    ]


def dot(left, right, dims):
    return lax.dot_general(left, right, ((dims[0], dims[1]), ((), ())), preferred_element_type=F32)


NN = ((1,), (0,))
NT = ((1,), (1,))
TN = ((0,), (0,))


def spread(tail, rows, rem):
    extra = tail.shape[0]
    count = -(-rows // extra)
    return jnp.concatenate([tail[:, k * rem : (k + 1) * rem] for k in range(count)], 0)[:rows]


def squeezed(block, extra, main, column=None):
    parts = []
    for piece in (block,) if column is None else (block, column):
        rows, each = piece.shape
        count = -(-rows // extra)
        short = count * extra - rows
        if short:
            piece = jnp.concatenate([piece, jnp.zeros((short, each), piece.dtype)], 0)
        parts += [piece[k * extra : (k + 1) * extra] for k in range(count)]
    used = sum(p.shape[1] for p in parts)
    if used < main:
        parts.append(jnp.zeros((extra, main - used), block.dtype))
    return jnp.concatenate(parts, 1)


def store_packed(ref, index, value, main, rem):
    rows = value.shape[0]
    for h in range(2):
        at = ref.at[(h,) + index]
        at[0:rows, :] = value[:, h * main : (h + 1) * main].astype(ref.dtype)
        low = value[:, 2 * main + h * rem : 2 * main + (h + 1) * rem]
        at[rows:, :] = squeezed(low, at.shape[0] - rows, main).astype(ref.dtype)


def gelu_and_slope(u):
    share = 0.5 * (1.0 + lax.erf(u * 0.7071067811865476))
    return u * share, share + u * (jnp.exp(-0.5 * u * u) * 0.3989422804014327)


def mlp_kernel(
    wide, fc, rem, low2, cot_in, gm, residual, vec,
    pm, lo, grad_res, sums,
    weights, grads, tails, cot, low2_all, acc, got, wsem, rsend, rrecv, psem, xs, xr
):
    c, z, y, n, first, second = place()
    outer = wide // 2
    part = (outer + 1) // 2
    other = (1 - c, wide_of(z, y), n)
    beside = (c, wide_of(z, second[0]), second[1])
    rows, padded = low2.shape
    main = gm.shape[3]
    width = 2 * (main + rem)
    extra = gm.shape[2] - 2 * fc
    nf = wide * fc
    base = -(-2 * fc // extra) * rem
    greet([other, beside])
    mine, theirs = pl.ds(c * rows, rows), pl.ds((1 - c) * rows, rows)
    swap_low = remote(low2, low2_all.at[mine], xs.at[0], xr.at[0], other)
    swap_low.start()
    spots = [(y, n), first, second, (1 - y, 1 - n)]

    def pieces(d, spot):
        src = gm.at[wide_of(lax.rem(z + outer - d, outer), spot[0]), spot[1]]
        lanes = pl.ds(pl.multiple_of(spot[1] * main, LANES), main)
        out = []
        for k in range(2):
            at = pl.ds(pl.multiple_of((2 * d + spot[0]) * fc, 16), fc)
            out.append((src.at[pl.ds(k * fc, fc)], weights.at[k, at, lanes]))
        return out + [(src.at[pl.ds(2 * fc, extra)], tails.at[2 * d + spot[0], spot[1]])]

    def local(d):
        return [
            pltpu.make_async_copy(src, dst, wsem.at[d, i, k])
            for i, spot in enumerate(spots if d < part else spots[:2])
            for k, (src, dst) in enumerate(pieces(d, spot))
        ]

    def afar(d):
        return [
            remote(src, dst, rsend.at[d - part, i, k], rrecv.at[d - part, i, k], beside)
            for i, spot in enumerate(spots[:2])
            for k, (src, dst) in enumerate(pieces(d, spot))
        ]

    def landed(d):
        for i, spot in enumerate(spots[2:]):
            for k, (_, dst) in enumerate(pieces(d, spot)):
                remote(dst, dst, rrecv.at[d - part, i, k], rrecv.at[d - part, i, k], other).wait_recv()

    for d in range(part, outer):
        for copy in afar(d):
            copy.start()
    for d in range(outer):
        for copy in local(d):
            copy.start()

    low2_all[mine] = low2[...]
    for k in range(2):
        span = slice(k * rows, (k + 1) * rows)
        for h in range(2):
            cot[span, h * main : (h + 1) * main] = cot_in[k, h, 0:rows, :]
        cot[span, 2 * main :] = edge_tile([cot_in[k, h, rows:, :] for h in range(2)], rows, rem)

    def ready(begin, end):
        for d in range(begin, end):
            for copy in local(d):
                copy.wait()
            if d >= part:
                landed(d)
        for i in range(2 * begin, 2 * end):
            both = edge_tile([tails[i, h] for h in range(2)], 2 * fc, rem, base)
            for k in range(2):
                weights[k, i * fc : (i + 1) * fc, 2 * main :] = both[k * fc : (k + 1) * fc]

    ready(0, part)
    done = 2 * part * fc // 256 * 256
    acc[...] = jnp.zeros_like(acc)
    swap_low.wait_recv()

    def step(start, size):
        at = pl.ds(start, size)
        before = dot(low2_all[...], weights[0, at, :], NT)
        hidden, slope = gelu_and_slope(before)
        hidden = hidden.astype(BF)
        acc[0] += dot(hidden, weights[1, at, :], NN)
        grads[1, at, :] = dot(hidden, cot[...], TN).astype(BF)
        grad = dot(cot[...], weights[1, at, :], NT) * slope
        grad = grad.astype(BF)
        acc[1] += dot(grad, weights[0, at, :], NN)
        grads[0, at, :] = dot(grad, low2_all[...], TN).astype(BF)

    size = 256

    def steps(begin, end):
        full = (end - begin) // size

        @pl.loop(0, full)
        def _(j):
            step(pl.multiple_of(begin + j * size, size), size)

        if (end - begin) % size:
            step(begin + full * size, (end - begin) % size)

    steps(0, done)
    for d in range(part, outer):
        ready(d, d + 1)
        reach = nf if d == outer - 1 else 2 * (d + 1) * fc // size * size
        steps(done, reach)
        done = reach

    swap_acc = remote(acc.at[:, theirs], got, xs.at[1], xr.at[1], other)
    swap_acc.start()

    def grad_copies(i):
        dst = pm.at[wide_of(lax.rem(z + outer - i // 2, outer), i % 2)]
        out = []
        for h in range(2):
            for k in range(2):
                src = grads.at[k, i * fc : (i + 1) * fc, h * main : (h + 1) * main]
                out.append(pltpu.make_async_copy(src, dst.at[h, pl.ds(k * fc, fc)], psem.at[i, h, k]))
            out.append(pltpu.make_async_copy(tails.at[i, h], dst.at[h, pl.ds(2 * fc, extra)], psem.at[i, h, 2]))
        return out

    for i in range(wide):
        low = jnp.concatenate([grads[k, i * fc : (i + 1) * fc, 2 * main :] for k in range(2)], 0).astype(F32)
        for h in range(2):
            tails[i, h] = squeezed(
                low[:, h * rem : (h + 1) * rem], extra, main, low[:, 2 * rem : 2 * rem + 1]
            ).astype(BF)
        for copy in grad_copies(i):
            copy.start()

    swap_acc.wait_recv()
    result = residual[...] + (acc[0, mine] + got[0]) + vec[5:6]
    store_packed(lo, (), result, main, rem)
    normed2, scale2 = normed_rows(residual[...], width)
    grad_low2 = acc[1, mine] + got[1]
    grad_out = cot[mine].astype(F32)
    lane = lax.broadcasted_iota(jnp.int32, grad_out.shape, 1)
    total = jnp.where(lane < width, grad_out + norm_back(grad_low2, normed2, scale2, vec[3:4], width), 0.0)
    grad_res[...] = total
    sums[...] = jnp.zeros_like(sums)
    sums[2:3] = jnp.sum(total.astype(BF).astype(F32), 0, keepdims=True)
    sums[3:4] = jnp.sum(grad_low2 * normed2, 0, keepdims=True)
    sums[4:5] = jnp.sum(grad_low2, 0, keepdims=True)
    sums[5:6] = jnp.sum(grad_out, 0, keepdims=True)

    for i in range(wide):
        for copy in grad_copies(i):
            copy.wait()
    for d in range(part, outer):
        for copy in afar(d):
            copy.wait_send()
    swap_low.wait_send()
    swap_acc.wait_send()


def mlp(low2, cot_in, gm, residual, vec, fc, rem):
    wide = gm.shape[0]
    rows, padded = low2.shape
    nf = wide * fc
    main = gm.shape[3]
    extra = gm.shape[2] - 2 * fc
    vmem = pl.BlockSpec(memory_space=pltpu.VMEM)
    return pl.pallas_call(
        functools.partial(mlp_kernel, wide, fc, rem),
        out_shape=(
            jax.ShapeDtypeStruct(gm.shape, BF),
            jax.ShapeDtypeStruct((2,) + cot_in.shape[2:], BF),
            jax.ShapeDtypeStruct((rows, padded), F32),
            jax.ShapeDtypeStruct((16, padded), F32),
        ),
        in_specs=[vmem, vmem, ANY, vmem, vmem],
        out_specs=(ANY, vmem, vmem, vmem),
        scratch_shapes=[
            pltpu.VMEM((2, nf, padded), BF),
            pltpu.VMEM((2, nf, padded), BF),
            pltpu.VMEM((wide, 2, extra, main), BF),
            pltpu.VMEM((2 * rows, padded), BF),
            pltpu.VMEM((2 * rows, padded), BF),
            pltpu.VMEM((2, 2 * rows, padded), F32),
            pltpu.VMEM((2, rows, padded), F32),
            DMA((wide // 2, 4, 3)),
            DMA((wide // 2, 2, 3)),
            DMA((wide // 2, 2, 3)),
            DMA((wide, 2, 3)),
            DMA((2,)),
            DMA((2,)),
        ],
        compiler_params=pltpu.CompilerParams(
            collective_id=2, has_side_effects=True, vmem_limit_bytes=LIMIT
        ),
    )(low2, cot_in, gm, residual, vec)


def fill_mask(q_seg, k_seg, mask):
    keys, queries = mask.shape
    key = lax.broadcasted_iota(jnp.int32, (keys, queries), 0)
    query = lax.broadcasted_iota(jnp.int32, (keys, queries), 1) + (keys - queries)
    allowed = (k_seg[...] == q_seg[...]) & (key <= query)
    mask[...] = jnp.where(allowed, 0.0, NEGATIVE)


def turned(block):
    return block.astype(F32).T


def attend_pair(q, k, v, mask):
    q_t = turned(q) * SCALE
    row = lax.broadcasted_iota(jnp.int32, q_t.shape, 0)
    parts, logs = [], []
    for h in range(2):
        mine = (row >= h * HEAD) & (row < (h + 1) * HEAD)
        s = dot(k, jnp.where(mine, q_t, 0.0).astype(BF), NN) + mask[...]
        top = jnp.max(s, 0, keepdims=True)
        p = jnp.exp(s - top)
        total = jnp.sum(p, 0, keepdims=True)
        p = (p * (1.0 / total)).astype(BF)
        parts.append(dot(v, p, TN)[h * HEAD : (h + 1) * HEAD])
        logs.append(top + jnp.log(total))
    return jnp.concatenate(parts, 0).T.astype(BF), logs


def normed_rows(values, width):
    lane = lax.broadcasted_iota(jnp.int32, values.shape, 1)
    mean = jnp.sum(values, 1, keepdims=True) * (1.0 / width)
    centred = jnp.where(lane < width, values - mean, 0.0)
    scale = lax.rsqrt(jnp.sum(centred * centred, 1, keepdims=True) * (1.0 / width) + EPS)
    return centred * scale, scale


def norm_back(grad, normed, scale, gain, width):
    lane = lax.broadcasted_iota(jnp.int32, grad.shape, 1)
    scaled = jnp.where(lane < width, grad * gain, 0.0)
    first = jnp.sum(scaled, 1, keepdims=True) * (1.0 / width)
    second = jnp.sum(scaled * normed, 1, keepdims=True) * (1.0 / width)
    return scale * (scaled - first - normed * second)


def edge_tile(tails, rows, rem, base=None):
    tails = [t.astype(F32) for t in tails]
    parts = [spread(t, rows, rem) for t in tails]
    used = 2 * rem
    if base is not None:
        parts.append(spread(tails[0][:, base:], rows, 1))
        used += 1
    parts.append(jnp.zeros((rows, LANES - used), F32))
    return jnp.concatenate(parts, 1).astype(BF)


def forward_kernel(
    outer, hc, rem, xin, cot, sa, sm, q_seg, k_seg,
    cot_out, gm, wa_out, x_out, low1_out, k_out, v_out, q, mixed, lse, residual, low2, vec,
    ga, xs6, wa, x5, low1, k, v, mask, xs, xr, hs, hr, ks, kr, ls, os, *sems
):
    c, z, y, n, first, second = place()
    me = wide_of(z, y)
    wide = 2 * outer
    greet(partners(outer))
    other_n = (c, me, 1 - n)
    other_y = (c, wide_of(z, 1 - y), n)
    other_c = (1 - c, me, n)
    later = (c, wide_of(lax.rem(z + 1, outer), y), n)
    main = sa.shape[1]
    width = 2 * (main + rem)
    rows = q.shape[0]
    span = x5.shape[0]
    cols = 2 * hc
    sent = []

    def go(copy):
        copy.start()
        sent.append(copy)

    def arrived(dst, recv):
        remote(dst, dst, recv, recv, other_c).wait_recv()

    def x_send(j):
        src = xs6.at[n, j + 1 - n] if j < 4 else xin.at[1 - n]
        go(remote(src, xs6.at[n, j + 1 - n], hs.at[j], hr.at[j], other_n))

    own = xs6.at[n, pl.ds(4, 2)]
    keep = pltpu.make_async_copy(xin, own, ls.at[0])
    keep.start()
    keep_cot = pltpu.make_async_copy(cot.at[n], cot_out.at[c, n], ls.at[1])
    keep_cot.start()
    go(remote(xin, xs6.at[n, pl.ds(0, 2)], xs.at[0], xr.at[0], later))
    x_send(4)
    heads = Gather(outer, sa, ga, True, (y, 1 - n), (1 - y, n), sems[:9])
    heads.start()
    heads.start_rest()
    fill_mask(q_seg, k_seg, mask)
    wa[:, width:, :] = jnp.zeros((4, wa.shape[1] - width, wa.shape[2]), BF)
    arrived(xs6.at[n, pl.ds(0, 2)], xr.at[0])
    keep.wait()
    x_send(0)
    go(remote(xs6.at[n, pl.ds(4 * (1 - y), 2)], xs6.at[n, pl.ds(2, 2)], xs.at[1], xr.at[1], other_y))
    for d in range(1, outer):
        heads.along_z(d)
    feed = Gather(outer, sm, gm, False, first, second, sems[9:], (outer + 1) // 2)
    feed.start()
    arrived(xs6.at[n, pl.ds(2, 2)], xr.at[1])
    for j in (1, 2, 3):
        x_send(j)
    for d in range(outer):
        heads.along_first(d)
    go(remote(cot.at[1 - n], cot_out.at[c, n], ks.at[0], kr.at[0], other_n))
    go(remote(cot.at[n], cot_out.at[c, n], ks.at[1], kr.at[1], other_c))
    feed.start_rest()

    for j in range(5):
        arrived(xs6.at[1 - n, j + n], hr.at[j])
    for j in range(5):
        at = slice(j * rows, (j + 1) * rows)
        for h in range(2):
            x5[at, h * main : (h + 1) * main] = xs6[h, n + j, 0:rows, :]
        x5[at, 2 * main :] = edge_tile([xs6[h, n + j, rows:, :] for h in range(2)], rows, rem)
    outs = [pltpu.make_async_copy(x5, x_out, os.at[0])]
    outs[0].start()
    for kk in range(2):
        for d in range(outer):
            heads.along_second(d, kk)
    heads.finish()
    for d in range(1, outer):
        feed.along_z(d)

    block_rows = 16 + up16(4 * hc)
    extra = ga.shape[3] - block_rows
    base = -(-block_rows // extra) * rem
    for i in range(wide):
        for half in range(2):
            edge = edge_tile([ga[half, i, h, block_rows:, :] for h in range(2)], block_rows, rem, base)
            for s in range(4):
                src = slice(s * hc, (s + 1) * hc)
                to = slice(i * cols + half * hc, i * cols + (half + 1) * hc)
                for h in range(2):
                    wa[s, to, h * main : (h + 1) * main] = ga[half, i, h, src, :]
                wa[s, to, 2 * main :] = edge[src]
            if i == 0 and half == 0:
                at = slice(block_rows - 16, block_rows)
                for h in range(2):
                    vec[:, h * main : (h + 1) * main] = ga[0, 0, h, at, :].astype(F32)
                vec[:, 2 * main :] = edge[at].astype(F32)
    outs.append(pltpu.make_async_copy(wa, wa_out, os.at[1]))
    outs[1].start()

    @pl.loop(0, span // rows)
    def _(j):
        at = pl.ds(pl.multiple_of(j * rows, rows), rows)
        normed, _ = normed_rows(x5[at, :].astype(F32), width)
        low1[at, :] = (normed * vec[0:1] + vec[1:2]).astype(BF)
        k[at, :] = dot(low1[at, :], wa[1], NT).astype(BF)
        v[at, :] = dot(low1[at, :], wa[2], NT).astype(BF)

    q[...] = dot(low1[span - rows :, :], wa[0], NT).astype(BF)
    for src, dst in ((low1, low1_out), (k, k_out), (v, v_out)):
        outs.append(pltpu.make_async_copy(src, dst, os.at[len(outs)]))
        outs[-1].start()

    pairs = q.shape[1] // LANES
    lse[...] = jnp.zeros_like(lse)

    def some(begin, end):
        @pl.loop(begin, end)
        def _(i):
            at = pl.ds(pl.multiple_of(i * LANES, LANES), LANES)
            out, logs = attend_pair(q[:, at], k[:, at], v[:, at], mask)
            mixed[:, at] = out
            for h in range(2):
                lse[i, pl.ds(h, 1), :] = logs[h]

    cut = pairs // 2
    some(0, cut)
    for d in range(outer):
        feed.along_first(d)
    arrived(cot_out.at[c, 1 - n], kr.at[0])
    go(remote(cot_out.at[c, 1 - n], cot_out.at[c, 1 - n], ks.at[2], kr.at[2], other_c))
    some(cut, pairs)
    value = x5[span - rows :, :].astype(F32) + dot(mixed[...], wa[3], NN) + vec[2:3]
    residual[...] = value
    normed, _ = normed_rows(value, width)
    low2[...] = (normed * vec[3:4] + vec[4:5]).astype(BF)

    for kk in range(2):
        for d in range(outer):
            feed.along_second(d, kk)
    arrived(cot_out.at[1 - c, n], kr.at[1])
    arrived(cot_out.at[1 - c, 1 - n], kr.at[2])
    keep_cot.wait()
    for copy in outs:
        copy.wait()
    for copy in sent:
        copy.wait_send()
    feed.finish()


def forward(xin, cot, sa, sm, q_seg, k_seg, hc, rem):
    wide = lax.axis_size("wide")
    outer = wide // 2
    main = sa.shape[1]
    width = 2 * (main + rem)
    padded = -(-(width + 1) // LANES) * LANES
    rows = q_seg.shape[1]
    span = k_seg.shape[0]
    pairs = padded // LANES
    vmem = pl.BlockSpec(memory_space=pltpu.VMEM)
    shape = jax.ShapeDtypeStruct
    return pl.pallas_call(
        functools.partial(forward_kernel, outer, hc, rem),
        out_shape=(
            shape((2,) + cot.shape, BF),
            shape((wide, 2) + sm.shape, BF),
            shape((4, padded, padded), BF),
            shape((span, padded), BF),
            shape((span, padded), BF),
            shape((span, padded), BF),
            shape((span, padded), BF),
            shape((rows, padded), BF),
            shape((rows, padded), BF),
            shape((pairs, 8, rows), F32),
            shape((rows, padded), F32),
            shape((rows, padded), BF),
            shape((16, padded), F32),
        ),
        in_specs=[ANY] * 4 + [vmem] * 2,
        out_specs=(ANY,) * 7 + (vmem,) * 6,
        scratch_shapes=[
            pltpu.VMEM((2, wide, 2) + sa.shape, BF),
            pltpu.VMEM((2, 6) + xin.shape[1:], BF),
            pltpu.VMEM((4, padded, padded), BF),
            pltpu.VMEM((span, padded), BF),
            pltpu.VMEM((span, padded), BF),
            pltpu.VMEM((span, padded), BF),
            pltpu.VMEM((span, padded), BF),
            pltpu.VMEM((span, rows), F32),
        ]
        + [DMA((2,)), DMA((2,)), DMA((5,)), DMA((5,)), DMA((3,)), DMA((3,)), DMA((2,)), DMA((5,))]
        + gather_sems(outer)
        + gather_sems(outer),
        compiler_params=pltpu.CompilerParams(
            collective_id=0, has_side_effects=True, vmem_limit_bytes=LIMIT
        ),
    )(xin, cot, sa, sm, q_seg, k_seg)


def attend_back_pair(q, k, v, g, lse, mask):
    q_n = q.astype(F32) * SCALE
    g_n = g.astype(F32)
    q_t, g_t = q_n.T, g_n.T
    row = lax.broadcasted_iota(jnp.int32, q_t.shape, 0)
    lane = lax.broadcasted_iota(jnp.int32, q_n.shape, 1)
    parts = []
    dk_sum = dv_sum = None
    for h in range(2):
        in_row = (row >= h * HEAD) & (row < (h + 1) * HEAD)
        in_lane = (lane >= h * HEAD) & (lane < (h + 1) * HEAD)
        s = dot(k, jnp.where(in_row, q_t, 0.0).astype(BF), NN) + mask[...]
        p = jnp.exp(s - lse[h : h + 1])
        dp = dot(v, jnp.where(in_row, g_t, 0.0).astype(BF), NN)
        delta = jnp.sum(p * dp, 0, keepdims=True)
        ds = (p * (dp - delta)).astype(BF)
        one = dot(ds, jnp.where(in_lane, q_n, 0.0).astype(BF), NN)
        two = dot(p.astype(BF), jnp.where(in_lane, g_n, 0.0).astype(BF), NN)
        dk_sum = one if dk_sum is None else dk_sum + one
        dv_sum = two if dv_sum is None else dv_sum + two
        parts.append(dot(k, ds, TN)[h * HEAD : (h + 1) * HEAD] * SCALE)
    return jnp.concatenate(parts, 0).T.astype(BF), dk_sum.astype(BF), dv_sum.astype(BF)


def backward_kernel(
    outer, hc, rem, grad_res, q, lse, q_seg, k_seg, vec, sums_in, k_in, v_in, wa_in, x_in, low1_in, mixed_in, pm, lo,
    mo, ao, xg, vec_out, lo_out, m1, m2, m3, pcore,
    pool, k, v, dk, dv, dq, g, branch, mask, stage, firsts, a1, a2, a3, pa, po, pin, edge,
    pg, got_x, got_y, got_z, out_y, out_z, sums, vx, vz,
    ls, xs, xr, hs, hr, cs, cr, vs, vr, ps, ms, *sems
):
    c, z, y, n, first, second = place()
    me = wide_of(z, y)
    wide = 2 * outer
    greet(partners(outer))
    other_n = (c, me, 1 - n)
    other_y = (c, wide_of(z, 1 - y), n)
    other_c = (1 - c, me, n)
    earlier = (c, wide_of(lax.rem(z + outer - 1, outer), y), n)
    main = pm.shape[3]
    width = 2 * (main + rem)
    rows, padded = q.shape
    span = k.shape[0]
    blocks = span // rows
    cols = 2 * hc
    block_rows = edge.shape[0]
    extra = pa.shape[2] - block_rows
    sent = []

    def go(copy):
        copy.start()
        sent.append(copy)

    def arrived(dst, recv):
        remote(dst, dst, recv, recv, other_c).wait_recv()

    feed = StagedScatter(
        outer, first, second, lambda z, y, n: pm.at[wide_of(z, y), n], m1, m2, m3, mo, sems[:8]
    )
    feed.stage(stage, ms, firsts)
    loads = [
        pltpu.make_async_copy(src, dst, ls.at[i])
        for i, (src, dst) in enumerate(
            (
                (wa_in.at[3], pool.at[0]),
                (k_in, k),
                (v_in, v),
                (wa_in.at[1], pool.at[1]),
                (wa_in.at[2], pool.at[2]),
                (wa_in.at[0], pool.at[0]),
                (x_in, v),
                (low1_in, k),
                (mixed_in, g),
                (lo.at[n], lo_out.at[n]),
            )
        )
    ]
    for copy in loads[:5] + loads[9:]:
        copy.start()
    feed.start()
    go(remote(lo.at[1 - n], lo_out.at[n], xs.at[2], xr.at[2], other_n))
    fill_mask(q_seg, k_seg, mask)
    branch[...] = grad_res[...].astype(BF)
    loads[0].wait()
    g[...] = dot(branch[...], pool[0], NT).astype(BF)
    loads[5].start()
    loads[1].wait()
    loads[2].wait()
    pairs = padded // LANES

    def some(begin, end):
        @pl.loop(begin, end)
        def _(i):
            at = pl.ds(pl.multiple_of(i * LANES, LANES), LANES)
            one, two, three = attend_back_pair(q[:, at], k[:, at], v[:, at], g[:, at], lse[i], mask)
            dq[:, at] = one
            dk[:, at] = two
            dv[:, at] = three

    steps = feed.steps()

    def pump(count):
        for _ in range(min(count, len(steps))):
            steps.pop(0)()

    some(0, pairs // 2)
    pump(1)
    some(pairs // 2, pairs)
    for copy in loads[6:9]:
        copy.start()
    sums[...] = sums_in[...]
    for copy in loads[3:7]:
        copy.wait()

    def input_part(j, extra_part):
        at = pl.ds(j * rows, rows)
        grad = dot(dk[at, :], pool[1], NN) + dot(dv[at, :], pool[2], NN)
        if extra_part:
            grad = grad + dot(dq[...], pool[0], NN)
        normed, scale = normed_rows(v[at, :].astype(F32), width)
        sums[0:1] += jnp.sum(grad * normed, 0, keepdims=True)
        sums[1:2] += jnp.sum(grad, 0, keepdims=True)
        back = norm_back(grad, normed, scale, vec[0:1], width)
        if extra_part:
            back = back + grad_res[...]
        store_packed(pg, (j,), back, main, rem)

    def x_back(j):
        go(remote(pg.at[1 - n, j], got_x.at[j], hs.at[j], hr.at[j], other_n))

    for j in (2, 1, 3, 0):
        input_part(j, False)
        x_back(j)
        if j == 1:
            pump(1)
    input_part(blocks - 1, True)
    x_back(blocks - 1)
    vx[0] = sums[...]
    go(remote(vx.at[0], vx.at[1], vs.at[0], vr.at[0], other_c))

    def products(s, left, right):
        size = 256
        for begin in range(0, padded, size):
            stop = min(begin + size, padded)
            pool[s, begin:stop, :] = dot(left[:, begin:stop], right, TN).astype(BF)

    for copy in loads[7:9]:
        copy.wait()
    products(3, g, branch[...])
    pump(1)
    products(0, dq, k[span - rows :, :])
    arrived(vx.at[1], vr.at[0])
    vz[z] = vx[0] + vx[1]
    for d in range(1, outer):
        device = (c, wide_of(lax.rem(z + d, outer), y), n)
        go(remote(vz.at[z], vz.at[z], vs.at[2 + d], vr.at[2 + d], device))
    products(1, dk, k[...])
    pump(2)
    products(2, dv, k[...])
    pump(1)

    def place_rows(i, core, out):
        for s in range(4):
            to = slice(s * hc, (s + 1) * hc)
            src = slice(i * cols + core * hc, i * cols + (core + 1) * hc)
            for h in range(2):
                out[h, to, :] = pool[s, src, h * main : (h + 1) * main]
            edge[to, :] = pool[s, src, 2 * main :]
        if block_rows > 4 * hc:
            gap = slice(4 * hc, block_rows)
            for h in range(2):
                out[h, gap, :] = jnp.zeros((block_rows - 4 * hc, main), BF)
            edge[gap, :] = jnp.zeros((block_rows - 4 * hc, LANES), BF)
        low = edge[...].astype(F32)
        for h in range(2):
            out[h, block_rows:, :] = squeezed(
                low[:, h * rem : (h + 1) * rem], extra, main, low[:, 2 * rem : 2 * rem + 1]
            ).astype(BF)

    def to_core(i):
        return remote(po.at[i % 2], pcore.at[i], cs.at[i], cr.at[i], other_c)

    for i in range(wide):
        if i >= 2:
            to_core(i - 2).wait_send()
        for core in range(2):
            pl.when(c == core)(functools.partial(place_rows, i, 1 - core, po.at[i % 2]))
        to_core(i).start()

    for i in range(wide):
        for core in range(2):
            pl.when(c == core)(functools.partial(place_rows, i, core, pa.at[i]))
    def fetch(i):
        arrived(pcore.at[i], cr.at[i])
        copy = pltpu.make_async_copy(pcore.at[i], pin.at[i % 2], ps.at[i % 2])
        copy.start()
        return copy

    copies = [fetch(0)]
    for i in range(wide):
        if i + 1 < wide:
            copies.append(fetch(i + 1))
        copies[i].wait()
        for h in range(2):
            pa[i, h] = (pa[i, h].astype(F32) + pin[i % 2, h].astype(F32)).astype(BF)
    heads = Scatter(
        outer, first, second, lambda z, y, n: pa.at[wide_of(z, y), n], a1, a2, a3, ao, sems[8:]
    )
    heads.start(0, 2)
    pump(len(steps))
    late = heads.steps()
    for d in range(1, outer):
        arrived(vz.at[lax.rem(z + outer - d, outer)], vr.at[2 + d])
    total = vz[0]
    for i in range(1, outer):
        total = total + vz[i]
    vx[2] = total
    go(remote(vx.at[2], vx.at[3], vs.at[1], vr.at[1], other_y))

    def summed(b):
        if b == 0:
            return jnp.where(n == 0, pg[n, 0].astype(F32), got_x[0].astype(F32))
        if b == 5:
            return jnp.where(n == 1, pg[n, 4].astype(F32), got_x[4].astype(F32))
        return pg[n, b - n].astype(F32) + got_x[b - 1 + n].astype(F32)

    for j in (2, 1, 3):
        arrived(got_x.at[j], hr.at[j])
    for b in range(2):
        out_y[b] = summed(2 + b).astype(BF)
    go(remote(out_y, got_y, xs.at[0], xr.at[0], other_y))
    heads.start(2)
    late.pop(0)()
    arrived(vx.at[3], vr.at[1])
    vx[4] = vx[2] + vx[3]
    go(remote(vx.at[4], vx.at[5], vs.at[2], vr.at[2], other_n))
    for j in (0, 4):
        arrived(got_x.at[j], hr.at[j])
    arrived(got_y, xr.at[0])
    for b in range(2):
        out_z[b] = (summed(b) + jnp.where(y == 1, got_y[b].astype(F32), 0.0)).astype(BF)
    go(remote(out_z, got_z, xs.at[1], xr.at[1], earlier))
    for _ in range(min(2, len(late))):
        late.pop(0)()
    feed.close()
    for step in late:
        step()
    arrived(got_z, xr.at[1])
    for b in range(2):
        value = summed(4 + b) + jnp.where(y == 0, got_y[b].astype(F32), 0.0)
        xg[b] = (value + got_z[b].astype(F32)).astype(BF)
    arrived(vx.at[5], vr.at[2])
    vec_out[...] = vx[4] + vx[5]
    heads.close()
    loads[9].wait()
    arrived(lo_out.at[1 - n], xr.at[2])
    for i in range(max(wide - 2, 0), wide):
        to_core(i).wait_send()
    for copy in sent:
        copy.wait_send()
    feed.finish()
    heads.finish()


def backward(grad_res, q, lse, q_seg, k_seg, vec, sums, k, v, wa, x5, low1, mixed, pm, lo, hc, rem):
    wide = pm.shape[0]
    outer = wide // 2
    rows, padded = q.shape
    span = k.shape[0]
    main = pm.shape[3]
    bm, bx = pm.shape[2:], lo.shape[1:]
    block_rows = up16(4 * hc)
    ba = (block_rows + rem_rows(block_rows, main + rem), main)
    vmem = pl.BlockSpec(memory_space=pltpu.VMEM)
    shape = jax.ShapeDtypeStruct
    few = max(outer - 1, 1)
    return pl.pallas_call(
        functools.partial(backward_kernel, outer, hc, rem),
        out_shape=(
            shape((2,) + bm, F32),
            shape((2,) + ba, F32),
            shape((2,) + bx, BF),
            shape(sums.shape, F32),
            shape((2,) + bx, BF),
            shape((2 * outer,) + bm, BF),
            shape((outer,) + bm, BF),
            shape((few,) + bm, BF),
            shape((wide, 2) + ba, BF),
        ),
        in_specs=[vmem] * 7 + [ANY] * 8,
        out_specs=(vmem,) * 4 + (ANY,) * 5,
        scratch_shapes=[
            pltpu.VMEM((4, padded, padded), BF),
            pltpu.VMEM((span, padded), BF),
            pltpu.VMEM((span, padded), BF),
            pltpu.VMEM((span, padded), BF),
            pltpu.VMEM((span, padded), BF),
            pltpu.VMEM((rows, padded), BF),
            pltpu.VMEM((rows, padded), BF),
            pltpu.VMEM((rows, padded), BF),
            pltpu.VMEM((span, rows), F32),
            pltpu.VMEM((3,) + bm, BF),
            pltpu.VMEM((outer,) + bm, BF),
        ]
        + scatter_scratch(outer, ba)
        + [
            pltpu.VMEM((wide, 2) + ba, BF),
            pltpu.VMEM((2, 2) + ba, BF),
            pltpu.VMEM((2, 2) + ba, BF),
            pltpu.VMEM((block_rows, LANES), BF),
            pltpu.VMEM((2, span // rows) + bx, BF),
            pltpu.VMEM((5,) + bx, BF),
            pltpu.VMEM((2,) + bx, BF),
            pltpu.VMEM((2,) + bx, BF),
            pltpu.VMEM((2,) + bx, BF),
            pltpu.VMEM((2,) + bx, BF),
            pltpu.VMEM(sums.shape, F32),
            pltpu.VMEM((6,) + sums.shape, F32),
            pltpu.VMEM((outer,) + sums.shape, F32),
        ]
        + [DMA((10,)), DMA((3,)), DMA((3,)), DMA((5,)), DMA((5,)), DMA((wide,)), DMA((wide,))]
        + [DMA((2 + outer,)), DMA((2 + outer,)), DMA((2,)), DMA((3,))]
        + scatter_sems(outer)
        + scatter_sems(outer),
        compiler_params=pltpu.CompilerParams(
            collective_id=1, has_side_effects=True, vmem_limit_bytes=LIMIT
        ),
    )(grad_res, q, lse, q_seg, k_seg, vec, sums, k, v, wa, x5, low1, mixed, pm, lo)


def shards(
    layer_input,
    doc_segments,
    first_gain,
    first_shift,
    heads_weight,
    query_bias,
    value_bias,
    merge_weight,
    merge_bias,
    second_gain,
    second_shift,
    up_weight,
    up_bias,
    down_weight,
    down_bias,
    out_cotangent,
):
    parts = lax.axis_size("narrow")
    wide = lax.axis_size("wide")
    c, w, n = lax.axis_index("dp"), lax.axis_index("wide"), lax.axis_index("narrow")
    half = heads_weight.shape[0]
    width = half * parts
    padded = -(-width // LANES) * LANES
    cols = heads_weight.shape[2]
    units = up_weight.shape[1]
    hc, fc = cols // 2, up16(units // 2)
    short = fc - units // 2
    rows = layer_input.shape[0] // parts
    span = (REACH + 1) * rows

    by_half = heads_weight.transpose(1, 2, 0).reshape(3, 2, hc, half)
    heads_rows = lax.dynamic_index_in_dim(by_half, c, 1, False).reshape(3 * hc, half)
    merge_rows = lax.dynamic_slice_in_dim(merge_weight, c * hc, hc, 0)
    up_rows = lax.dynamic_slice_in_dim(up_weight, c * (units // 2), units // 2, 1).T
    down_rows = lax.dynamic_slice_in_dim(down_weight, c * (units // 2), units // 2, 0)
    up_rows = jnp.pad(up_rows, ((0, short), (0, 0)))
    down_rows = jnp.pad(down_rows, ((0, short), (0, 0)))
    line = lambda *v: jnp.pad(jnp.concatenate(v), (0, half - sum(e.shape[0] for e in v)))
    vectors = jnp.stack([first_gain, first_shift, merge_bias, second_gain, second_shift, down_bias])
    gap = up16(4 * hc) - 4 * hc
    sa = jnp.concatenate([heads_rows, merge_rows, jnp.zeros((gap, half), BF), vectors, jnp.zeros((10, half), BF)], 0)
    part = lambda v, size: lax.dynamic_slice_in_dim(v, c * size, size, 0)
    zero = lambda size: jnp.zeros((size,), BF)
    unit = jnp.array([0, 1, 0, 0, 1, 0], BF)
    column_a = jnp.concatenate(
        [part(query_bias, hc), zero(hc), part(value_bias, hc), zero(hc + gap), unit, zero(10)]
    )
    sm = jnp.concatenate([up_rows, down_rows], 0)
    column_m = jnp.concatenate([part(up_bias, units // 2), zero(short + fc)])
    xin = pack(layer_input.reshape(2, rows, half))
    cot_in = pack(out_cotangent.reshape(2, rows, half))
    seg_row = lax.dynamic_index_in_dim(doc_segments, c, 0, keepdims=False)
    start = (w * parts + n) * rows
    ahead = jnp.concatenate([jnp.full((REACH * rows,), -1, jnp.int32), seg_row])
    k_seg = lax.dynamic_slice_in_dim(ahead, start, span, 0)[:, None]
    q_seg = lax.dynamic_slice_in_dim(seg_row, start, rows, 0)[None]

    rem = widths(half)[1]
    cot_all, gm, wa, x5, low1, key, value, query, mixed, lse, residual, low2, vec = forward(
        xin, cot_in, pack(sa, column_a), pack(sm, column_m), q_seg, k_seg, hc, rem
    )
    pm, lo, grad_residual, sums = mlp(low2, cot_all, gm, residual, vec, fc, rem)

    mo, ao, xg, sums, lo_out, _, _, _, _ = backward(
        grad_residual, query, lse, q_seg, k_seg, vec, sums, key, value, wa, x5, low1, mixed, pm, lo, hc, rem
    )

    layer_output = unpack_half(lo_out, rows, half).reshape(2 * rows, half)
    input_grad = unpack_half(xg, rows, half).reshape(2 * rows, half)
    biases = column_of(ao, up16(4 * hc), half)
    ao = unpack_half(ao, up16(4 * hc), half)
    heads_total = ao[:, : 3 * hc].reshape(2, 3, hc, half).transpose(3, 1, 0, 2).reshape(half, 3, cols)
    merge_total = ao[:, 3 * hc : 4 * hc].reshape(cols, half)
    up_bias_total = column_of(mo, 2 * fc, half)[:, : units // 2].reshape(units)
    mo = unpack_half(mo, 2 * fc, half)
    up_total = mo[:, : units // 2].reshape(units, half).T
    down_total = mo[:, fc : fc + units // 2].reshape(units, half)

    lines = lax.dynamic_index_in_dim(halves(sums[:6, :width]), n, 0, False)
    query_total = biases[:, :hc].reshape(cols)
    value_total = biases[:, 2 * hc : 3 * hc].reshape(cols)
    return (
        layer_output,
        input_grad,
        lines[0],
        lines[1],
        heads_total,
        query_total,
        value_total,
        merge_total,
        lines[2],
        lines[3],
        lines[4],
        up_total,
        up_bias_total,
        down_total,
        lines[5],
    )


def solution(mesh):
    return jax.shard_map(
        shards,
        mesh=mesh,
        in_specs=(
            P(("dp", "wide"), "narrow"),
            P(),
            P("narrow"),
            P("narrow"),
            P("narrow", None, "wide"),
            P("wide"),
            P("wide"),
            P("wide", "narrow"),
            P("narrow"),
            P("narrow"),
            P("narrow"),
            P("narrow", "wide"),
            P("wide"),
            P("wide", "narrow"),
            P("narrow"),
            P(("dp", "wide"), "narrow"),
        ),
        out_specs=(
            P(("dp", "wide"), "narrow"),
            P(("dp", "wide"), "narrow"),
            P("narrow"),
            P("narrow"),
            P("narrow", None, "wide"),
            P("wide"),
            P("wide"),
            P("wide", "narrow"),
            P("narrow"),
            P("narrow"),
            P("narrow"),
            P("narrow", "wide"),
            P("wide"),
            P("wide", "narrow"),
            P("narrow"),
        ),
        check_vma=False,
    )
```

```python
import functools

import jax
import jax.numpy as jnp
from jax import lax
from jax.experimental import pallas as pl
from jax.experimental.pallas import tpu as pltpu
from jax.sharding import PartitionSpec as P

HEAD = 64
REACH = 4
EPS = 1e-05
NEGATIVE = -1e30
LANES = 128
BF = jnp.bfloat16
F32 = jnp.float32
MESH = pl.DeviceIdType.MESH
ANY = pl.BlockSpec(memory_space=pl.ANY)
DMA = pltpu.SemaphoreType.DMA
SCALE = HEAD ** (-0.5)
LIMIT = 62 * 1024 * 1024


def widths(half):
    main = half // LANES * LANES
    return main, half - main


def rem_rows(rows, half):
    main, rem = widths(half)
    return up16(-(-rows // (main // rem)))


def up16(rows):
    return -(-rows // 16) * 16


def pack(block, column=None):
    rows, half = block.shape[-2:]
    main, rem = widths(half)
    count = main // rem
    extra = rem_rows(rows, half)
    lead = block.shape[:-2]
    none = [(0, 0)] * len(lead)
    tail = jnp.pad(block[..., main:], none + [(0, count * extra - rows), (0, 0)])
    tail = jnp.swapaxes(tail.reshape(lead + (count, extra, rem)), -2, -3).reshape(lead + (extra, main))
    if column is not None:
        base, groups = column_base(rows, half), -(-rows // extra)
        column = jnp.pad(column, (0, groups * extra - rows)).reshape(groups, extra).T
        tail = jnp.concatenate([tail[:, :base], column, tail[:, base + groups :]], 1)
    return jnp.concatenate([block[..., :main], tail], -2)


def column_base(rows, half):
    return -(-rows // rem_rows(rows, half)) * widths(half)[1]


def column_of(block, rows, half):
    base, extra = column_base(rows, half), rem_rows(rows, half)
    groups = -(-rows // extra)
    tail = block[..., rows : rows + extra, base : base + groups]
    return jnp.swapaxes(tail, -1, -2).reshape(block.shape[:-2] + (groups * extra,))[..., :rows]


def unpack(block, rows, half):
    main, rem = widths(half)
    count = main // rem
    extra = rem_rows(rows, half)
    lead = block.shape[:-2]
    tail = block[..., rows : rows + extra, :].reshape(lead + (extra, count, rem))
    tail = jnp.swapaxes(tail, -2, -3).reshape(lead + (count * extra, rem))[..., :rows, :]
    return block[..., :rows, :], tail


def unpack_half(block, rows, half):
    return jnp.concatenate(unpack(block, rows, half), -1)


def join(blocks, rows, half):
    body, tail = unpack(blocks, rows, half)
    return jnp.concatenate([body[0], body[1], tail[0], tail[1]], -1)


def halves(full):
    half = full.shape[-1] // 2
    main, rem = widths(half)
    edge = 2 * main
    return jnp.stack(
        [
            jnp.concatenate([full[..., :main], full[..., edge : edge + rem]], -1),
            jnp.concatenate([full[..., main:edge], full[..., edge + rem :]], -1),
        ]
    )


def place():
    c, w, n = lax.axis_index("dp"), lax.axis_index("wide"), lax.axis_index("narrow")
    z, y = lax.div(w, 2), lax.rem(w, 2)
    first = (y + c * (1 - 2 * y), n + (1 - c) * (1 - 2 * n))
    second = (y + (1 - c) * (1 - 2 * y), n + c * (1 - 2 * n))
    return c, z, y, n, first, second


def wide_of(z, y):
    return z * 2 + y


def remote(src, dst, send, recv, device):
    return pltpu.make_async_remote_copy(
        src_ref=src, dst_ref=dst, send_sem=send, recv_sem=recv, device_id=device, device_id_type=MESH
    )


def greet(devices):
    barrier = pltpu.get_barrier_semaphore()
    for device in devices:
        pl.semaphore_signal(barrier, inc=1, device_id=device, device_id_type=MESH)
    pl.semaphore_wait(barrier, len(devices))


def partners(outer):
    c, z, y, n, _, _ = place()
    out = [(c, wide_of(lax.rem(z + d, outer), y), n) for d in range(1, outer)]
    out.append((c, wide_of(z, 1 - y), n))
    out.append((c, wide_of(z, y), 1 - n))
    out.append((1 - c, wide_of(z, y), n))
    return out


class Gather:
    def __init__(self, outer, src, out, both, first, second, sems, part=None):
        self.outer, self.src, self.out, self.both = outer, src, out, both
        self.part = outer if part is None else part
        self.first, self.second = first, second
        self.zs, self.zr, self.fs, self.fr, self.ss, self.sr, self.cs, self.cr, self.local = sems
        self.sent = []

    def block(self, z, y, n):
        c = lax.axis_index("dp")
        return self.out.at[c, wide_of(z, y), n] if self.both else self.out.at[wide_of(z, y), n]

    def go(self, copy):
        copy.start()
        self.sent.append(copy)

    def z_at(self, d):
        return lax.rem(place()[1] + self.outer - d, self.outer)

    def to_first(self, d, src):
        c, z, y, n, _, _ = place()
        first, second = self.first, self.second
        device = (c, wide_of(z, first[0]), first[1])
        self.go(remote(src, self.block(self.z_at(d), y, n), self.fs.at[d], self.fr.at[d], device))

    def to_second(self, d, src, k):
        if d >= self.part:
            return
        c, z, y, n, _, _ = place()
        first, second = self.first, self.second
        device = (c, wide_of(z, second[0]), second[1])
        dst = self.block(self.z_at(d), y, n) if k == 0 else self.block(self.z_at(d), *first)
        i = k * self.outer + d
        self.go(remote(src, dst, self.ss.at[i], self.sr.at[i], device))

    def to_core(self, i, src, dst):
        if self.both:
            c, z, y, n, _, _ = place()
            self.go(remote(src, dst, self.cs.at[i], self.cr.at[i], (1 - c, wide_of(z, y), n)))

    def start(self):
        c, z, y, n, _, _ = place()
        first, second = self.first, self.second
        own = self.block(z, y, n)
        self.keep = pltpu.make_async_copy(self.src, own, self.local)
        self.keep.start()
        for d in range(1, self.outer):
            device = (c, wide_of(lax.rem(z + d, self.outer), y), n)
            self.go(remote(self.src, own, self.zs.at[d - 1], self.zr.at[d - 1], device))

    def start_rest(self):
        c, z, y, n, _, _ = place()
        own = self.block(z, y, n)
        self.to_first(0, self.src)
        self.to_second(0, self.src, 0)
        self.to_core(0, self.src, own)

    def arrived(self, dst, recv):
        c, z, y, n, _, _ = place()
        remote(dst, dst, recv, recv, (1 - c, wide_of(z, y), n)).wait_recv()

    def along_z(self, d):
        c, z, y, n, _, _ = place()
        first, second = self.first, self.second
        got = self.block(self.z_at(d), y, n)
        self.arrived(got, self.zr.at[d - 1])
        self.to_first(d, got)
        self.to_second(d, got, 0)
        self.to_core(d, got, got)

    def along_first(self, d):
        c, z, y, n, _, _ = place()
        first, second = self.first, self.second
        got = self.block(self.z_at(d), *first)
        self.arrived(got, self.fr.at[d])
        self.to_second(d, got, 1)
        self.to_core(self.outer + d, got, got)

    def along_second(self, d, k):
        if d >= self.part:
            return
        c, z, y, n, _, _ = place()
        first, second = self.first, self.second
        got = self.block(self.z_at(d), *second) if k == 0 else self.block(self.z_at(d), 1 - y, 1 - n)
        i = k * self.outer + d
        self.arrived(got, self.sr.at[i])
        self.to_core(2 * self.outer + i, got, got)

    def finish(self):
        c, z, y, n, _, _ = place()
        first, second = self.first, self.second
        if self.both:
            spots = [(y, n), first, second, (1 - y, 1 - n)]
            for k, spot in enumerate(spots):
                for d in range(self.outer):
                    got = self.out.at[1 - c, wide_of(self.z_at(d), spot[0]), spot[1]]
                    self.arrived(got, self.cr.at[k * self.outer + d])
        self.keep.wait()
        for copy in self.sent:
            copy.wait_send()


def gather_sems(outer):
    return [
        DMA((outer,)),
        DMA((outer,)),
        DMA((outer,)),
        DMA((outer,)),
        DMA((2 * outer,)),
        DMA((2 * outer,)),
        DMA((4 * outer,)),
        DMA((4 * outer,)),
        DMA,
    ]


class Scatter:
    def __init__(self, outer, first, second, part, one, two, three, fin, sems):
        self.outer, self.part, self.first, self.second = outer, part, first, second
        self.one, self.two, self.three, self.fin = one, two, three, fin
        self.ss, self.sr, self.fs, self.fr, self.zs, self.zr, self.cs, self.cr = sems
        self.sent, self.along_first = [], {}

    def go(self, copy):
        copy.start()
        self.sent.append(copy)

    def arrived(self, dst, recv):
        c, z, y, n, _, _ = place()
        remote(dst, dst, recv, recv, (1 - c, wide_of(z, y), n)).wait_recv()

    def z_at(self, d):
        return lax.rem(place()[1] + d, self.outer)

    def order(self):
        return [d for d in range(1, self.outer)] + [0]

    def start(self, begin=0, end=None):
        c, z, y, n, _, _ = place()
        first, second = self.first, self.second
        device = (c, wide_of(z, second[0]), second[1])
        for d in self.order()[begin:end]:
            for k, spot in ((1, (1 - y, 1 - n)), (0, second)):
                i = k * self.outer + d
                self.go(
                    remote(self.part(self.z_at(d), *spot), self.one.at[i], self.ss.at[i], self.sr.at[i], device)
                )

    def steps(self):
        order = self.order()
        out = [functools.partial(self.to_first, order[0])]
        for here, there in zip(order[1:], order):
            out.append(functools.partial(self.to_first, here))
            out.append(functools.partial(self.to_z, there))
        return out + [functools.partial(self.to_z, order[-1])]

    def read(self, *refs):
        return [ref[...].astype(F32) for ref in refs]

    def to_first(self, d):
        c, z, y, n, _, _ = place()
        first, second = self.first, self.second
        device = (c, wide_of(z, first[0]), first[1])
        i = self.outer + d
        self.arrived(self.one.at[i], self.sr.at[i])
        own, got = self.read(self.part(self.z_at(d), *first), self.one.at[i])
        src = self.for_first(d)
        src[...] = (got + own).astype(BF)
        self.along_first[d] = remote(src, self.two.at[d], self.fs.at[d], self.fr.at[d], device)
        self.go(self.along_first[d])

    def for_first(self, d):
        return self.one.at[self.outer + d]

    def for_z(self, d):
        return self.one.at[d]

    def to_z(self, d):
        c, z, y, n, _, _ = place()
        self.arrived(self.one.at[d], self.sr.at[d])
        self.arrived(self.two.at[d], self.fr.at[d])
        own, one, two = self.read(self.part(self.z_at(d), y, n), self.one.at[d], self.two.at[d])
        value = (one + own).astype(BF).astype(F32) + two
        if d == 0:
            self.fin[c] = value
        else:
            src = self.for_z(d)
            src[...] = value.astype(BF)
            device = (c, wide_of(self.z_at(d), y), n)
            self.go(remote(src, self.three.at[d - 1], self.zs.at[d - 1], self.zr.at[d - 1], device))

    def close(self, edges, rem, edge_sems):
        c, z, y, n, _, _ = place()
        for d in range(1, self.outer):
            self.arrived(self.three.at[d - 1], self.zr.at[d - 1])
        value = self.fin[c]
        for d in range(1, self.outer):
            value = value + self.read(self.three.at[d - 1])[0]
        self.fin[c] = value
        other = (1 - c, wide_of(z, y), n)
        self.go(remote(self.fin.at[c], self.fin.at[c], self.cs, self.cr, other))
        rows = edges.shape[1]
        tail = value[rows:]
        base = -(-rows // tail.shape[0]) * rem
        empty = jnp.zeros((rows, LANES - rem - 1), F32)
        edges[c] = jnp.concatenate([spread(tail, rows, rem), spread(tail[:, base:], rows, 1), empty], 1)
        self.edges, self.edge_recv = edges, edge_sems.at[1]
        self.go(remote(edges.at[c], edges.at[c], edge_sems.at[0], edge_sems.at[1], other))

    def finish(self):
        c = lax.axis_index("dp")
        self.arrived(self.fin.at[1 - c], self.cr)
        self.arrived(self.edges.at[1 - c], self.edge_recv)
        for copy in self.sent:
            copy.wait_send()


class StagedScatter(Scatter):
    def stage(self, buffers, sems, firsts):
        self.buffers, self.load_sems, self.firsts = buffers, sems, firsts

    def read(self, *refs):
        copies = [
            pltpu.make_async_copy(ref, self.buffers.at[i], self.load_sems.at[i]) for i, ref in enumerate(refs)
        ]
        for copy in copies:
            copy.start()
        for copy in copies:
            copy.wait()
        return [self.buffers[i].astype(F32) for i in range(len(refs))]

    def for_first(self, d):
        return self.firsts.at[d]

    def for_z(self, d):
        slot = self.firsts.at[d]
        copy = self.along_first.pop(d)
        copy.wait_send()
        self.sent = [e for e in self.sent if e is not copy]
        return slot


def scatter_scratch(outer, block):
    return [
        pltpu.VMEM((2 * outer,) + block, BF),
        pltpu.VMEM((outer,) + block, BF),
        pltpu.VMEM((max(outer - 1, 1),) + block, BF),
    ]


def scatter_sems(outer):
    return [
        DMA((2 * outer,)),
        DMA((2 * outer,)),
        DMA((outer,)),
        DMA((outer,)),
        DMA((outer,)),
        DMA((outer,)),
        DMA,
        DMA,
    ]


def dot(left, right, dims):
    return lax.dot_general(left, right, ((dims[0], dims[1]), ((), ())), preferred_element_type=F32)


NN = ((1,), (0,))
NT = ((1,), (1,))
TN = ((0,), (0,))


def spread(tail, rows, rem):
    extra = tail.shape[0]
    count = -(-rows // extra)
    return jnp.concatenate([tail[:, k * rem : (k + 1) * rem] for k in range(count)], 0)[:rows]


def squeezed(block, extra, main, column=None):
    parts = []
    for piece in (block,) if column is None else (block, column):
        rows, each = piece.shape
        count = -(-rows // extra)
        short = count * extra - rows
        if short:
            piece = jnp.concatenate([piece, jnp.zeros((short, each), piece.dtype)], 0)
        parts += [piece[k * extra : (k + 1) * extra] for k in range(count)]
    used = sum(p.shape[1] for p in parts)
    if used < main:
        parts.append(jnp.zeros((extra, main - used), block.dtype))
    return jnp.concatenate(parts, 1)


def store_rows(dst, src, main, rem):
    rows = src.shape[1] // 2
    for i in range(2):
        at = slice(i * rows, (i + 1) * rows)
        dst[i, 0:rows, :] = src[0:main, at].astype(F32).T.astype(dst.dtype)
        low = src[main : main + rem, at].astype(F32).T
        dst[i, rows:, :] = squeezed(low, dst.shape[1] - rows, main).astype(dst.dtype)


def store_packed(ref, index, value, main, rem):
    rows = value.shape[0]
    for h in range(2):
        at = ref.at[(h,) + index]
        at[0:rows, :] = value[:, h * main : (h + 1) * main].astype(ref.dtype)
        low = value[:, 2 * main + h * rem : 2 * main + (h + 1) * rem]
        at[rows:, :] = squeezed(low, at.shape[0] - rows, main).astype(ref.dtype)


def gelu_and_slope(u):
    share = 0.5 * (1.0 + lax.erf(u * 0.7071067811865476))
    return u * share, share + u * (jnp.exp(-0.5 * u * u) * 0.3989422804014327)


def mlp_kernel(
    wide, fc, rem, low2, cot_in, gm, residual, vec,
    pm, lo, grad_res, sums,
    weights, grads, tails, cot, low2_all, acc, got, wsem, rsend, rrecv, psem, xs, xr
):
    c, z, y, n, first, second = place()
    outer = wide // 2
    part = (outer + 1) // 2
    other = (1 - c, wide_of(z, y), n)
    beside = (c, wide_of(z, second[0]), second[1])
    rows, padded = low2.shape
    main = gm.shape[3]
    width = 2 * (main + rem)
    extra = gm.shape[2] - 2 * fc
    nf = wide * fc
    base = -(-2 * fc // extra) * rem
    greet([other, beside])
    mine, theirs = pl.ds(c * rows, rows), pl.ds((1 - c) * rows, rows)
    swap_low = remote(low2, low2_all.at[mine], xs.at[0], xr.at[0], other)
    swap_low.start()
    spots = [(y, n), first, second, (1 - y, 1 - n)]

    def pieces(d, spot):
        src = gm.at[wide_of(lax.rem(z + outer - d, outer), spot[0]), spot[1]]
        lanes = pl.ds(pl.multiple_of(spot[1] * main, LANES), main)
        out = []
        for k in range(2):
            at = pl.ds(pl.multiple_of((2 * d + spot[0]) * fc, 16), fc)
            out.append((src.at[pl.ds(k * fc, fc)], weights.at[k, at, lanes]))
        return out + [(src.at[pl.ds(2 * fc, extra)], tails.at[2 * d + spot[0], spot[1]])]

    def local(d):
        return [
            pltpu.make_async_copy(src, dst, wsem.at[d, i, k])
            for i, spot in enumerate(spots if d < part else spots[:2])
            for k, (src, dst) in enumerate(pieces(d, spot))
        ]

    def afar(d):
        return [
            remote(src, dst, rsend.at[d - part, i, k], rrecv.at[d - part, i, k], beside)
            for i, spot in enumerate(spots[:2])
            for k, (src, dst) in enumerate(pieces(d, spot))
        ]

    def landed(d):
        for i, spot in enumerate(spots[2:]):
            for k, (_, dst) in enumerate(pieces(d, spot)):
                remote(dst, dst, rrecv.at[d - part, i, k], rrecv.at[d - part, i, k], other).wait_recv()

    for d in range(part, outer):
        for copy in afar(d):
            copy.start()
    for d in range(outer):
        for copy in local(d):
            copy.start()

    low2_all[mine] = low2[...]
    for k in range(2):
        span = slice(k * rows, (k + 1) * rows)
        for h in range(2):
            cot[span, h * main : (h + 1) * main] = cot_in[k, h, 0:rows, :]
        cot[span, 2 * main :] = edge_tile([cot_in[k, h, rows:, :] for h in range(2)], rows, rem)

    def ready(begin, end):
        for d in range(begin, end):
            for copy in local(d):
                copy.wait()
            if d >= part:
                landed(d)
        for i in range(2 * begin, 2 * end):
            both = edge_tile([tails[i, h] for h in range(2)], 2 * fc, rem, base)
            for k in range(2):
                weights[k, i * fc : (i + 1) * fc, 2 * main :] = both[k * fc : (k + 1) * fc]

    ready(0, part)
    done = 2 * part * fc // 256 * 256
    acc[...] = jnp.zeros_like(acc)
    swap_low.wait_recv()

    def step(start, size):
        at = pl.ds(start, size)
        before = dot(low2_all[...], weights[0, at, :], NT)
        hidden, slope = gelu_and_slope(before)
        hidden = hidden.astype(BF)
        acc[0] += dot(hidden, weights[1, at, :], NN)
        grads[1, at, :] = dot(hidden, cot[...], TN).astype(BF)
        grad = dot(cot[...], weights[1, at, :], NT) * slope
        grad = grad.astype(BF)
        acc[1] += dot(grad, weights[0, at, :], NN)
        grads[0, at, :] = dot(grad, low2_all[...], TN).astype(BF)

    size = 256

    def steps(begin, end):
        full = (end - begin) // size

        @pl.loop(0, full)
        def _(j):
            step(pl.multiple_of(begin + j * size, size), size)

        if (end - begin) % size:
            step(begin + full * size, (end - begin) % size)

    steps(0, done)
    for d in range(part, outer):
        ready(d, d + 1)
        reach = nf if d == outer - 1 else 2 * (d + 1) * fc // size * size
        steps(done, reach)
        done = reach

    swap_acc = remote(acc.at[:, theirs], got, xs.at[1], xr.at[1], other)
    swap_acc.start()

    def grad_copies(i):
        dst = pm.at[wide_of(lax.rem(z + outer - i // 2, outer), i % 2)]
        out = []
        for h in range(2):
            for k in range(2):
                src = grads.at[k, i * fc : (i + 1) * fc, h * main : (h + 1) * main]
                out.append(pltpu.make_async_copy(src, dst.at[h, pl.ds(k * fc, fc)], psem.at[i, h, k]))
            out.append(pltpu.make_async_copy(tails.at[i, h], dst.at[h, pl.ds(2 * fc, extra)], psem.at[i, h, 2]))
        return out

    for i in range(wide):
        low = jnp.concatenate([grads[k, i * fc : (i + 1) * fc, 2 * main :] for k in range(2)], 0).astype(F32)
        for h in range(2):
            tails[i, h] = squeezed(
                low[:, h * rem : (h + 1) * rem], extra, main, low[:, 2 * rem : 2 * rem + 1]
            ).astype(BF)
        for copy in grad_copies(i):
            copy.start()

    swap_acc.wait_recv()
    result = residual[...] + (acc[0, mine] + got[0]) + vec[5:6]
    for h in range(2):
        lo[h, 0:main, :] = result[:, h * main : (h + 1) * main].T.astype(BF)
    edge = result[:, 2 * main :].T
    for h in range(2):
        lo[h, main:, :] = edge[h * rem : (h + 1) * rem].astype(BF)
    normed2, scale2 = normed_rows(residual[...], width)
    grad_low2 = acc[1, mine] + got[1]
    grad_out = cot[mine].astype(F32)
    lane = lax.broadcasted_iota(jnp.int32, grad_out.shape, 1)
    total = jnp.where(lane < width, grad_out + norm_back(grad_low2, normed2, scale2, vec[3:4], width), 0.0)
    grad_res[...] = total
    sums[...] = jnp.zeros_like(sums)
    sums[2:3] = jnp.sum(total.astype(BF).astype(F32), 0, keepdims=True)
    sums[3:4] = jnp.sum(grad_low2 * normed2, 0, keepdims=True)
    sums[4:5] = jnp.sum(grad_low2, 0, keepdims=True)
    sums[5:6] = jnp.sum(grad_out, 0, keepdims=True)

    for i in range(wide):
        for copy in grad_copies(i):
            copy.wait()
    for d in range(part, outer):
        for copy in afar(d):
            copy.wait_send()
    swap_low.wait_send()
    swap_acc.wait_send()


def mlp(low2, cot_in, gm, residual, vec, fc, rem):
    wide = gm.shape[0]
    rows, padded = low2.shape
    nf = wide * fc
    main = gm.shape[3]
    extra = gm.shape[2] - 2 * fc
    vmem = pl.BlockSpec(memory_space=pltpu.VMEM)
    return pl.pallas_call(
        functools.partial(mlp_kernel, wide, fc, rem),
        out_shape=(
            jax.ShapeDtypeStruct(gm.shape, BF),
            jax.ShapeDtypeStruct((2, main + rem, rows), BF),
            jax.ShapeDtypeStruct((rows, padded), F32),
            jax.ShapeDtypeStruct((16, padded), F32),
        ),
        in_specs=[vmem, vmem, ANY, vmem, vmem],
        out_specs=(ANY, vmem, vmem, vmem),
        scratch_shapes=[
            pltpu.VMEM((2, nf, padded), BF),
            pltpu.VMEM((2, nf, padded), BF),
            pltpu.VMEM((wide, 2, extra, main), BF),
            pltpu.VMEM((2 * rows, padded), BF),
            pltpu.VMEM((2 * rows, padded), BF),
            pltpu.VMEM((2, 2 * rows, padded), F32),
            pltpu.VMEM((2, rows, padded), F32),
            DMA((wide // 2, 4, 3)),
            DMA((wide // 2, 2, 3)),
            DMA((wide // 2, 2, 3)),
            DMA((wide, 2, 3)),
            DMA((2,)),
            DMA((2,)),
        ],
        compiler_params=pltpu.CompilerParams(
            collective_id=2, has_side_effects=True, vmem_limit_bytes=LIMIT
        ),
    )(low2, cot_in, gm, residual, vec)


def fill_mask(q_seg, k_seg, mask):
    keys, queries = mask.shape
    key = lax.broadcasted_iota(jnp.int32, (keys, queries), 0)
    query = lax.broadcasted_iota(jnp.int32, (keys, queries), 1) + (keys - queries)
    allowed = (k_seg[...] == q_seg[...]) & (key <= query)
    mask[...] = jnp.where(allowed, 0.0, NEGATIVE)


def turned(block):
    return block.astype(F32).T


def attend_pair(q, k, v, mask):
    q_t = turned(q) * SCALE
    row = lax.broadcasted_iota(jnp.int32, q_t.shape, 0)
    parts, logs = [], []
    for h in range(2):
        mine = (row >= h * HEAD) & (row < (h + 1) * HEAD)
        s = dot(k, jnp.where(mine, q_t, 0.0).astype(BF), NN) + mask[...]
        top = jnp.max(s, 0, keepdims=True)
        p = jnp.exp(s - top)
        total = jnp.sum(p, 0, keepdims=True)
        p = (p * (1.0 / total)).astype(BF)
        parts.append(dot(v, p, TN)[h * HEAD : (h + 1) * HEAD])
        logs.append(top + jnp.log(total))
    return jnp.concatenate(parts, 0).T.astype(BF), logs


def normed_rows(values, width):
    lane = lax.broadcasted_iota(jnp.int32, values.shape, 1)
    mean = jnp.sum(values, 1, keepdims=True) * (1.0 / width)
    centred = jnp.where(lane < width, values - mean, 0.0)
    scale = lax.rsqrt(jnp.sum(centred * centred, 1, keepdims=True) * (1.0 / width) + EPS)
    return centred * scale, scale


def norm_back(grad, normed, scale, gain, width):
    lane = lax.broadcasted_iota(jnp.int32, grad.shape, 1)
    scaled = jnp.where(lane < width, grad * gain, 0.0)
    first = jnp.sum(scaled, 1, keepdims=True) * (1.0 / width)
    second = jnp.sum(scaled * normed, 1, keepdims=True) * (1.0 / width)
    return scale * (scaled - first - normed * second)


def edge_tile(tails, rows, rem, base=None):
    tails = [t.astype(F32) for t in tails]
    parts = [spread(t, rows, rem) for t in tails]
    used = 2 * rem
    if base is not None:
        parts.append(spread(tails[0][:, base:], rows, 1))
        used += 1
    parts.append(jnp.zeros((rows, LANES - used), F32))
    return jnp.concatenate(parts, 1).astype(BF)


def forward_kernel(
    outer, hc, rem, x_in, cot_in, sa, sm, q_seg, k_seg, v0, v1, v2, v3, v4, v5,
    cot_out, gm, wa_out, x_out, low1_out, k_out, v_out, q, mixed, lse, residual, low2, vec,
    xin, cot, lines, ga, xs6, wa, x5, low1, k, v, mask, xs, xr, hs, hr, ks, kr, ls, os, *sems
):
    c, z, y, n, first, second = place()
    me = wide_of(z, y)
    wide = 2 * outer
    for src, dst in ((x_in, xin), (cot_in, cot)):
        store_rows(dst, src, sa.shape[1], rem)
    lines[...] = jnp.zeros_like(lines)
    for i, line in enumerate((v0, v1, v2, v3, v4, v5)):
        lines[n, i : i + 1, :] = line[...].astype(F32).reshape(1, -1)
    greet(partners(outer))
    other_n = (c, me, 1 - n)
    other_y = (c, wide_of(z, 1 - y), n)
    other_c = (1 - c, me, n)
    later = (c, wide_of(lax.rem(z + 1, outer), y), n)
    main = sa.shape[1]
    width = 2 * (main + rem)
    rows = q.shape[0]
    span = x5.shape[0]
    cols = 2 * hc
    sent = []

    def go(copy):
        copy.start()
        sent.append(copy)

    def arrived(dst, recv):
        remote(dst, dst, recv, recv, other_c).wait_recv()

    def x_send(j):
        src = xs6.at[n, j + 1 - n] if j < 4 else xin.at[1 - n]
        go(remote(src, xs6.at[n, j + 1 - n], hs.at[j], hr.at[j], other_n))

    own = xs6.at[n, pl.ds(4, 2)]
    keep = pltpu.make_async_copy(xin, own, ls.at[0])
    keep.start()
    keep_cot = pltpu.make_async_copy(cot.at[n], cot_out.at[c, n], ls.at[1])
    keep_cot.start()
    go(remote(lines.at[n], lines.at[n], xs.at[2], xr.at[2], other_n))
    go(remote(xin, xs6.at[n, pl.ds(0, 2)], xs.at[0], xr.at[0], later))
    x_send(4)
    heads = Gather(outer, sa, ga, True, (y, 1 - n), (1 - y, n), sems[:9])
    heads.start()
    heads.start_rest()
    fill_mask(q_seg, k_seg, mask)
    wa[:, width:, :] = jnp.zeros((4, wa.shape[1] - width, wa.shape[2]), BF)
    arrived(xs6.at[n, pl.ds(0, 2)], xr.at[0])
    keep.wait()
    x_send(0)
    go(remote(xs6.at[n, pl.ds(4 * (1 - y), 2)], xs6.at[n, pl.ds(2, 2)], xs.at[1], xr.at[1], other_y))
    for d in range(1, outer):
        heads.along_z(d)
    feed = Gather(outer, sm, gm, False, first, second, sems[9:], (outer + 1) // 2)
    feed.start()
    arrived(xs6.at[n, pl.ds(2, 2)], xr.at[1])
    for j in (1, 2, 3):
        x_send(j)
    for d in range(outer):
        heads.along_first(d)
    go(remote(cot.at[1 - n], cot_out.at[c, n], ks.at[0], kr.at[0], other_n))
    go(remote(cot.at[n], cot_out.at[c, n], ks.at[1], kr.at[1], other_c))
    feed.start_rest()

    arrived(lines.at[1 - n], xr.at[2])
    row = lax.broadcasted_iota(jnp.int32, (8, LANES), 0)
    lane = lax.broadcasted_iota(jnp.int32, (8, LANES), 1)
    unit = jnp.where(((row == 1) | (row == 4)) & (lane == 2 * rem), 1.0, 0.0)
    vec[...] = jnp.zeros_like(vec)
    for h in range(2):
        vec[0:8, h * main : (h + 1) * main] = lines[h, :, 0:main]
    edges = [lines[h, :, main:] for h in range(2)]
    vec[0:8, 2 * main :] = unit + jnp.concatenate(edges + [jnp.zeros((8, LANES - 2 * rem), F32)], 1)
    for j in range(5):
        arrived(xs6.at[1 - n, j + n], hr.at[j])
    for j in range(5):
        at = slice(j * rows, (j + 1) * rows)
        for h in range(2):
            x5[at, h * main : (h + 1) * main] = xs6[h, n + j, 0:rows, :]
        x5[at, 2 * main :] = edge_tile([xs6[h, n + j, rows:, :] for h in range(2)], rows, rem)
    outs = [pltpu.make_async_copy(x5, x_out, os.at[0])]
    outs[0].start()
    for kk in range(2):
        for d in range(outer):
            heads.along_second(d, kk)
    heads.finish()
    for d in range(1, outer):
        feed.along_z(d)

    block_rows = up16(4 * hc)
    extra = ga.shape[3] - block_rows
    base = -(-block_rows // extra) * rem
    for i in range(wide):
        for half in range(2):
            edge = edge_tile([ga[half, i, h, block_rows:, :] for h in range(2)], block_rows, rem, base)
            for s in range(4):
                src = slice(s * hc, (s + 1) * hc)
                to = slice(i * cols + half * hc, i * cols + (half + 1) * hc)
                for h in range(2):
                    wa[s, to, h * main : (h + 1) * main] = ga[half, i, h, src, :]
                wa[s, to, 2 * main :] = edge[src]
    outs.append(pltpu.make_async_copy(wa, wa_out, os.at[1]))
    outs[1].start()

    @pl.loop(0, span // rows)
    def _(j):
        at = pl.ds(pl.multiple_of(j * rows, rows), rows)
        normed, _ = normed_rows(x5[at, :].astype(F32), width)
        low1[at, :] = (normed * vec[0:1] + vec[1:2]).astype(BF)
        k[at, :] = dot(low1[at, :], wa[1], NT).astype(BF)
        v[at, :] = dot(low1[at, :], wa[2], NT).astype(BF)

    q[...] = dot(low1[span - rows :, :], wa[0], NT).astype(BF)
    for src, dst in ((low1, low1_out), (k, k_out), (v, v_out)):
        outs.append(pltpu.make_async_copy(src, dst, os.at[len(outs)]))
        outs[-1].start()

    pairs = q.shape[1] // LANES
    lse[...] = jnp.zeros_like(lse)

    def some(begin, end):
        @pl.loop(begin, end)
        def _(i):
            at = pl.ds(pl.multiple_of(i * LANES, LANES), LANES)
            out, logs = attend_pair(q[:, at], k[:, at], v[:, at], mask)
            mixed[:, at] = out
            for h in range(2):
                lse[i, pl.ds(h, 1), :] = logs[h]

    cut = pairs // 2
    some(0, cut)
    for d in range(outer):
        feed.along_first(d)
    arrived(cot_out.at[c, 1 - n], kr.at[0])
    go(remote(cot_out.at[c, 1 - n], cot_out.at[c, 1 - n], ks.at[2], kr.at[2], other_c))
    some(cut, pairs)
    value = x5[span - rows :, :].astype(F32) + dot(mixed[...], wa[3], NN) + vec[2:3]
    residual[...] = value
    normed, _ = normed_rows(value, width)
    low2[...] = (normed * vec[3:4] + vec[4:5]).astype(BF)

    for kk in range(2):
        for d in range(outer):
            feed.along_second(d, kk)
    arrived(cot_out.at[1 - c, n], kr.at[1])
    arrived(cot_out.at[1 - c, 1 - n], kr.at[2])
    keep_cot.wait()
    for copy in outs:
        copy.wait()
    for copy in sent:
        copy.wait_send()
    feed.finish()


def forward(x_in, cot_in, sa, sm, q_seg, k_seg, vectors, hc, rem):
    wide = lax.axis_size("wide")
    outer = wide // 2
    main = sa.shape[1]
    width = 2 * (main + rem)
    padded = -(-(width + 1) // LANES) * LANES
    rows = q_seg.shape[1]
    span = k_seg.shape[0]
    block = (2, rows + rem_rows(rows, main + rem), main)
    pairs = padded // LANES
    vmem = pl.BlockSpec(memory_space=pltpu.VMEM)
    shape = jax.ShapeDtypeStruct
    return pl.pallas_call(
        functools.partial(forward_kernel, outer, hc, rem),
        out_shape=(
            shape((2,) + block, BF),
            shape((wide, 2) + sm.shape, BF),
            shape((4, padded, padded), BF),
            shape((span, padded), BF),
            shape((span, padded), BF),
            shape((span, padded), BF),
            shape((span, padded), BF),
            shape((rows, padded), BF),
            shape((rows, padded), BF),
            shape((pairs, 8, rows), F32),
            shape((rows, padded), F32),
            shape((rows, padded), BF),
            shape((16, padded), F32),
        ),
        in_specs=[vmem] * 2 + [ANY] * 2 + [vmem] * (2 + len(vectors)),
        out_specs=(ANY,) * 7 + (vmem,) * 6,
        scratch_shapes=[
            pltpu.VMEM(block, BF),
            pltpu.VMEM(block, BF),
            pltpu.VMEM((2, 8, main + rem), F32),
            pltpu.VMEM((2, wide, 2) + sa.shape, BF),
            pltpu.VMEM((2, 6) + block[1:], BF),
            pltpu.VMEM((4, padded, padded), BF),
            pltpu.VMEM((span, padded), BF),
            pltpu.VMEM((span, padded), BF),
            pltpu.VMEM((span, padded), BF),
            pltpu.VMEM((span, padded), BF),
            pltpu.VMEM((span, rows), F32),
        ]
        + [DMA((3,)), DMA((3,)), DMA((5,)), DMA((5,)), DMA((3,)), DMA((3,)), DMA((2,)), DMA((5,))]
        + gather_sems(outer)
        + gather_sems(outer),
        compiler_params=pltpu.CompilerParams(
            collective_id=0, has_side_effects=True, vmem_limit_bytes=LIMIT
        ),
    )(x_in, cot_in, sa, sm, q_seg, k_seg, *vectors)


def attend_back_pair(q, k, v, g, lse, mask):
    q_n = q.astype(F32) * SCALE
    g_n = g.astype(F32)
    q_t, g_t = q_n.T, g_n.T
    row = lax.broadcasted_iota(jnp.int32, q_t.shape, 0)
    lane = lax.broadcasted_iota(jnp.int32, q_n.shape, 1)
    parts = []
    dk_sum = dv_sum = None
    for h in range(2):
        in_row = (row >= h * HEAD) & (row < (h + 1) * HEAD)
        in_lane = (lane >= h * HEAD) & (lane < (h + 1) * HEAD)
        s = dot(k, jnp.where(in_row, q_t, 0.0).astype(BF), NN) + mask[...]
        p = jnp.exp(s - lse[h : h + 1])
        dp = dot(v, jnp.where(in_row, g_t, 0.0).astype(BF), NN)
        delta = jnp.sum(p * dp, 0, keepdims=True)
        ds = (p * (dp - delta)).astype(BF)
        one = dot(ds, jnp.where(in_lane, q_n, 0.0).astype(BF), NN)
        two = dot(p.astype(BF), jnp.where(in_lane, g_n, 0.0).astype(BF), NN)
        dk_sum = one if dk_sum is None else dk_sum + one
        dv_sum = two if dv_sum is None else dv_sum + two
        parts.append(dot(k, ds, TN)[h * HEAD : (h + 1) * HEAD] * SCALE)
    return jnp.concatenate(parts, 0).T.astype(BF), dk_sum.astype(BF), dv_sum.astype(BF)


def backward_kernel(
    outer, hc, rem, grad_res, q, lse, q_seg, k_seg, vec, sums_in, k_in, v_in, wa_in, x_in, low1_in, mixed_in, pm, lo,
    mo, ao, em, ea, xg, vec_out, lo_out, m1, m2, m3, pcore,
    pool, k, v, dk, dv, dq, g, branch, mask, stage, firsts, a1, a2, a3, pa, po, edge,
    pg, got_x, got_y, got_z, out_y, out_z, sums, vx, vz,
    ls, xs, xr, hs, hr, cs, cr, vs, vr, ps, ms, es, *sems
):
    c, z, y, n, first, second = place()
    me = wide_of(z, y)
    wide = 2 * outer
    greet(partners(outer))
    other_n = (c, me, 1 - n)
    other_y = (c, wide_of(z, 1 - y), n)
    other_c = (1 - c, me, n)
    earlier = (c, wide_of(lax.rem(z + outer - 1, outer), y), n)
    main = pm.shape[3]
    width = 2 * (main + rem)
    rows, padded = q.shape
    span = k.shape[0]
    blocks = span // rows
    cols = 2 * hc
    block_rows = edge.shape[0]
    extra = pa.shape[2] - block_rows
    sent = []

    def go(copy):
        copy.start()
        sent.append(copy)

    def arrived(dst, recv):
        remote(dst, dst, recv, recv, other_c).wait_recv()

    feed = StagedScatter(
        outer, first, second, lambda z, y, n: pm.at[wide_of(z, y), n], m1, m2, m3, mo, sems[:8]
    )
    feed.stage(stage, ms, firsts)
    loads = [
        pltpu.make_async_copy(src, dst, ls.at[i])
        for i, (src, dst) in enumerate(
            (
                (wa_in.at[3], pool.at[0]),
                (k_in, k),
                (v_in, v),
                (wa_in.at[1], pool.at[1]),
                (wa_in.at[2], pool.at[2]),
                (wa_in.at[0], pool.at[0]),
                (x_in, v),
                (low1_in, k),
                (mixed_in, g),
                (lo.at[n], lo_out.at[:, pl.ds(pl.multiple_of(n * rows, LANES), rows)]),
            )
        )
    ]
    for copy in loads[:5] + loads[9:]:
        copy.start()
    feed.start()
    mine = lo_out.at[:, pl.ds(pl.multiple_of(n * rows, LANES), rows)]
    go(remote(lo.at[1 - n], mine, xs.at[2], xr.at[2], other_n))
    fill_mask(q_seg, k_seg, mask)
    branch[...] = grad_res[...].astype(BF)
    loads[0].wait()
    g[...] = dot(branch[...], pool[0], NT).astype(BF)
    loads[5].start()
    loads[1].wait()
    loads[2].wait()
    pairs = padded // LANES

    def some(begin, end):
        @pl.loop(begin, end)
        def _(i):
            at = pl.ds(pl.multiple_of(i * LANES, LANES), LANES)
            one, two, three = attend_back_pair(q[:, at], k[:, at], v[:, at], g[:, at], lse[i], mask)
            dq[:, at] = one
            dk[:, at] = two
            dv[:, at] = three

    steps = feed.steps()

    def pump(count):
        for _ in range(min(count, len(steps))):
            steps.pop(0)()

    some(0, pairs // 2)
    pump(1)
    some(pairs // 2, pairs)
    for copy in loads[6:9]:
        copy.start()
    sums[...] = sums_in[...]
    for copy in loads[3:7]:
        copy.wait()

    def input_part(j, extra_part):
        at = pl.ds(j * rows, rows)
        grad = dot(dk[at, :], pool[1], NN) + dot(dv[at, :], pool[2], NN)
        if extra_part:
            grad = grad + dot(dq[...], pool[0], NN)
        normed, scale = normed_rows(v[at, :].astype(F32), width)
        sums[0:1] += jnp.sum(grad * normed, 0, keepdims=True)
        sums[1:2] += jnp.sum(grad, 0, keepdims=True)
        back = norm_back(grad, normed, scale, vec[0:1], width)
        if extra_part:
            back = back + grad_res[...]
        store_packed(pg, (j,), back, main, rem)

    def x_back(j):
        go(remote(pg.at[1 - n, j], got_x.at[j], hs.at[j], hr.at[j], other_n))

    for j in (2, 1, 3, 0):
        input_part(j, False)
        x_back(j)
        if j == 1:
            pump(1)
    input_part(blocks - 1, True)
    x_back(blocks - 1)
    vx[0] = sums[...]
    go(remote(vx.at[0], vx.at[1], vs.at[0], vr.at[0], other_c))

    def products(s, left, right):
        size = 256
        for begin in range(0, padded, size):
            stop = min(begin + size, padded)
            pool[s, begin:stop, :] = dot(left[:, begin:stop], right, TN).astype(BF)

    for copy in loads[7:9]:
        copy.wait()
    products(3, g, branch[...])
    pump(1)
    products(0, dq, k[span - rows :, :])
    arrived(vx.at[1], vr.at[0])
    vz[z] = vx[0] + vx[1]
    for d in range(1, outer):
        device = (c, wide_of(lax.rem(z + d, outer), y), n)
        go(remote(vz.at[z], vz.at[z], vs.at[2 + d], vr.at[2 + d], device))
    products(1, dk, k[...])
    pump(2)
    products(2, dv, k[...])
    pump(1)

    def place_rows(i, core, out):
        for s in range(4):
            to = slice(s * hc, (s + 1) * hc)
            src = slice(i * cols + core * hc, i * cols + (core + 1) * hc)
            for h in range(2):
                out[h, to, :] = pool[s, src, h * main : (h + 1) * main]
            edge[to, :] = pool[s, src, 2 * main :]
        if block_rows > 4 * hc:
            gap = slice(4 * hc, block_rows)
            for h in range(2):
                out[h, gap, :] = jnp.zeros((block_rows - 4 * hc, main), BF)
            edge[gap, :] = jnp.zeros((block_rows - 4 * hc, LANES), BF)
        low = edge[...].astype(F32)
        for h in range(2):
            out[h, block_rows:, :] = squeezed(
                low[:, h * rem : (h + 1) * rem], extra, main, low[:, 2 * rem : 2 * rem + 1]
            ).astype(BF)

    def to_core(i):
        return remote(po.at[i % 2], pcore.at[i], cs.at[i], cr.at[i], other_c)

    for i in range(wide):
        if i >= 2:
            to_core(i - 2).wait_send()
        for core in range(2):
            pl.when(c == core)(functools.partial(place_rows, i, 1 - core, po.at[i % 2]))
        to_core(i).start()

    for i in range(wide):
        for core in range(2):
            pl.when(c == core)(functools.partial(place_rows, i, core, pa.at[i]))
    def fetch(i):
        arrived(pcore.at[i], cr.at[i])
        copy = pltpu.make_async_copy(pcore.at[i], po.at[i % 2], ps.at[i % 2])
        copy.start()
        return copy

    for i in range(max(wide - 2, 0), wide):
        to_core(i).wait_send()
    copies = [fetch(0)]
    for i in range(wide):
        if i + 1 < wide:
            copies.append(fetch(i + 1))
        copies[i].wait()
        for h in range(2):
            pa[i, h] = (pa[i, h].astype(F32) + po[i % 2, h].astype(F32)).astype(BF)
    heads = Scatter(
        outer, first, second, lambda z, y, n: pa.at[wide_of(z, y), n], a1, a2, a3, ao, sems[8:]
    )
    heads.start(0, 2)
    pump(len(steps))
    late = heads.steps()
    for d in range(1, outer):
        arrived(vz.at[lax.rem(z + outer - d, outer)], vr.at[2 + d])
    total = vz[0]
    for i in range(1, outer):
        total = total + vz[i]
    vx[2] = total
    go(remote(vx.at[2], vx.at[3], vs.at[1], vr.at[1], other_y))

    def summed(b):
        if b == 0:
            return jnp.where(n == 0, pg[n, 0].astype(F32), got_x[0].astype(F32))
        if b == 5:
            return jnp.where(n == 1, pg[n, 4].astype(F32), got_x[4].astype(F32))
        return pg[n, b - n].astype(F32) + got_x[b - 1 + n].astype(F32)

    for j in (2, 1, 3):
        arrived(got_x.at[j], hr.at[j])
    for b in range(2):
        out_y[b] = summed(2 + b).astype(BF)
    go(remote(out_y, got_y, xs.at[0], xr.at[0], other_y))
    heads.start(2)
    late.pop(0)()
    arrived(vx.at[3], vr.at[1])
    vx[4] = vx[2] + vx[3]
    go(remote(vx.at[4], vx.at[5], vs.at[2], vr.at[2], other_n))
    for j in (0, 4):
        arrived(got_x.at[j], hr.at[j])
    arrived(got_y, xr.at[0])
    for b in range(2):
        out_z[b] = (summed(b) + jnp.where(y == 1, got_y[b].astype(F32), 0.0)).astype(BF)
    go(remote(out_z, got_z, xs.at[1], xr.at[1], earlier))
    for _ in range(min(2, len(late))):
        late.pop(0)()
    feed.close(em, rem, es.at[0])
    for step in late:
        step()
    arrived(got_z, xr.at[1])
    for b in range(2):
        value = summed(4 + b) + jnp.where(y == 0, got_y[b].astype(F32), 0.0)
        value = value + got_z[b].astype(F32)
        at = slice(b * rows, (b + 1) * rows)
        xg[0:main, at] = value[0:rows].T.astype(BF)
        edge_x = jnp.concatenate([spread(value[rows:], rows, rem), jnp.zeros((rows, LANES - rem), F32)], 1)
        xg[main:, at] = edge_x.T[0:rem].astype(BF)
    arrived(vx.at[5], vr.at[2])
    total = vx[4] + vx[5]
    vec_out[:, 0:main] = jnp.where(n == 0, total[:, 0:main], total[:, main : 2 * main])
    edge_a, edge_b = total[:, 2 * main : 2 * main + rem], total[:, 2 * main + rem : 2 * main + 2 * rem]
    vec_out[:, main:] = jnp.where(n == 0, edge_a, edge_b)
    heads.close(ea, rem, es.at[1])
    loads[9].wait()
    arrived(lo_out.at[:, pl.ds(pl.multiple_of((1 - n) * rows, LANES), rows)], xr.at[2])
    for copy in sent:
        copy.wait_send()
    feed.finish()
    heads.finish()


def backward(grad_res, q, lse, q_seg, k_seg, vec, sums, k, v, wa, x5, low1, mixed, pm, lo, hc, fc2, rem):
    wide = pm.shape[0]
    outer = wide // 2
    rows, padded = q.shape
    span = k.shape[0]
    main = pm.shape[3]
    half = main + rem
    bm, bx = pm.shape[2:], (rows + rem_rows(rows, half), main)
    block_rows = up16(4 * hc)
    ba = (block_rows + rem_rows(block_rows, main + rem), main)
    vmem = pl.BlockSpec(memory_space=pltpu.VMEM)
    shape = jax.ShapeDtypeStruct
    few = max(outer - 1, 1)
    return pl.pallas_call(
        functools.partial(backward_kernel, outer, hc, rem),
        out_shape=(
            shape((2,) + bm, F32),
            shape((2,) + ba, F32),
            shape((2, fc2, LANES), F32),
            shape((2, block_rows, LANES), F32),
            shape((half, 2 * rows), BF),
            shape((sums.shape[0], half), F32),
            shape((half, 2 * rows), BF),
            shape((2 * outer,) + bm, BF),
            shape((outer,) + bm, BF),
            shape((few,) + bm, BF),
            shape((wide, 2) + ba, BF),
        ),
        in_specs=[vmem] * 7 + [ANY] * 8,
        out_specs=(vmem,) * 6 + (ANY,) * 5,
        scratch_shapes=[
            pltpu.VMEM((4, padded, padded), BF),
            pltpu.VMEM((span, padded), BF),
            pltpu.VMEM((span, padded), BF),
            pltpu.VMEM((span, padded), BF),
            pltpu.VMEM((span, padded), BF),
            pltpu.VMEM((rows, padded), BF),
            pltpu.VMEM((rows, padded), BF),
            pltpu.VMEM((rows, padded), BF),
            pltpu.VMEM((span, rows), F32),
            pltpu.VMEM((3,) + bm, BF),
            pltpu.VMEM((outer,) + bm, BF),
        ]
        + scatter_scratch(outer, ba)
        + [
            pltpu.VMEM((wide, 2) + ba, BF),
            pltpu.VMEM((2, 2) + ba, BF),
            pltpu.VMEM((block_rows, LANES), BF),
            pltpu.VMEM((2, span // rows) + bx, BF),
            pltpu.VMEM((5,) + bx, BF),
            pltpu.VMEM((2,) + bx, BF),
            pltpu.VMEM((2,) + bx, BF),
            pltpu.VMEM((2,) + bx, BF),
            pltpu.VMEM((2,) + bx, BF),
            pltpu.VMEM(sums.shape, F32),
            pltpu.VMEM((6,) + sums.shape, F32),
            pltpu.VMEM((outer,) + sums.shape, F32),
        ]
        + [DMA((10,)), DMA((3,)), DMA((3,)), DMA((5,)), DMA((5,)), DMA((wide,)), DMA((wide,))]
        + [DMA((2 + outer,)), DMA((2 + outer,)), DMA((2,)), DMA((3,)), DMA((2, 2))]
        + scatter_sems(outer)
        + scatter_sems(outer),
        compiler_params=pltpu.CompilerParams(
            collective_id=1, has_side_effects=True, vmem_limit_bytes=LIMIT
        ),
    )(grad_res, q, lse, q_seg, k_seg, vec, sums, k, v, wa, x5, low1, mixed, pm, lo)


def shards(
    layer_input,
    doc_segments,
    first_gain,
    first_shift,
    heads_weight,
    query_bias,
    value_bias,
    merge_weight,
    merge_bias,
    second_gain,
    second_shift,
    up_weight,
    up_bias,
    down_weight,
    down_bias,
    out_cotangent,
):
    parts = lax.axis_size("narrow")
    wide = lax.axis_size("wide")
    c, w, n = lax.axis_index("dp"), lax.axis_index("wide"), lax.axis_index("narrow")
    half = heads_weight.shape[0]
    width = half * parts
    padded = -(-width // LANES) * LANES
    cols = heads_weight.shape[2]
    units = up_weight.shape[1]
    hc, fc = cols // 2, up16(units // 2)
    short = fc - units // 2
    rows = layer_input.shape[0] // parts
    span = (REACH + 1) * rows

    by_half = heads_weight.transpose(1, 2, 0).reshape(3, 2, hc, half)
    heads_rows = lax.dynamic_index_in_dim(by_half, c, 1, False).reshape(3 * hc, half)
    merge_rows = lax.dynamic_slice_in_dim(merge_weight, c * hc, hc, 0)
    up_rows = lax.dynamic_slice_in_dim(up_weight, c * (units // 2), units // 2, 1).T
    down_rows = lax.dynamic_slice_in_dim(down_weight, c * (units // 2), units // 2, 0)
    up_rows = jnp.pad(up_rows, ((0, short), (0, 0)))
    down_rows = jnp.pad(down_rows, ((0, short), (0, 0)))
    line = lambda *v: jnp.pad(jnp.concatenate(v), (0, half - sum(e.shape[0] for e in v)))
    vectors = [first_gain, first_shift, merge_bias, second_gain, second_shift, down_bias]
    gap = up16(4 * hc) - 4 * hc
    sa = jnp.concatenate([heads_rows, merge_rows] + ([jnp.zeros((gap, half), BF)] if gap else []), 0)
    part = lambda v, size: lax.dynamic_slice_in_dim(v, c * size, size, 0)
    zero = lambda size: jnp.zeros((size,), BF)
    column_a = jnp.concatenate([part(query_bias, hc), zero(hc), part(value_bias, hc), zero(hc + gap)])
    sm = jnp.concatenate([up_rows, down_rows], 0)
    column_m = jnp.concatenate([part(up_bias, units // 2), zero(short + fc)])
    start = (w * parts + n) * rows
    ahead = jnp.pad(doc_segments, ((0, 0), (REACH * rows, 0)), constant_values=-1)
    segments = lax.dynamic_slice(ahead, (c, start), (1, span))
    k_seg = segments.reshape(span, 1)
    q_seg = segments[:, span - rows :]

    rem = widths(half)[1]
    cot_all, gm, wa, x5, low1, key, value, query, mixed, lse, residual, low2, vec = forward(
        layer_input.T, out_cotangent.T, pack(sa, column_a), pack(sm, column_m), q_seg, k_seg, vectors, hc, rem
    )
    pm, lo, grad_residual, sums = mlp(low2, cot_all, gm, residual, vec, fc, rem)

    mo, ao, em, ea, input_grad, lines, layer_output, _, _, _, _ = backward(
        grad_residual, query, lse, q_seg, k_seg, vec, sums, key, value, wa, x5, low1, mixed, pm, lo, hc, 2 * fc, rem
    )

    def total(block, edge, begin, size):
        at = slice(begin, begin + size)
        return jnp.concatenate([block[:, at], edge[:, at, :rem]], -1)

    input_grad, layer_output = input_grad.T, layer_output.T
    heads_total = total(ao, ea, 0, 3 * hc).reshape(2, 3, hc, half).transpose(3, 1, 0, 2).reshape(half, 3, cols)
    merge_total = total(ao, ea, 3 * hc, hc).reshape(cols, half)
    up_total = total(mo, em, 0, units // 2).reshape(units, half).T
    down_total = total(mo, em, fc, units // 2).reshape(units, half)
    up_bias_total = em[:, : units // 2, rem].reshape(units)
    query_total = ea[:, :hc, rem].reshape(cols)
    value_total = ea[:, 2 * hc : 3 * hc, rem].reshape(cols)
    return (
        layer_output,
        input_grad,
        lines[0],
        lines[1],
        heads_total,
        query_total,
        value_total,
        merge_total,
        lines[2],
        lines[3],
        lines[4],
        up_total,
        up_bias_total,
        down_total,
        lines[5],
    )


def solution(mesh):
    return jax.shard_map(
        shards,
        mesh=mesh,
        in_specs=(
            P(("dp", "wide"), "narrow"),
            P(),
            P("narrow"),
            P("narrow"),
            P("narrow", None, "wide"),
            P("wide"),
            P("wide"),
            P("wide", "narrow"),
            P("narrow"),
            P("narrow"),
            P("narrow"),
            P("narrow", "wide"),
            P("wide"),
            P("wide", "narrow"),
            P("narrow"),
            P(("dp", "wide"), "narrow"),
        ),
        out_specs=(
            P(("dp", "wide"), "narrow"),
            P(("dp", "wide"), "narrow"),
            P("narrow"),
            P("narrow"),
            P("narrow", None, "wide"),
            P("wide"),
            P("wide"),
            P("wide", "narrow"),
            P("narrow"),
            P("narrow"),
            P("narrow"),
            P("narrow", "wide"),
            P("wide"),
            P("wide", "narrow"),
            P("narrow"),
        ),
        check_vma=False,
    )
```

```python
import functools

import jax
import jax.numpy as jnp
from jax import lax
from jax.experimental import pallas as pl
from jax.experimental.pallas import tpu as pltpu
from jax.sharding import PartitionSpec as P

HEAD = 64
REACH = 4
EPS = 1e-05
NEGATIVE = -1e30
LANES = 128
BF = jnp.bfloat16
F32 = jnp.float32
MESH = pl.DeviceIdType.MESH
ANY = pl.BlockSpec(memory_space=pl.ANY)
DMA = pltpu.SemaphoreType.DMA
SCALE = HEAD ** (-0.5)
LIMIT = 62 * 1024 * 1024


def widths(half):
    main = half // LANES * LANES
    return main, half - main


def rem_rows(rows, half):
    main, rem = widths(half)
    return up16(-(-rows // (main // rem)))


def up16(rows):
    return -(-rows // 16) * 16


def pack(block, column=None):
    rows, half = block.shape[-2:]
    main, rem = widths(half)
    count = main // rem
    extra = rem_rows(rows, half)
    lead = block.shape[:-2]
    none = [(0, 0)] * len(lead)
    tail = jnp.pad(block[..., main:], none + [(0, count * extra - rows), (0, 0)])
    tail = jnp.swapaxes(tail.reshape(lead + (count, extra, rem)), -2, -3).reshape(lead + (extra, main))
    if column is not None:
        base, groups = column_base(rows, half), -(-rows // extra)
        column = jnp.pad(column, (0, groups * extra - rows)).reshape(groups, extra).T
        tail = jnp.concatenate([tail[:, :base], column, tail[:, base + groups :]], 1)
    return jnp.concatenate([block[..., :main], tail], -2)


def column_base(rows, half):
    return -(-rows // rem_rows(rows, half)) * widths(half)[1]


def column_of(block, rows, half):
    base, extra = column_base(rows, half), rem_rows(rows, half)
    groups = -(-rows // extra)
    tail = block[..., rows : rows + extra, base : base + groups]
    return jnp.swapaxes(tail, -1, -2).reshape(block.shape[:-2] + (groups * extra,))[..., :rows]


def unpack(block, rows, half):
    main, rem = widths(half)
    count = main // rem
    extra = rem_rows(rows, half)
    lead = block.shape[:-2]
    tail = block[..., rows : rows + extra, :].reshape(lead + (extra, count, rem))
    tail = jnp.swapaxes(tail, -2, -3).reshape(lead + (count * extra, rem))[..., :rows, :]
    return block[..., :rows, :], tail


def unpack_half(block, rows, half):
    return jnp.concatenate(unpack(block, rows, half), -1)


def join(blocks, rows, half):
    body, tail = unpack(blocks, rows, half)
    return jnp.concatenate([body[0], body[1], tail[0], tail[1]], -1)


def halves(full):
    half = full.shape[-1] // 2
    main, rem = widths(half)
    edge = 2 * main
    return jnp.stack(
        [
            jnp.concatenate([full[..., :main], full[..., edge : edge + rem]], -1),
            jnp.concatenate([full[..., main:edge], full[..., edge + rem :]], -1),
        ]
    )


def place():
    c, w, n = lax.axis_index("dp"), lax.axis_index("wide"), lax.axis_index("narrow")
    z, y = lax.div(w, 2), lax.rem(w, 2)
    first = (y + c * (1 - 2 * y), n + (1 - c) * (1 - 2 * n))
    second = (y + (1 - c) * (1 - 2 * y), n + c * (1 - 2 * n))
    return c, z, y, n, first, second


def wide_of(z, y):
    return z * 2 + y


def remote(src, dst, send, recv, device):
    return pltpu.make_async_remote_copy(
        src_ref=src, dst_ref=dst, send_sem=send, recv_sem=recv, device_id=device, device_id_type=MESH
    )


def greet(devices):
    barrier = pltpu.get_barrier_semaphore()
    for device in devices:
        pl.semaphore_signal(barrier, inc=1, device_id=device, device_id_type=MESH)
    pl.semaphore_wait(barrier, len(devices))


def partners(outer):
    c, z, y, n, _, _ = place()
    out = [(c, wide_of(lax.rem(z + d, outer), y), n) for d in range(1, outer)]
    out.append((c, wide_of(z, 1 - y), n))
    out.append((c, wide_of(z, y), 1 - n))
    out.append((1 - c, wide_of(z, y), n))
    return out


class Gather:
    def __init__(self, outer, src, out, both, first, second, sems, part=None):
        self.outer, self.src, self.out, self.both = outer, src, out, both
        self.part = outer if part is None else part
        self.first, self.second = first, second
        self.zs, self.zr, self.fs, self.fr, self.ss, self.sr, self.cs, self.cr, self.local = sems
        self.sent = []

    def block(self, z, y, n):
        c = lax.axis_index("dp")
        return self.out.at[c, wide_of(z, y), n] if self.both else self.out.at[wide_of(z, y), n]

    def go(self, copy):
        copy.start()
        self.sent.append(copy)

    def z_at(self, d):
        return lax.rem(place()[1] + self.outer - d, self.outer)

    def to_first(self, d, src):
        c, z, y, n, _, _ = place()
        first, second = self.first, self.second
        device = (c, wide_of(z, first[0]), first[1])
        self.go(remote(src, self.block(self.z_at(d), y, n), self.fs.at[d], self.fr.at[d], device))

    def to_second(self, d, src, k):
        if d >= self.part:
            return
        c, z, y, n, _, _ = place()
        first, second = self.first, self.second
        device = (c, wide_of(z, second[0]), second[1])
        dst = self.block(self.z_at(d), y, n) if k == 0 else self.block(self.z_at(d), *first)
        i = k * self.outer + d
        self.go(remote(src, dst, self.ss.at[i], self.sr.at[i], device))

    def to_core(self, i, src, dst):
        if self.both:
            c, z, y, n, _, _ = place()
            self.go(remote(src, dst, self.cs.at[i], self.cr.at[i], (1 - c, wide_of(z, y), n)))

    def start(self):
        c, z, y, n, _, _ = place()
        first, second = self.first, self.second
        own = self.block(z, y, n)
        self.keep = pltpu.make_async_copy(self.src, own, self.local)
        self.keep.start()
        for d in range(1, self.outer):
            device = (c, wide_of(lax.rem(z + d, self.outer), y), n)
            self.go(remote(self.src, own, self.zs.at[d - 1], self.zr.at[d - 1], device))

    def start_rest(self):
        c, z, y, n, _, _ = place()
        own = self.block(z, y, n)
        self.to_first(0, self.src)
        self.to_second(0, self.src, 0)
        self.to_core(0, self.src, own)

    def arrived(self, dst, recv):
        c, z, y, n, _, _ = place()
        remote(dst, dst, recv, recv, (1 - c, wide_of(z, y), n)).wait_recv()

    def along_z(self, d):
        c, z, y, n, _, _ = place()
        first, second = self.first, self.second
        got = self.block(self.z_at(d), y, n)
        self.arrived(got, self.zr.at[d - 1])
        self.to_first(d, got)
        self.to_second(d, got, 0)
        self.to_core(d, got, got)

    def along_first(self, d):
        c, z, y, n, _, _ = place()
        first, second = self.first, self.second
        got = self.block(self.z_at(d), *first)
        self.arrived(got, self.fr.at[d])
        self.to_second(d, got, 1)
        self.to_core(self.outer + d, got, got)

    def along_second(self, d, k):
        if d >= self.part:
            return
        c, z, y, n, _, _ = place()
        first, second = self.first, self.second
        got = self.block(self.z_at(d), *second) if k == 0 else self.block(self.z_at(d), 1 - y, 1 - n)
        i = k * self.outer + d
        self.arrived(got, self.sr.at[i])
        self.to_core(2 * self.outer + i, got, got)

    def finish(self):
        c, z, y, n, _, _ = place()
        first, second = self.first, self.second
        if self.both:
            spots = [(y, n), first, second, (1 - y, 1 - n)]
            for k, spot in enumerate(spots):
                for d in range(self.outer):
                    got = self.out.at[1 - c, wide_of(self.z_at(d), spot[0]), spot[1]]
                    self.arrived(got, self.cr.at[k * self.outer + d])
        self.keep.wait()
        for copy in self.sent:
            copy.wait_send()


def gather_sems(outer):
    return [
        DMA((outer,)),
        DMA((outer,)),
        DMA((outer,)),
        DMA((outer,)),
        DMA((2 * outer,)),
        DMA((2 * outer,)),
        DMA((4 * outer,)),
        DMA((4 * outer,)),
        DMA,
    ]


class Scatter:
    def __init__(self, outer, first, second, part, one, two, three, fin, sems):
        self.outer, self.part, self.first, self.second = outer, part, first, second
        self.one, self.two, self.three, self.fin = one, two, three, fin
        self.ss, self.sr, self.fs, self.fr, self.zs, self.zr, self.cs, self.cr = sems
        self.sent, self.along_first = [], {}

    def go(self, copy):
        copy.start()
        self.sent.append(copy)

    def arrived(self, dst, recv):
        c, z, y, n, _, _ = place()
        remote(dst, dst, recv, recv, (1 - c, wide_of(z, y), n)).wait_recv()

    def z_at(self, d):
        return lax.rem(place()[1] + d, self.outer)

    def order(self):
        return [d for d in range(1, self.outer)] + [0]

    def start(self, begin=0, end=None):
        c, z, y, n, _, _ = place()
        first, second = self.first, self.second
        device = (c, wide_of(z, second[0]), second[1])
        for d in self.order()[begin:end]:
            for k, spot in ((1, (1 - y, 1 - n)), (0, second)):
                i = k * self.outer + d
                self.go(
                    remote(self.part(self.z_at(d), *spot), self.one.at[i], self.ss.at[i], self.sr.at[i], device)
                )

    def steps(self):
        order = self.order()
        out = [functools.partial(self.to_first, order[0])]
        for here, there in zip(order[1:], order):
            out.append(functools.partial(self.to_first, here))
            out.append(functools.partial(self.to_z, there))
        return out + [functools.partial(self.to_z, order[-1])]

    def read(self, *refs):
        return [ref[...].astype(F32) for ref in refs]

    def to_first(self, d):
        c, z, y, n, _, _ = place()
        first, second = self.first, self.second
        device = (c, wide_of(z, first[0]), first[1])
        i = self.outer + d
        self.arrived(self.one.at[i], self.sr.at[i])
        own, got = self.read(self.part(self.z_at(d), *first), self.one.at[i])
        src = self.for_first(d)
        src[...] = (got + own).astype(BF)
        self.along_first[d] = remote(src, self.two.at[d], self.fs.at[d], self.fr.at[d], device)
        self.go(self.along_first[d])

    def for_first(self, d):
        return self.one.at[self.outer + d]

    def for_z(self, d):
        return self.one.at[d]

    def to_z(self, d):
        c, z, y, n, _, _ = place()
        self.arrived(self.one.at[d], self.sr.at[d])
        self.arrived(self.two.at[d], self.fr.at[d])
        own, one, two = self.read(self.part(self.z_at(d), y, n), self.one.at[d], self.two.at[d])
        value = (one + own).astype(BF).astype(F32) + two
        if d == 0:
            self.fin[c] = value
        else:
            src = self.for_z(d)
            src[...] = value.astype(BF)
            device = (c, wide_of(self.z_at(d), y), n)
            self.go(remote(src, self.three.at[d - 1], self.zs.at[d - 1], self.zr.at[d - 1], device))

    def close(self, edges, rem, edge_sems):
        c, z, y, n, _, _ = place()
        for d in range(1, self.outer):
            self.arrived(self.three.at[d - 1], self.zr.at[d - 1])
        value = self.fin[c]
        for d in range(1, self.outer):
            value = value + self.read(self.three.at[d - 1])[0]
        self.fin[c] = value
        other = (1 - c, wide_of(z, y), n)
        self.go(remote(self.fin.at[c], self.fin.at[c], self.cs, self.cr, other))
        rows = edges.shape[1]
        tail = value[rows:]
        base = -(-rows // tail.shape[0]) * rem
        empty = jnp.zeros((rows, LANES - rem - 1), F32)
        edges[c] = jnp.concatenate([spread(tail, rows, rem), spread(tail[:, base:], rows, 1), empty], 1)
        self.edges, self.edge_recv = edges, edge_sems.at[1]
        self.go(remote(edges.at[c], edges.at[c], edge_sems.at[0], edge_sems.at[1], other))

    def finish(self):
        c = lax.axis_index("dp")
        self.arrived(self.fin.at[1 - c], self.cr)
        self.arrived(self.edges.at[1 - c], self.edge_recv)
        for copy in self.sent:
            copy.wait_send()


class StagedScatter(Scatter):
    def stage(self, buffers, sems, firsts):
        self.buffers, self.load_sems, self.firsts = buffers, sems, firsts

    def read(self, *refs):
        copies = [
            pltpu.make_async_copy(ref, self.buffers.at[i], self.load_sems.at[i]) for i, ref in enumerate(refs)
        ]
        for copy in copies:
            copy.start()
        for copy in copies:
            copy.wait()
        return [self.buffers[i].astype(F32) for i in range(len(refs))]

    def for_first(self, d):
        return self.firsts.at[d]

    def for_z(self, d):
        slot = self.firsts.at[d]
        copy = self.along_first.pop(d)
        copy.wait_send()
        self.sent = [e for e in self.sent if e is not copy]
        return slot


def scatter_scratch(outer, block):
    return [
        pltpu.VMEM((2 * outer,) + block, BF),
        pltpu.VMEM((outer,) + block, BF),
        pltpu.VMEM((max(outer - 1, 1),) + block, BF),
    ]


def scatter_sems(outer):
    return [
        DMA((2 * outer,)),
        DMA((2 * outer,)),
        DMA((outer,)),
        DMA((outer,)),
        DMA((outer,)),
        DMA((outer,)),
        DMA,
        DMA,
    ]


def dot(left, right, dims):
    return lax.dot_general(left, right, ((dims[0], dims[1]), ((), ())), preferred_element_type=F32)


NN = ((1,), (0,))
NT = ((1,), (1,))
TN = ((0,), (0,))


def spread(tail, rows, rem):
    extra = tail.shape[0]
    count = -(-rows // extra)
    return jnp.concatenate([tail[:, k * rem : (k + 1) * rem] for k in range(count)], 0)[:rows]


def squeezed(block, extra, main, column=None):
    parts = []
    for piece in (block,) if column is None else (block, column):
        rows, each = piece.shape
        count = -(-rows // extra)
        short = count * extra - rows
        if short:
            piece = jnp.concatenate([piece, jnp.zeros((short, each), piece.dtype)], 0)
        parts += [piece[k * extra : (k + 1) * extra] for k in range(count)]
    used = sum(p.shape[1] for p in parts)
    if used < main:
        parts.append(jnp.zeros((extra, main - used), block.dtype))
    return jnp.concatenate(parts, 1)


def store_rows(dst, src, main, rem):
    rows = src.shape[1] // 2
    for i in range(2):
        at = slice(i * rows, (i + 1) * rows)
        dst[i, 0:rows, :] = src[0:main, at].astype(F32).T.astype(dst.dtype)
        low = src[main : main + rem, at].astype(F32).T
        dst[i, rows:, :] = squeezed(low, dst.shape[1] - rows, main).astype(dst.dtype)


def store_packed(ref, index, value, main, rem):
    rows = value.shape[0]
    for h in range(2):
        at = ref.at[(h,) + index]
        at[0:rows, :] = value[:, h * main : (h + 1) * main].astype(ref.dtype)
        low = value[:, 2 * main + h * rem : 2 * main + (h + 1) * rem]
        at[rows:, :] = squeezed(low, at.shape[0] - rows, main).astype(ref.dtype)


def gelu_and_slope(u):
    share = 0.5 * (1.0 + lax.erf(u * 0.7071067811865476))
    return u * share, share + u * (jnp.exp(-0.5 * u * u) * 0.3989422804014327)


def mlp_kernel(
    wide, fc, rem, low2, cot_in, gm, residual, vec,
    pm, lo, grad_res, sums,
    weights, grads, tails, cot, low2_all, acc, got, wsem, rsend, rrecv, psem, xs, xr
):
    c, z, y, n, first, second = place()
    outer = wide // 2
    part = (outer + 1) // 2
    other = (1 - c, wide_of(z, y), n)
    beside = (c, wide_of(z, second[0]), second[1])
    rows, padded = low2.shape
    main = gm.shape[3]
    width = 2 * (main + rem)
    extra = gm.shape[2] - 2 * fc
    nf = wide * fc
    base = -(-2 * fc // extra) * rem
    greet([other, beside])
    mine, theirs = pl.ds(c * rows, rows), pl.ds((1 - c) * rows, rows)
    swap_low = remote(low2, low2_all.at[mine], xs.at[0], xr.at[0], other)
    swap_low.start()
    spots = [(y, n), first, second, (1 - y, 1 - n)]

    def pieces(d, spot):
        src = gm.at[wide_of(lax.rem(z + outer - d, outer), spot[0]), spot[1]]
        lanes = pl.ds(pl.multiple_of(spot[1] * main, LANES), main)
        out = []
        for k in range(2):
            at = pl.ds(pl.multiple_of((2 * d + spot[0]) * fc, 16), fc)
            out.append((src.at[pl.ds(k * fc, fc)], weights.at[k, at, lanes]))
        return out + [(src.at[pl.ds(2 * fc, extra)], tails.at[2 * d + spot[0], spot[1]])]

    def local(d):
        return [
            pltpu.make_async_copy(src, dst, wsem.at[d, i, k])
            for i, spot in enumerate(spots if d < part else spots[:2])
            for k, (src, dst) in enumerate(pieces(d, spot))
        ]

    def afar(d):
        return [
            remote(src, dst, rsend.at[d - part, i, k], rrecv.at[d - part, i, k], beside)
            for i, spot in enumerate(spots[:2])
            for k, (src, dst) in enumerate(pieces(d, spot))
        ]

    def landed(d):
        for i, spot in enumerate(spots[2:]):
            for k, (_, dst) in enumerate(pieces(d, spot)):
                remote(dst, dst, rrecv.at[d - part, i, k], rrecv.at[d - part, i, k], other).wait_recv()

    for d in range(part, outer):
        for copy in afar(d):
            copy.start()
    for d in range(outer):
        for copy in local(d):
            copy.start()

    low2_all[mine] = low2[...]
    for k in range(2):
        span = slice(k * rows, (k + 1) * rows)
        for h in range(2):
            cot[span, h * main : (h + 1) * main] = cot_in[k, h, 0:rows, :]
        cot[span, 2 * main :] = edge_tile([cot_in[k, h, rows:, :] for h in range(2)], rows, rem)

    def ready(begin, end):
        for d in range(begin, end):
            for copy in local(d):
                copy.wait()
            if d >= part:
                landed(d)
        for i in range(2 * begin, 2 * end):
            both = edge_tile([tails[i, h] for h in range(2)], 2 * fc, rem, base)
            for k in range(2):
                weights[k, i * fc : (i + 1) * fc, 2 * main :] = both[k * fc : (k + 1) * fc]

    ready(0, part)
    done = 2 * part * fc // 256 * 256
    acc[...] = jnp.zeros_like(acc)
    swap_low.wait_recv()

    def step(start, size):
        at = pl.ds(start, size)
        before = dot(low2_all[...], weights[0, at, :], NT)
        hidden, slope = gelu_and_slope(before)
        hidden = hidden.astype(BF)
        acc[0] += dot(hidden, weights[1, at, :], NN)
        grads[1, at, :] = dot(hidden, cot[...], TN).astype(BF)
        grad = dot(cot[...], weights[1, at, :], NT) * slope
        grad = grad.astype(BF)
        acc[1] += dot(grad, weights[0, at, :], NN)
        grads[0, at, :] = dot(grad, low2_all[...], TN).astype(BF)

    size = 256

    def steps(begin, end):
        full = (end - begin) // size

        @pl.loop(0, full)
        def _(j):
            step(pl.multiple_of(begin + j * size, size), size)

        if (end - begin) % size:
            step(begin + full * size, (end - begin) % size)

    steps(0, done)
    for d in range(part, outer):
        ready(d, d + 1)
        reach = nf if d == outer - 1 else 2 * (d + 1) * fc // size * size
        steps(done, reach)
        done = reach

    swap_acc = remote(acc.at[:, theirs], got, xs.at[1], xr.at[1], other)
    swap_acc.start()

    def grad_copies(i):
        dst = pm.at[wide_of(lax.rem(z + outer - i // 2, outer), i % 2)]
        out = []
        for h in range(2):
            for k in range(2):
                src = grads.at[k, i * fc : (i + 1) * fc, h * main : (h + 1) * main]
                out.append(pltpu.make_async_copy(src, dst.at[h, pl.ds(k * fc, fc)], psem.at[i, h, k]))
            out.append(pltpu.make_async_copy(tails.at[i, h], dst.at[h, pl.ds(2 * fc, extra)], psem.at[i, h, 2]))
        return out

    for i in range(wide):
        low = jnp.concatenate([grads[k, i * fc : (i + 1) * fc, 2 * main :] for k in range(2)], 0).astype(F32)
        for h in range(2):
            tails[i, h] = squeezed(
                low[:, h * rem : (h + 1) * rem], extra, main, low[:, 2 * rem : 2 * rem + 1]
            ).astype(BF)
        for copy in grad_copies(i):
            copy.start()

    swap_acc.wait_recv()
    result = residual[...] + (acc[0, mine] + got[0]) + vec[5:6]
    for h in range(2):
        lo[h, 0:main, :] = result[:, h * main : (h + 1) * main].T.astype(BF)
    edge = result[:, 2 * main :].T
    for h in range(2):
        lo[h, main:, :] = edge[h * rem : (h + 1) * rem].astype(BF)
    normed2, scale2 = normed_rows(residual[...], width)
    grad_low2 = acc[1, mine] + got[1]
    grad_out = cot[mine].astype(F32)
    lane = lax.broadcasted_iota(jnp.int32, grad_out.shape, 1)
    total = jnp.where(lane < width, grad_out + norm_back(grad_low2, normed2, scale2, vec[3:4], width), 0.0)
    grad_res[...] = total
    sums[...] = jnp.zeros_like(sums)
    sums[2:3] = jnp.sum(total.astype(BF).astype(F32), 0, keepdims=True)
    sums[3:4] = jnp.sum(grad_low2 * normed2, 0, keepdims=True)
    sums[4:5] = jnp.sum(grad_low2, 0, keepdims=True)
    sums[5:6] = jnp.sum(grad_out, 0, keepdims=True)

    for i in range(wide):
        for copy in grad_copies(i):
            copy.wait()
    for d in range(part, outer):
        for copy in afar(d):
            copy.wait_send()
    swap_low.wait_send()
    swap_acc.wait_send()


def mlp(low2, cot_in, gm, residual, vec, fc, rem):
    wide = gm.shape[0]
    rows, padded = low2.shape
    nf = wide * fc
    main = gm.shape[3]
    extra = gm.shape[2] - 2 * fc
    vmem = pl.BlockSpec(memory_space=pltpu.VMEM)
    return pl.pallas_call(
        functools.partial(mlp_kernel, wide, fc, rem),
        out_shape=(
            jax.ShapeDtypeStruct(gm.shape, BF),
            jax.ShapeDtypeStruct((2, main + rem, rows), BF),
            jax.ShapeDtypeStruct((rows, padded), F32),
            jax.ShapeDtypeStruct((16, padded), F32),
        ),
        in_specs=[vmem, vmem, ANY, vmem, vmem],
        out_specs=(ANY, vmem, vmem, vmem),
        scratch_shapes=[
            pltpu.VMEM((2, nf, padded), BF),
            pltpu.VMEM((2, nf, padded), BF),
            pltpu.VMEM((wide, 2, extra, main), BF),
            pltpu.VMEM((2 * rows, padded), BF),
            pltpu.VMEM((2 * rows, padded), BF),
            pltpu.VMEM((2, 2 * rows, padded), F32),
            pltpu.VMEM((2, rows, padded), F32),
            DMA((wide // 2, 4, 3)),
            DMA((wide // 2, 2, 3)),
            DMA((wide // 2, 2, 3)),
            DMA((wide, 2, 3)),
            DMA((2,)),
            DMA((2,)),
        ],
        compiler_params=pltpu.CompilerParams(
            collective_id=2, has_side_effects=True, vmem_limit_bytes=LIMIT
        ),
    )(low2, cot_in, gm, residual, vec)


def fill_mask(q_seg, k_seg, mask):
    keys, queries = mask.shape
    key = lax.broadcasted_iota(jnp.int32, (keys, queries), 0)
    query = lax.broadcasted_iota(jnp.int32, (keys, queries), 1) + (keys - queries)
    allowed = (k_seg[...] == q_seg[...]) & (key <= query)
    mask[...] = jnp.where(allowed, 0.0, NEGATIVE)


def turned(block):
    return block.astype(F32).T


def attend_pair(q, k, v, mask):
    q_t = turned(q) * SCALE
    row = lax.broadcasted_iota(jnp.int32, q_t.shape, 0)
    parts, logs = [], []
    for h in range(2):
        mine = (row >= h * HEAD) & (row < (h + 1) * HEAD)
        s = dot(k, jnp.where(mine, q_t, 0.0).astype(BF), NN) + mask[...]
        top = jnp.max(s, 0, keepdims=True)
        p = jnp.exp(s - top)
        total = jnp.sum(p, 0, keepdims=True)
        p = (p * (1.0 / total)).astype(BF)
        parts.append(dot(v, p, TN)[h * HEAD : (h + 1) * HEAD])
        logs.append(top + jnp.log(total))
    return jnp.concatenate(parts, 0).T.astype(BF), logs


def normed_rows(values, width):
    lane = lax.broadcasted_iota(jnp.int32, values.shape, 1)
    mean = jnp.sum(values, 1, keepdims=True) * (1.0 / width)
    centred = jnp.where(lane < width, values - mean, 0.0)
    scale = lax.rsqrt(jnp.sum(centred * centred, 1, keepdims=True) * (1.0 / width) + EPS)
    return centred * scale, scale


def norm_back(grad, normed, scale, gain, width):
    lane = lax.broadcasted_iota(jnp.int32, grad.shape, 1)
    scaled = jnp.where(lane < width, grad * gain, 0.0)
    first = jnp.sum(scaled, 1, keepdims=True) * (1.0 / width)
    second = jnp.sum(scaled * normed, 1, keepdims=True) * (1.0 / width)
    return scale * (scaled - first - normed * second)


def edge_tile(tails, rows, rem, base=None):
    tails = [t.astype(F32) for t in tails]
    parts = [spread(t, rows, rem) for t in tails]
    used = 2 * rem
    if base is not None:
        parts.append(spread(tails[0][:, base:], rows, 1))
        used += 1
    parts.append(jnp.zeros((rows, LANES - used), F32))
    return jnp.concatenate(parts, 1).astype(BF)


def forward_kernel(
    outer, hc, rem, x_in, cot_in, sa, sm, q_seg, k_seg, v0, v1, v2, v3, v4, v5,
    cot_out, gm, wa_out, x_out, low1_out, k_out, v_out, q, mixed, lse, residual, low2, vec,
    xin, cot, lines, ga, xs6, wa, x5, low1, k, v, mask, xs, xr, hs, hr, ks, kr, ls, os, *sems
):
    c, z, y, n, first, second = place()
    me = wide_of(z, y)
    wide = 2 * outer
    for src, dst in ((x_in, xin), (cot_in, cot)):
        store_rows(dst, src, sa.shape[1], rem)
    lines[...] = jnp.zeros_like(lines)
    for i, line in enumerate((v0, v1, v2, v3, v4, v5)):
        lines[n, i : i + 1, :] = line[...].astype(F32).reshape(1, -1)
    greet(partners(outer))
    other_n = (c, me, 1 - n)
    other_y = (c, wide_of(z, 1 - y), n)
    other_c = (1 - c, me, n)
    later = (c, wide_of(lax.rem(z + 1, outer), y), n)
    main = sa.shape[1]
    width = 2 * (main + rem)
    rows = q.shape[0]
    span = x5.shape[0]
    cols = 2 * hc
    sent = []

    def go(copy):
        copy.start()
        sent.append(copy)

    def arrived(dst, recv):
        remote(dst, dst, recv, recv, other_c).wait_recv()

    def x_send(j):
        src = xs6.at[n, j + 1 - n] if j < 4 else xin.at[1 - n]
        go(remote(src, xs6.at[n, j + 1 - n], hs.at[j], hr.at[j], other_n))

    own = xs6.at[n, pl.ds(4, 2)]
    keep = pltpu.make_async_copy(xin, own, ls.at[0])
    keep.start()
    keep_cot = pltpu.make_async_copy(cot.at[n], cot_out.at[c, n], ls.at[1])
    keep_cot.start()
    go(remote(lines.at[n], lines.at[n], xs.at[2], xr.at[2], other_n))
    go(remote(xin, xs6.at[n, pl.ds(0, 2)], xs.at[0], xr.at[0], later))
    x_send(4)
    heads = Gather(outer, sa, ga, True, (y, 1 - n), (1 - y, n), sems[:9])
    heads.start()
    heads.start_rest()
    fill_mask(q_seg, k_seg, mask)
    wa[:, width:, :] = jnp.zeros((4, wa.shape[1] - width, wa.shape[2]), BF)
    arrived(xs6.at[n, pl.ds(0, 2)], xr.at[0])
    keep.wait()
    x_send(0)
    go(remote(xs6.at[n, pl.ds(4 * (1 - y), 2)], xs6.at[n, pl.ds(2, 2)], xs.at[1], xr.at[1], other_y))
    for d in range(1, outer):
        heads.along_z(d)
    feed = Gather(outer, sm, gm, False, first, second, sems[9:], (outer + 1) // 2)
    feed.start()
    arrived(xs6.at[n, pl.ds(2, 2)], xr.at[1])
    for j in (1, 2, 3):
        x_send(j)
    for d in range(outer):
        heads.along_first(d)
    go(remote(cot.at[1 - n], cot_out.at[c, n], ks.at[0], kr.at[0], other_n))
    go(remote(cot.at[n], cot_out.at[c, n], ks.at[1], kr.at[1], other_c))
    feed.start_rest()

    arrived(lines.at[1 - n], xr.at[2])
    row = lax.broadcasted_iota(jnp.int32, (8, LANES), 0)
    lane = lax.broadcasted_iota(jnp.int32, (8, LANES), 1)
    unit = jnp.where(((row == 1) | (row == 4)) & (lane == 2 * rem), 1.0, 0.0)
    vec[...] = jnp.zeros_like(vec)
    for h in range(2):
        vec[0:8, h * main : (h + 1) * main] = lines[h, :, 0:main]
    edges = [lines[h, :, main:] for h in range(2)]
    vec[0:8, 2 * main :] = unit + jnp.concatenate(edges + [jnp.zeros((8, LANES - 2 * rem), F32)], 1)
    for j in range(5):
        arrived(xs6.at[1 - n, j + n], hr.at[j])
    for j in range(5):
        at = slice(j * rows, (j + 1) * rows)
        for h in range(2):
            x5[at, h * main : (h + 1) * main] = xs6[h, n + j, 0:rows, :]
        x5[at, 2 * main :] = edge_tile([xs6[h, n + j, rows:, :] for h in range(2)], rows, rem)
    outs = [pltpu.make_async_copy(x5, x_out, os.at[0])]
    outs[0].start()
    for kk in range(2):
        for d in range(outer):
            heads.along_second(d, kk)
    heads.finish()

    block_rows = up16(4 * hc)
    extra = ga.shape[3] - block_rows
    base = -(-block_rows // extra) * rem
    for i in range(wide):
        for half in range(2):
            edge = edge_tile([ga[half, i, h, block_rows:, :] for h in range(2)], block_rows, rem, base)
            for s in range(4):
                src = slice(s * hc, (s + 1) * hc)
                to = slice(i * cols + half * hc, i * cols + (half + 1) * hc)
                for h in range(2):
                    wa[s, to, h * main : (h + 1) * main] = ga[half, i, h, src, :]
                wa[s, to, 2 * main :] = edge[src]
    outs.append(pltpu.make_async_copy(wa, wa_out, os.at[1]))
    outs[1].start()
    feed.along_z(1)

    @pl.loop(0, span // rows)
    def _(j):
        at = pl.ds(pl.multiple_of(j * rows, rows), rows)
        normed, _ = normed_rows(x5[at, :].astype(F32), width)
        low1[at, :] = (normed * vec[0:1] + vec[1:2]).astype(BF)
        k[at, :] = dot(low1[at, :], wa[1], NT).astype(BF)
        v[at, :] = dot(low1[at, :], wa[2], NT).astype(BF)

    q[...] = dot(low1[span - rows :, :], wa[0], NT).astype(BF)
    for src, dst in ((low1, low1_out), (k, k_out), (v, v_out)):
        outs.append(pltpu.make_async_copy(src, dst, os.at[len(outs)]))
        outs[-1].start()

    pairs = q.shape[1] // LANES
    lse[...] = jnp.zeros_like(lse)

    def some(begin, end):
        @pl.loop(begin, end)
        def _(i):
            at = pl.ds(pl.multiple_of(i * LANES, LANES), LANES)
            out, logs = attend_pair(q[:, at], k[:, at], v[:, at], mask)
            mixed[:, at] = out
            for h in range(2):
                lse[i, pl.ds(h, 1), :] = logs[h]

    for d in range(2, outer):
        feed.along_z(d)
    cuts = [0, pairs // 3, 2 * pairs // 3, pairs]
    some(cuts[0], cuts[1])
    for d in range(feed.part):
        feed.along_first(d)
    arrived(cot_out.at[c, 1 - n], kr.at[0])
    go(remote(cot_out.at[c, 1 - n], cot_out.at[c, 1 - n], ks.at[2], kr.at[2], other_c))
    some(cuts[1], cuts[2])
    some(cuts[2], cuts[3])
    value = x5[span - rows :, :].astype(F32) + dot(mixed[...], wa[3], NN) + vec[2:3]
    residual[...] = value
    normed, _ = normed_rows(value, width)
    low2[...] = (normed * vec[3:4] + vec[4:5]).astype(BF)

    for d in range(feed.part, outer):
        feed.along_first(d)
    for kk in range(2):
        for d in range(outer):
            feed.along_second(d, kk)
    arrived(cot_out.at[1 - c, n], kr.at[1])
    arrived(cot_out.at[1 - c, 1 - n], kr.at[2])
    keep_cot.wait()
    for copy in outs:
        copy.wait()
    for copy in sent:
        copy.wait_send()
    feed.finish()


def forward(x_in, cot_in, sa, sm, q_seg, k_seg, vectors, hc, rem):
    wide = lax.axis_size("wide")
    outer = wide // 2
    main = sa.shape[1]
    width = 2 * (main + rem)
    padded = -(-(width + 1) // LANES) * LANES
    rows = q_seg.shape[1]
    span = k_seg.shape[0]
    block = (2, rows + rem_rows(rows, main + rem), main)
    pairs = padded // LANES
    vmem = pl.BlockSpec(memory_space=pltpu.VMEM)
    shape = jax.ShapeDtypeStruct
    return pl.pallas_call(
        functools.partial(forward_kernel, outer, hc, rem),
        out_shape=(
            shape((2,) + block, BF),
            shape((wide, 2) + sm.shape, BF),
            shape((4, padded, padded), BF),
            shape((span, padded), BF),
            shape((span, padded), BF),
            shape((span, padded), BF),
            shape((span, padded), BF),
            shape((rows, padded), BF),
            shape((rows, padded), BF),
            shape((pairs, 8, rows), F32),
            shape((rows, padded), F32),
            shape((rows, padded), BF),
            shape((16, padded), F32),
        ),
        in_specs=[vmem] * 2 + [ANY] * 2 + [vmem] * (2 + len(vectors)),
        out_specs=(ANY,) * 7 + (vmem,) * 6,
        scratch_shapes=[
            pltpu.VMEM(block, BF),
            pltpu.VMEM(block, BF),
            pltpu.VMEM((2, 8, main + rem), F32),
            pltpu.VMEM((2, wide, 2) + sa.shape, BF),
            pltpu.VMEM((2, 6) + block[1:], BF),
            pltpu.VMEM((4, padded, padded), BF),
            pltpu.VMEM((span, padded), BF),
            pltpu.VMEM((span, padded), BF),
            pltpu.VMEM((span, padded), BF),
            pltpu.VMEM((span, padded), BF),
            pltpu.VMEM((span, rows), F32),
        ]
        + [DMA((3,)), DMA((3,)), DMA((5,)), DMA((5,)), DMA((3,)), DMA((3,)), DMA((2,)), DMA((5,))]
        + gather_sems(outer)
        + gather_sems(outer),
        compiler_params=pltpu.CompilerParams(
            collective_id=0, has_side_effects=True, vmem_limit_bytes=LIMIT
        ),
    )(x_in, cot_in, sa, sm, q_seg, k_seg, *vectors)


def attend_back_pair(q, k, v, g, lse, mask):
    q_n = q.astype(F32) * SCALE
    g_n = g.astype(F32)
    q_t, g_t = q_n.T, g_n.T
    row = lax.broadcasted_iota(jnp.int32, q_t.shape, 0)
    lane = lax.broadcasted_iota(jnp.int32, q_n.shape, 1)
    parts = []
    dk_sum = dv_sum = None
    for h in range(2):
        in_row = (row >= h * HEAD) & (row < (h + 1) * HEAD)
        in_lane = (lane >= h * HEAD) & (lane < (h + 1) * HEAD)
        s = dot(k, jnp.where(in_row, q_t, 0.0).astype(BF), NN) + mask[...]
        p = jnp.exp(s - lse[h : h + 1])
        dp = dot(v, jnp.where(in_row, g_t, 0.0).astype(BF), NN)
        delta = jnp.sum(p * dp, 0, keepdims=True)
        ds = (p * (dp - delta)).astype(BF)
        one = dot(ds, jnp.where(in_lane, q_n, 0.0).astype(BF), NN)
        two = dot(p.astype(BF), jnp.where(in_lane, g_n, 0.0).astype(BF), NN)
        dk_sum = one if dk_sum is None else dk_sum + one
        dv_sum = two if dv_sum is None else dv_sum + two
        parts.append(dot(k, ds, TN)[h * HEAD : (h + 1) * HEAD] * SCALE)
    return jnp.concatenate(parts, 0).T.astype(BF), dk_sum.astype(BF), dv_sum.astype(BF)


def backward_kernel(
    outer, hc, rem, grad_res, q, lse, q_seg, k_seg, vec, sums_in, k_in, v_in, wa_in, x_in, low1_in, mixed_in, pm, lo,
    mo, ao, em, ea, xg, vec_out, lo_out, m1, m2, m3, pcore,
    pool, k, v, dk, dv, dq, g, branch, mask, stage, firsts, a1, a2, a3, pa, po, edge,
    pg, got_x, got_y, got_z, out_y, out_z, sums, vx, vz,
    ls, xs, xr, hs, hr, cs, cr, vs, vr, ps, ms, es, *sems
):
    c, z, y, n, first, second = place()
    me = wide_of(z, y)
    wide = 2 * outer
    greet(partners(outer))
    other_n = (c, me, 1 - n)
    other_y = (c, wide_of(z, 1 - y), n)
    other_c = (1 - c, me, n)
    earlier = (c, wide_of(lax.rem(z + outer - 1, outer), y), n)
    main = pm.shape[3]
    width = 2 * (main + rem)
    rows, padded = q.shape
    span = k.shape[0]
    blocks = span // rows
    cols = 2 * hc
    block_rows = edge.shape[0]
    extra = pa.shape[2] - block_rows
    sent = []

    def go(copy):
        copy.start()
        sent.append(copy)

    def arrived(dst, recv):
        remote(dst, dst, recv, recv, other_c).wait_recv()

    feed = StagedScatter(
        outer, first, second, lambda z, y, n: pm.at[wide_of(z, y), n], m1, m2, m3, mo, sems[:8]
    )
    feed.stage(stage, ms, firsts)
    loads = [
        pltpu.make_async_copy(src, dst, ls.at[i])
        for i, (src, dst) in enumerate(
            (
                (wa_in.at[3], pool.at[0]),
                (k_in, k),
                (v_in, v),
                (wa_in.at[1], pool.at[1]),
                (wa_in.at[2], pool.at[2]),
                (wa_in.at[0], pool.at[0]),
                (x_in, v),
                (low1_in, k),
                (mixed_in, g),
                (lo.at[n], lo_out.at[:, pl.ds(pl.multiple_of(n * rows, LANES), rows)]),
            )
        )
    ]
    for copy in loads[:5] + loads[9:]:
        copy.start()
    feed.start()
    mine = lo_out.at[:, pl.ds(pl.multiple_of(n * rows, LANES), rows)]
    go(remote(lo.at[1 - n], mine, xs.at[2], xr.at[2], other_n))
    fill_mask(q_seg, k_seg, mask)
    branch[...] = grad_res[...].astype(BF)
    loads[0].wait()
    g[...] = dot(branch[...], pool[0], NT).astype(BF)
    loads[5].start()
    loads[1].wait()
    loads[2].wait()
    pairs = padded // LANES

    def some(begin, end):
        @pl.loop(begin, end)
        def _(i):
            at = pl.ds(pl.multiple_of(i * LANES, LANES), LANES)
            one, two, three = attend_back_pair(q[:, at], k[:, at], v[:, at], g[:, at], lse[i], mask)
            dq[:, at] = one
            dk[:, at] = two
            dv[:, at] = three

    steps = feed.steps()

    def pump(count):
        for _ in range(min(count, len(steps))):
            steps.pop(0)()

    some(0, pairs // 2)
    pump(1)
    some(pairs // 2, pairs)
    for copy in loads[6:9]:
        copy.start()
    sums[...] = sums_in[...]
    for copy in loads[3:7]:
        copy.wait()

    def input_part(j, extra_part):
        at = pl.ds(j * rows, rows)
        grad = dot(dk[at, :], pool[1], NN) + dot(dv[at, :], pool[2], NN)
        if extra_part:
            grad = grad + dot(dq[...], pool[0], NN)
        normed, scale = normed_rows(v[at, :].astype(F32), width)
        sums[0:1] += jnp.sum(grad * normed, 0, keepdims=True)
        sums[1:2] += jnp.sum(grad, 0, keepdims=True)
        back = norm_back(grad, normed, scale, vec[0:1], width)
        if extra_part:
            back = back + grad_res[...]
        store_packed(pg, (j,), back, main, rem)

    def x_back(j):
        go(remote(pg.at[1 - n, j], got_x.at[j], hs.at[j], hr.at[j], other_n))

    for j in (2, 1, 3, 0):
        input_part(j, False)
        x_back(j)
        if j == 1:
            pump(1)
    input_part(blocks - 1, True)
    x_back(blocks - 1)
    vx[0] = sums[...]
    go(remote(vx.at[0], vx.at[1], vs.at[0], vr.at[0], other_c))

    def products(s, left, right):
        size = 256
        for begin in range(0, padded, size):
            stop = min(begin + size, padded)
            pool[s, begin:stop, :] = dot(left[:, begin:stop], right, TN).astype(BF)

    for copy in loads[7:9]:
        copy.wait()
    products(3, g, branch[...])
    pump(1)
    products(0, dq, k[span - rows :, :])
    arrived(vx.at[1], vr.at[0])
    vz[z] = vx[0] + vx[1]
    for d in range(1, outer):
        device = (c, wide_of(lax.rem(z + d, outer), y), n)
        go(remote(vz.at[z], vz.at[z], vs.at[2 + d], vr.at[2 + d], device))
    products(1, dk, k[...])
    pump(2)
    products(2, dv, k[...])
    pump(1)

    def place_rows(i, core, out):
        for s in range(4):
            to = slice(s * hc, (s + 1) * hc)
            src = slice(i * cols + core * hc, i * cols + (core + 1) * hc)
            for h in range(2):
                out[h, to, :] = pool[s, src, h * main : (h + 1) * main]
            edge[to, :] = pool[s, src, 2 * main :]
        if block_rows > 4 * hc:
            gap = slice(4 * hc, block_rows)
            for h in range(2):
                out[h, gap, :] = jnp.zeros((block_rows - 4 * hc, main), BF)
            edge[gap, :] = jnp.zeros((block_rows - 4 * hc, LANES), BF)
        low = edge[...].astype(F32)
        for h in range(2):
            out[h, block_rows:, :] = squeezed(
                low[:, h * rem : (h + 1) * rem], extra, main, low[:, 2 * rem : 2 * rem + 1]
            ).astype(BF)

    def to_core(i):
        return remote(po.at[i % 2], pcore.at[i], cs.at[i], cr.at[i], other_c)

    for i in range(wide):
        if i >= 2:
            to_core(i - 2).wait_send()
        for core in range(2):
            pl.when(c == core)(functools.partial(place_rows, i, 1 - core, po.at[i % 2]))
        to_core(i).start()

    for i in range(wide):
        for core in range(2):
            pl.when(c == core)(functools.partial(place_rows, i, core, pa.at[i]))
    def fetch(i):
        arrived(pcore.at[i], cr.at[i])
        copy = pltpu.make_async_copy(pcore.at[i], po.at[i % 2], ps.at[i % 2])
        copy.start()
        return copy

    for i in range(max(wide - 2, 0), wide):
        to_core(i).wait_send()
    copies = [fetch(0)]
    for i in range(wide):
        if i + 1 < wide:
            copies.append(fetch(i + 1))
        copies[i].wait()
        for h in range(2):
            pa[i, h] = (pa[i, h].astype(F32) + po[i % 2, h].astype(F32)).astype(BF)
    heads = Scatter(
        outer, first, second, lambda z, y, n: pa.at[wide_of(z, y), n], a1, a2, a3, ao, sems[8:]
    )
    heads.start(0, 1)
    pump(len(steps))
    late = heads.steps()
    for d in range(1, outer):
        arrived(vz.at[lax.rem(z + outer - d, outer)], vr.at[2 + d])
    total = vz[0]
    for i in range(1, outer):
        total = total + vz[i]
    vx[2] = total
    go(remote(vx.at[2], vx.at[3], vs.at[1], vr.at[1], other_y))

    def summed(b):
        if b == 0:
            return jnp.where(n == 0, pg[n, 0].astype(F32), got_x[0].astype(F32))
        if b == 5:
            return jnp.where(n == 1, pg[n, 4].astype(F32), got_x[4].astype(F32))
        return pg[n, b - n].astype(F32) + got_x[b - 1 + n].astype(F32)

    for j in (2, 1, 3):
        arrived(got_x.at[j], hr.at[j])
    for b in range(2):
        out_y[b] = summed(2 + b).astype(BF)
    go(remote(out_y, got_y, xs.at[0], xr.at[0], other_y))
    heads.start(1)
    late.pop(0)()
    arrived(vx.at[3], vr.at[1])
    vx[4] = vx[2] + vx[3]
    go(remote(vx.at[4], vx.at[5], vs.at[2], vr.at[2], other_n))
    for j in (0, 4):
        arrived(got_x.at[j], hr.at[j])
    arrived(got_y, xr.at[0])
    for b in range(2):
        out_z[b] = (summed(b) + jnp.where(y == 1, got_y[b].astype(F32), 0.0)).astype(BF)
    go(remote(out_z, got_z, xs.at[1], xr.at[1], earlier))
    for _ in range(min(2, len(late))):
        late.pop(0)()
    feed.close(em, rem, es.at[0])
    for step in late:
        step()
    arrived(got_z, xr.at[1])
    for b in range(2):
        value = summed(4 + b) + jnp.where(y == 0, got_y[b].astype(F32), 0.0)
        value = value + got_z[b].astype(F32)
        at = slice(b * rows, (b + 1) * rows)
        xg[0:main, at] = value[0:rows].T.astype(BF)
        edge_x = jnp.concatenate([spread(value[rows:], rows, rem), jnp.zeros((rows, LANES - rem), F32)], 1)
        xg[main:, at] = edge_x.T[0:rem].astype(BF)
    arrived(vx.at[5], vr.at[2])
    total = vx[4] + vx[5]
    vec_out[:, 0:main] = jnp.where(n == 0, total[:, 0:main], total[:, main : 2 * main])
    edge_a, edge_b = total[:, 2 * main : 2 * main + rem], total[:, 2 * main + rem : 2 * main + 2 * rem]
    vec_out[:, main:] = jnp.where(n == 0, edge_a, edge_b)
    heads.close(ea, rem, es.at[1])
    loads[9].wait()
    arrived(lo_out.at[:, pl.ds(pl.multiple_of((1 - n) * rows, LANES), rows)], xr.at[2])
    for copy in sent:
        copy.wait_send()
    feed.finish()
    heads.finish()


def backward(grad_res, q, lse, q_seg, k_seg, vec, sums, k, v, wa, x5, low1, mixed, pm, lo, hc, fc2, rem):
    wide = pm.shape[0]
    outer = wide // 2
    rows, padded = q.shape
    span = k.shape[0]
    main = pm.shape[3]
    half = main + rem
    bm, bx = pm.shape[2:], (rows + rem_rows(rows, half), main)
    block_rows = up16(4 * hc)
    ba = (block_rows + rem_rows(block_rows, main + rem), main)
    vmem = pl.BlockSpec(memory_space=pltpu.VMEM)
    shape = jax.ShapeDtypeStruct
    few = max(outer - 1, 1)
    return pl.pallas_call(
        functools.partial(backward_kernel, outer, hc, rem),
        out_shape=(
            shape((2,) + bm, F32),
            shape((2,) + ba, F32),
            shape((2, fc2, LANES), F32),
            shape((2, block_rows, LANES), F32),
            shape((half, 2 * rows), BF),
            shape((sums.shape[0], half), F32),
            shape((half, 2 * rows), BF),
            shape((2 * outer,) + bm, BF),
            shape((outer,) + bm, BF),
            shape((few,) + bm, BF),
            shape((wide, 2) + ba, BF),
        ),
        in_specs=[vmem] * 7 + [ANY] * 8,
        out_specs=(vmem,) * 6 + (ANY,) * 5,
        scratch_shapes=[
            pltpu.VMEM((4, padded, padded), BF),
            pltpu.VMEM((span, padded), BF),
            pltpu.VMEM((span, padded), BF),
            pltpu.VMEM((span, padded), BF),
            pltpu.VMEM((span, padded), BF),
            pltpu.VMEM((rows, padded), BF),
            pltpu.VMEM((rows, padded), BF),
            pltpu.VMEM((rows, padded), BF),
            pltpu.VMEM((span, rows), F32),
            pltpu.VMEM((3,) + bm, BF),
            pltpu.VMEM((outer,) + bm, BF),
        ]
        + scatter_scratch(outer, ba)
        + [
            pltpu.VMEM((wide, 2) + ba, BF),
            pltpu.VMEM((2, 2) + ba, BF),
            pltpu.VMEM((block_rows, LANES), BF),
            pltpu.VMEM((2, span // rows) + bx, BF),
            pltpu.VMEM((5,) + bx, BF),
            pltpu.VMEM((2,) + bx, BF),
            pltpu.VMEM((2,) + bx, BF),
            pltpu.VMEM((2,) + bx, BF),
            pltpu.VMEM((2,) + bx, BF),
            pltpu.VMEM(sums.shape, F32),
            pltpu.VMEM((6,) + sums.shape, F32),
            pltpu.VMEM((outer,) + sums.shape, F32),
        ]
        + [DMA((10,)), DMA((3,)), DMA((3,)), DMA((5,)), DMA((5,)), DMA((wide,)), DMA((wide,))]
        + [DMA((2 + outer,)), DMA((2 + outer,)), DMA((2,)), DMA((3,)), DMA((2, 2))]
        + scatter_sems(outer)
        + scatter_sems(outer),
        compiler_params=pltpu.CompilerParams(
            collective_id=1, has_side_effects=True, vmem_limit_bytes=LIMIT
        ),
    )(grad_res, q, lse, q_seg, k_seg, vec, sums, k, v, wa, x5, low1, mixed, pm, lo)


def shards(
    layer_input,
    doc_segments,
    first_gain,
    first_shift,
    heads_weight,
    query_bias,
    value_bias,
    merge_weight,
    merge_bias,
    second_gain,
    second_shift,
    up_weight,
    up_bias,
    down_weight,
    down_bias,
    out_cotangent,
):
    parts = lax.axis_size("narrow")
    wide = lax.axis_size("wide")
    c, w, n = lax.axis_index("dp"), lax.axis_index("wide"), lax.axis_index("narrow")
    half = heads_weight.shape[0]
    width = half * parts
    padded = -(-width // LANES) * LANES
    cols = heads_weight.shape[2]
    units = up_weight.shape[1]
    hc, fc = cols // 2, up16(units // 2)
    short = fc - units // 2
    rows = layer_input.shape[0] // parts
    span = (REACH + 1) * rows

    by_half = heads_weight.transpose(1, 2, 0).reshape(3, 2, hc, half)
    heads_rows = lax.dynamic_index_in_dim(by_half, c, 1, False).reshape(3 * hc, half)
    merge_rows = lax.dynamic_slice_in_dim(merge_weight, c * hc, hc, 0)
    up_rows = lax.dynamic_slice_in_dim(up_weight, c * (units // 2), units // 2, 1).T
    down_rows = lax.dynamic_slice_in_dim(down_weight, c * (units // 2), units // 2, 0)
    up_rows = jnp.pad(up_rows, ((0, short), (0, 0)))
    down_rows = jnp.pad(down_rows, ((0, short), (0, 0)))
    line = lambda *v: jnp.pad(jnp.concatenate(v), (0, half - sum(e.shape[0] for e in v)))
    vectors = [first_gain, first_shift, merge_bias, second_gain, second_shift, down_bias]
    gap = up16(4 * hc) - 4 * hc
    sa = jnp.concatenate([heads_rows, merge_rows] + ([jnp.zeros((gap, half), BF)] if gap else []), 0)
    part = lambda v, size: lax.dynamic_slice_in_dim(v, c * size, size, 0)
    zero = lambda size: jnp.zeros((size,), BF)
    column_a = jnp.concatenate([part(query_bias, hc), zero(hc), part(value_bias, hc), zero(hc + gap)])
    sm = jnp.concatenate([up_rows, down_rows], 0)
    column_m = jnp.concatenate([part(up_bias, units // 2), zero(short + fc)])
    start = (w * parts + n) * rows
    ahead = jnp.pad(doc_segments, ((0, 0), (REACH * rows, 0)), constant_values=-1)
    segments = lax.dynamic_slice(ahead, (c, start), (1, span))
    k_seg = segments.reshape(span, 1)
    q_seg = segments[:, span - rows :]

    rem = widths(half)[1]
    cot_all, gm, wa, x5, low1, key, value, query, mixed, lse, residual, low2, vec = forward(
        layer_input.T, out_cotangent.T, pack(sa, column_a), pack(sm, column_m), q_seg, k_seg, vectors, hc, rem
    )
    pm, lo, grad_residual, sums = mlp(low2, cot_all, gm, residual, vec, fc, rem)

    mo, ao, em, ea, input_grad, lines, layer_output, _, _, _, _ = backward(
        grad_residual, query, lse, q_seg, k_seg, vec, sums, key, value, wa, x5, low1, mixed, pm, lo, hc, 2 * fc, rem
    )

    def total(block, edge, begin, size):
        at = slice(begin, begin + size)
        return jnp.concatenate([block[:, at], edge[:, at, :rem]], -1)

    input_grad, layer_output = input_grad.T, layer_output.T
    heads_total = total(ao, ea, 0, 3 * hc).reshape(2, 3, hc, half).transpose(3, 1, 0, 2).reshape(half, 3, cols)
    merge_total = total(ao, ea, 3 * hc, hc).reshape(cols, half)
    up_total = total(mo, em, 0, units // 2).reshape(units, half).T
    down_total = total(mo, em, fc, units // 2).reshape(units, half)
    up_bias_total = em[:, : units // 2, rem].reshape(units)
    query_total = ea[:, :hc, rem].reshape(cols)
    value_total = ea[:, 2 * hc : 3 * hc, rem].reshape(cols)
    return (
        layer_output,
        input_grad,
        lines[0],
        lines[1],
        heads_total,
        query_total,
        value_total,
        merge_total,
        lines[2],
        lines[3],
        lines[4],
        up_total,
        up_bias_total,
        down_total,
        lines[5],
    )


def solution(mesh):
    return jax.shard_map(
        shards,
        mesh=mesh,
        in_specs=(
            P(("dp", "wide"), "narrow"),
            P(),
            P("narrow"),
            P("narrow"),
            P("narrow", None, "wide"),
            P("wide"),
            P("wide"),
            P("wide", "narrow"),
            P("narrow"),
            P("narrow"),
            P("narrow"),
            P("narrow", "wide"),
            P("wide"),
            P("wide", "narrow"),
            P("narrow"),
            P(("dp", "wide"), "narrow"),
        ),
        out_specs=(
            P(("dp", "wide"), "narrow"),
            P(("dp", "wide"), "narrow"),
            P("narrow"),
            P("narrow"),
            P("narrow", None, "wide"),
            P("wide"),
            P("wide"),
            P("wide", "narrow"),
            P("narrow"),
            P("narrow"),
            P("narrow"),
            P("narrow", "wide"),
            P("wide"),
            P("wide", "narrow"),
            P("narrow"),
        ),
        check_vma=False,
    )
```

```python
import functools

import jax
import jax.numpy as jnp
from jax import lax
from jax.experimental import pallas as pl
from jax.experimental.pallas import tpu as pltpu
from jax.sharding import PartitionSpec as P

HEAD = 64
REACH = 4
EPS = 1e-05
NEGATIVE = -1e30
LANES = 128
BF = jnp.bfloat16
F32 = jnp.float32
MESH = pl.DeviceIdType.MESH
ANY = pl.BlockSpec(memory_space=pl.ANY)
DMA = pltpu.SemaphoreType.DMA
SCALE = HEAD ** (-0.5)
LIMIT = 62 * 1024 * 1024


def widths(half):
    main = half // LANES * LANES
    return main, half - main


def rem_rows(rows, half):
    main, rem = widths(half)
    return up16(-(-rows // (main // rem)))


def up16(rows):
    return -(-rows // 16) * 16


def pack(block, column=None):
    rows, half = block.shape[-2:]
    main, rem = widths(half)
    count = main // rem
    extra = rem_rows(rows, half)
    lead = block.shape[:-2]
    none = [(0, 0)] * len(lead)
    tail = jnp.pad(block[..., main:], none + [(0, count * extra - rows), (0, 0)])
    tail = jnp.swapaxes(tail.reshape(lead + (count, extra, rem)), -2, -3).reshape(lead + (extra, main))
    if column is not None:
        base, groups = column_base(rows, half), -(-rows // extra)
        column = jnp.pad(column, (0, groups * extra - rows)).reshape(groups, extra).T
        tail = jnp.concatenate([tail[:, :base], column, tail[:, base + groups :]], 1)
    return jnp.concatenate([block[..., :main], tail], -2)


def column_base(rows, half):
    return -(-rows // rem_rows(rows, half)) * widths(half)[1]


def column_of(block, rows, half):
    base, extra = column_base(rows, half), rem_rows(rows, half)
    groups = -(-rows // extra)
    tail = block[..., rows : rows + extra, base : base + groups]
    return jnp.swapaxes(tail, -1, -2).reshape(block.shape[:-2] + (groups * extra,))[..., :rows]


def unpack(block, rows, half):
    main, rem = widths(half)
    count = main // rem
    extra = rem_rows(rows, half)
    lead = block.shape[:-2]
    tail = block[..., rows : rows + extra, :].reshape(lead + (extra, count, rem))
    tail = jnp.swapaxes(tail, -2, -3).reshape(lead + (count * extra, rem))[..., :rows, :]
    return block[..., :rows, :], tail


def unpack_half(block, rows, half):
    return jnp.concatenate(unpack(block, rows, half), -1)


def join(blocks, rows, half):
    body, tail = unpack(blocks, rows, half)
    return jnp.concatenate([body[0], body[1], tail[0], tail[1]], -1)


def halves(full):
    half = full.shape[-1] // 2
    main, rem = widths(half)
    edge = 2 * main
    return jnp.stack(
        [
            jnp.concatenate([full[..., :main], full[..., edge : edge + rem]], -1),
            jnp.concatenate([full[..., main:edge], full[..., edge + rem :]], -1),
        ]
    )


def place():
    c, w, n = lax.axis_index("dp"), lax.axis_index("wide"), lax.axis_index("narrow")
    z, y = lax.div(w, 2), lax.rem(w, 2)
    first = (y + c * (1 - 2 * y), n + (1 - c) * (1 - 2 * n))
    second = (y + (1 - c) * (1 - 2 * y), n + c * (1 - 2 * n))
    return c, z, y, n, first, second


def wide_of(z, y):
    return z * 2 + y


def remote(src, dst, send, recv, device):
    return pltpu.make_async_remote_copy(
        src_ref=src, dst_ref=dst, send_sem=send, recv_sem=recv, device_id=device, device_id_type=MESH
    )


def greet(devices):
    barrier = pltpu.get_barrier_semaphore()
    for device in devices:
        pl.semaphore_signal(barrier, inc=1, device_id=device, device_id_type=MESH)
    pl.semaphore_wait(barrier, len(devices))


def partners(outer):
    c, z, y, n, _, _ = place()
    out = [(c, wide_of(lax.rem(z + d, outer), y), n) for d in range(1, outer)]
    out.append((c, wide_of(z, 1 - y), n))
    out.append((c, wide_of(z, y), 1 - n))
    out.append((1 - c, wide_of(z, y), n))
    return out


class Gather:
    def __init__(self, outer, src, out, both, first, second, sems, part=None):
        self.outer, self.src, self.out, self.both = outer, src, out, both
        self.part = outer if part is None else part
        self.first, self.second = first, second
        self.zs, self.zr, self.fs, self.fr, self.ss, self.sr, self.cs, self.cr, self.local = sems
        self.sent = []

    def block(self, z, y, n):
        c = lax.axis_index("dp")
        return self.out.at[c, wide_of(z, y), n] if self.both else self.out.at[wide_of(z, y), n]

    def go(self, copy):
        copy.start()
        self.sent.append(copy)

    def z_at(self, d):
        return lax.rem(place()[1] + self.outer - d, self.outer)

    def to_first(self, d, src):
        c, z, y, n, _, _ = place()
        first, second = self.first, self.second
        device = (c, wide_of(z, first[0]), first[1])
        self.go(remote(src, self.block(self.z_at(d), y, n), self.fs.at[d], self.fr.at[d], device))

    def to_second(self, d, src, k):
        if d >= self.part:
            return
        c, z, y, n, _, _ = place()
        first, second = self.first, self.second
        device = (c, wide_of(z, second[0]), second[1])
        dst = self.block(self.z_at(d), y, n) if k == 0 else self.block(self.z_at(d), *first)
        i = k * self.outer + d
        self.go(remote(src, dst, self.ss.at[i], self.sr.at[i], device))

    def to_core(self, i, src, dst):
        if self.both:
            c, z, y, n, _, _ = place()
            self.go(remote(src, dst, self.cs.at[i], self.cr.at[i], (1 - c, wide_of(z, y), n)))

    def start(self):
        c, z, y, n, _, _ = place()
        first, second = self.first, self.second
        own = self.block(z, y, n)
        self.keep = pltpu.make_async_copy(self.src, own, self.local)
        self.keep.start()
        for d in range(1, self.outer):
            device = (c, wide_of(lax.rem(z + d, self.outer), y), n)
            self.go(remote(self.src, own, self.zs.at[d - 1], self.zr.at[d - 1], device))

    def start_rest(self):
        c, z, y, n, _, _ = place()
        own = self.block(z, y, n)
        self.to_first(0, self.src)
        self.to_second(0, self.src, 0)
        self.to_core(0, self.src, own)

    def arrived(self, dst, recv):
        c, z, y, n, _, _ = place()
        remote(dst, dst, recv, recv, (1 - c, wide_of(z, y), n)).wait_recv()

    def along_z(self, d):
        c, z, y, n, _, _ = place()
        first, second = self.first, self.second
        got = self.block(self.z_at(d), y, n)
        self.arrived(got, self.zr.at[d - 1])
        self.to_first(d, got)
        self.to_second(d, got, 0)
        self.to_core(d, got, got)

    def along_first(self, d):
        c, z, y, n, _, _ = place()
        first, second = self.first, self.second
        got = self.block(self.z_at(d), *first)
        self.arrived(got, self.fr.at[d])
        self.to_second(d, got, 1)
        self.to_core(self.outer + d, got, got)

    def along_second(self, d, k):
        if d >= self.part:
            return
        c, z, y, n, _, _ = place()
        first, second = self.first, self.second
        got = self.block(self.z_at(d), *second) if k == 0 else self.block(self.z_at(d), 1 - y, 1 - n)
        i = k * self.outer + d
        self.arrived(got, self.sr.at[i])
        self.to_core(2 * self.outer + i, got, got)

    def finish(self):
        c, z, y, n, _, _ = place()
        first, second = self.first, self.second
        if self.both:
            spots = [(y, n), first, second, (1 - y, 1 - n)]
            for k, spot in enumerate(spots):
                for d in range(self.outer):
                    got = self.out.at[1 - c, wide_of(self.z_at(d), spot[0]), spot[1]]
                    self.arrived(got, self.cr.at[k * self.outer + d])
        self.keep.wait()
        for copy in self.sent:
            copy.wait_send()


def gather_sems(outer):
    return [
        DMA((outer,)),
        DMA((outer,)),
        DMA((outer,)),
        DMA((outer,)),
        DMA((2 * outer,)),
        DMA((2 * outer,)),
        DMA((4 * outer,)),
        DMA((4 * outer,)),
        DMA,
    ]


class Scatter:
    def __init__(self, outer, first, second, part, one, two, three, fin, sems):
        self.outer, self.part, self.first, self.second = outer, part, first, second
        self.one, self.two, self.three, self.fin = one, two, three, fin
        self.ss, self.sr, self.fs, self.fr, self.zs, self.zr, self.cs, self.cr = sems
        self.sent, self.along_first = [], {}

    def go(self, copy):
        copy.start()
        self.sent.append(copy)

    def arrived(self, dst, recv):
        c, z, y, n, _, _ = place()
        remote(dst, dst, recv, recv, (1 - c, wide_of(z, y), n)).wait_recv()

    def z_at(self, d):
        return lax.rem(place()[1] + d, self.outer)

    def order(self):
        return [d for d in range(1, self.outer)] + [0]

    def start(self, begin=0, end=None):
        c, z, y, n, _, _ = place()
        first, second = self.first, self.second
        device = (c, wide_of(z, second[0]), second[1])
        for d in self.order()[begin:end]:
            for k, spot in ((1, (1 - y, 1 - n)), (0, second)):
                i = k * self.outer + d
                self.go(
                    remote(self.part(self.z_at(d), *spot), self.one.at[i], self.ss.at[i], self.sr.at[i], device)
                )

    def steps(self):
        order = self.order()
        out = [functools.partial(self.to_first, order[0])]
        for here, there in zip(order[1:], order):
            out.append(functools.partial(self.to_first, here))
            out.append(functools.partial(self.to_z, there))
        return out + [functools.partial(self.to_z, order[-1])]

    def read(self, *refs):
        return [ref[...].astype(F32) for ref in refs]

    def to_first(self, d):
        c, z, y, n, _, _ = place()
        first, second = self.first, self.second
        device = (c, wide_of(z, first[0]), first[1])
        i = self.outer + d
        self.arrived(self.one.at[i], self.sr.at[i])
        own, got = self.read(self.part(self.z_at(d), *first), self.one.at[i])
        src = self.for_first(d)
        src[...] = (got + own).astype(BF)
        self.along_first[d] = remote(src, self.two.at[d], self.fs.at[d], self.fr.at[d], device)
        self.go(self.along_first[d])

    def for_first(self, d):
        return self.one.at[self.outer + d]

    def for_z(self, d):
        return self.one.at[d]

    def to_z(self, d):
        c, z, y, n, _, _ = place()
        self.arrived(self.one.at[d], self.sr.at[d])
        self.arrived(self.two.at[d], self.fr.at[d])
        own, one, two = self.read(self.part(self.z_at(d), y, n), self.one.at[d], self.two.at[d])
        value = (one + own).astype(BF).astype(F32) + two
        if d == 0:
            self.fin[c] = value
        else:
            src = self.for_z(d)
            src[...] = value.astype(BF)
            device = (c, wide_of(self.z_at(d), y), n)
            self.go(remote(src, self.three.at[d - 1], self.zs.at[d - 1], self.zr.at[d - 1], device))

    def close(self, edges, rem, edge_sems):
        c, z, y, n, _, _ = place()
        for d in range(1, self.outer):
            self.arrived(self.three.at[d - 1], self.zr.at[d - 1])
        value = self.fin[c]
        for d in range(1, self.outer):
            value = value + self.read(self.three.at[d - 1])[0]
        self.fin[c] = value
        other = (1 - c, wide_of(z, y), n)
        self.go(remote(self.fin.at[c], self.fin.at[c], self.cs, self.cr, other))
        rows = edges.shape[1]
        tail = value[rows:]
        base = -(-rows // tail.shape[0]) * rem
        empty = jnp.zeros((rows, LANES - rem - 1), F32)
        edges[c] = jnp.concatenate([spread(tail, rows, rem), spread(tail[:, base:], rows, 1), empty], 1)
        self.edges, self.edge_recv = edges, edge_sems.at[1]
        self.go(remote(edges.at[c], edges.at[c], edge_sems.at[0], edge_sems.at[1], other))

    def finish(self):
        c = lax.axis_index("dp")
        self.arrived(self.fin.at[1 - c], self.cr)
        self.arrived(self.edges.at[1 - c], self.edge_recv)
        for copy in self.sent:
            copy.wait_send()


class StagedScatter(Scatter):
    def stage(self, buffers, sems, firsts):
        self.buffers, self.load_sems, self.firsts = buffers, sems, firsts

    def read(self, *refs):
        copies = [
            pltpu.make_async_copy(ref, self.buffers.at[i], self.load_sems.at[i]) for i, ref in enumerate(refs)
        ]
        for copy in copies:
            copy.start()
        for copy in copies:
            copy.wait()
        return [self.buffers[i].astype(F32) for i in range(len(refs))]

    def for_first(self, d):
        return self.firsts.at[d]

    def for_z(self, d):
        slot = self.firsts.at[d]
        copy = self.along_first.pop(d)
        copy.wait_send()
        self.sent = [e for e in self.sent if e is not copy]
        return slot


def scatter_scratch(outer, block):
    return [
        pltpu.VMEM((2 * outer,) + block, BF),
        pltpu.VMEM((outer,) + block, BF),
        pltpu.VMEM((max(outer - 1, 1),) + block, BF),
    ]


def scatter_sems(outer):
    return [
        DMA((2 * outer,)),
        DMA((2 * outer,)),
        DMA((outer,)),
        DMA((outer,)),
        DMA((outer,)),
        DMA((outer,)),
        DMA,
        DMA,
    ]


def dot(left, right, dims):
    return lax.dot_general(left, right, ((dims[0], dims[1]), ((), ())), preferred_element_type=F32)


NN = ((1,), (0,))
NT = ((1,), (1,))
TN = ((0,), (0,))


def spread(tail, rows, rem):
    extra = tail.shape[0]
    count = -(-rows // extra)
    return jnp.concatenate([tail[:, k * rem : (k + 1) * rem] for k in range(count)], 0)[:rows]


def squeezed(block, extra, main, column=None):
    parts = []
    for piece in (block,) if column is None else (block, column):
        rows, each = piece.shape
        count = -(-rows // extra)
        short = count * extra - rows
        if short:
            piece = jnp.concatenate([piece, jnp.zeros((short, each), piece.dtype)], 0)
        parts += [piece[k * extra : (k + 1) * extra] for k in range(count)]
    used = sum(p.shape[1] for p in parts)
    if used < main:
        parts.append(jnp.zeros((extra, main - used), block.dtype))
    return jnp.concatenate(parts, 1)


def store_rows(dst, src, main, rem):
    rows = src.shape[1] // 2
    for i in range(2):
        at = slice(i * rows, (i + 1) * rows)
        dst[i, 0:rows, :] = src[0:main, at].astype(F32).T.astype(dst.dtype)
        low = src[main : main + rem, at].astype(F32).T
        dst[i, rows:, :] = squeezed(low, dst.shape[1] - rows, main).astype(dst.dtype)


def store_packed(ref, index, value, main, rem):
    rows = value.shape[0]
    for h in range(2):
        at = ref.at[(h,) + index]
        at[0:rows, :] = value[:, h * main : (h + 1) * main].astype(ref.dtype)
        low = value[:, 2 * main + h * rem : 2 * main + (h + 1) * rem]
        at[rows:, :] = squeezed(low, at.shape[0] - rows, main).astype(ref.dtype)


def gelu_and_slope(u):
    share = 0.5 * (1.0 + lax.erf(u * 0.7071067811865476))
    return u * share, share + u * (jnp.exp(-0.5 * u * u) * 0.3989422804014327)


def mlp_kernel(
    wide, fc, rem, low2, cot_in, gm, residual, vec,
    pm, lo, grad_res, sums,
    weights, grads, tails, cot, low2_all, acc, got, wsem, rsend, rrecv, psem, xs, xr
):
    c, z, y, n, first, second = place()
    outer = wide // 2
    part = (outer + 1) // 2
    other = (1 - c, wide_of(z, y), n)
    beside = (c, wide_of(z, second[0]), second[1])
    rows, padded = low2.shape
    main = gm.shape[3]
    width = 2 * (main + rem)
    extra = gm.shape[2] - 2 * fc
    nf = wide * fc
    base = -(-2 * fc // extra) * rem
    greet([other, beside])
    mine, theirs = pl.ds(c * rows, rows), pl.ds((1 - c) * rows, rows)
    swap_low = remote(low2, low2_all.at[mine], xs.at[0], xr.at[0], other)
    swap_low.start()
    spots = [(y, n), first, second, (1 - y, 1 - n)]

    def pieces(d, spot):
        src = gm.at[wide_of(lax.rem(z + outer - d, outer), spot[0]), spot[1]]
        lanes = pl.ds(pl.multiple_of(spot[1] * main, LANES), main)
        out = []
        for k in range(2):
            at = pl.ds(pl.multiple_of((2 * d + spot[0]) * fc, 16), fc)
            out.append((src.at[pl.ds(k * fc, fc)], weights.at[k, at, lanes]))
        return out + [(src.at[pl.ds(2 * fc, extra)], tails.at[2 * d + spot[0], spot[1]])]

    def local(d):
        return [
            pltpu.make_async_copy(src, dst, wsem.at[d, i, k])
            for i, spot in enumerate(spots if d < part else spots[:2])
            for k, (src, dst) in enumerate(pieces(d, spot))
        ]

    def afar(d):
        return [
            remote(src, dst, rsend.at[d - part, i, k], rrecv.at[d - part, i, k], beside)
            for i, spot in enumerate(spots[:2])
            for k, (src, dst) in enumerate(pieces(d, spot))
        ]

    def landed(d):
        for i, spot in enumerate(spots[2:]):
            for k, (_, dst) in enumerate(pieces(d, spot)):
                remote(dst, dst, rrecv.at[d - part, i, k], rrecv.at[d - part, i, k], other).wait_recv()

    for d in range(part, outer):
        for copy in afar(d):
            copy.start()
    for d in range(outer):
        for copy in local(d):
            copy.start()

    low2_all[mine] = low2[...]
    for k in range(2):
        span = slice(k * rows, (k + 1) * rows)
        for h in range(2):
            cot[span, h * main : (h + 1) * main] = cot_in[k, h, 0:rows, :]
        cot[span, 2 * main :] = edge_tile([cot_in[k, h, rows:, :] for h in range(2)], rows, rem)

    def ready(begin, end):
        for d in range(begin, end):
            for copy in local(d):
                copy.wait()
            if d >= part:
                landed(d)
        for i in range(2 * begin, 2 * end):
            both = edge_tile([tails[i, h] for h in range(2)], 2 * fc, rem, base)
            for k in range(2):
                weights[k, i * fc : (i + 1) * fc, 2 * main :] = both[k * fc : (k + 1) * fc]

    ready(0, part)
    size = 512
    done = 2 * part * fc // size * size
    acc[...] = jnp.zeros_like(acc)
    swap_low.wait_recv()

    def step(start, size):
        at = pl.ds(start, size)
        before = dot(low2_all[...], weights[0, at, :], NT)
        hidden, slope = gelu_and_slope(before)
        hidden = hidden.astype(BF)
        acc[0] += dot(hidden, weights[1, at, :], NN)
        grads[1, at, :] = dot(hidden, cot[...], TN).astype(BF)
        grad = dot(cot[...], weights[1, at, :], NT) * slope
        grad = grad.astype(BF)
        acc[1] += dot(grad, weights[0, at, :], NN)
        grads[0, at, :] = dot(grad, low2_all[...], TN).astype(BF)


    def steps(begin, end):
        full = (end - begin) // size

        @pl.loop(0, full)
        def _(j):
            step(pl.multiple_of(begin + j * size, size), size)

        if (end - begin) % size:
            step(begin + full * size, (end - begin) % size)

    steps(0, done)
    for d in range(part, outer):
        ready(d, d + 1)
        reach = nf if d == outer - 1 else 2 * (d + 1) * fc // size * size
        steps(done, reach)
        done = reach

    swap_acc = remote(acc.at[:, theirs], got, xs.at[1], xr.at[1], other)
    swap_acc.start()

    def grad_copies(i):
        dst = pm.at[wide_of(lax.rem(z + outer - i // 2, outer), i % 2)]
        out = []
        for h in range(2):
            for k in range(2):
                src = grads.at[k, i * fc : (i + 1) * fc, h * main : (h + 1) * main]
                out.append(pltpu.make_async_copy(src, dst.at[h, pl.ds(k * fc, fc)], psem.at[i, h, k]))
            out.append(pltpu.make_async_copy(tails.at[i, h], dst.at[h, pl.ds(2 * fc, extra)], psem.at[i, h, 2]))
        return out

    for i in range(wide):
        low = jnp.concatenate([grads[k, i * fc : (i + 1) * fc, 2 * main :] for k in range(2)], 0).astype(F32)
        for h in range(2):
            tails[i, h] = squeezed(
                low[:, h * rem : (h + 1) * rem], extra, main, low[:, 2 * rem : 2 * rem + 1]
            ).astype(BF)
        for copy in grad_copies(i):
            copy.start()

    swap_acc.wait_recv()
    result = residual[...] + (acc[0, mine] + got[0]) + vec[5:6]
    for h in range(2):
        lo[h, 0:main, :] = result[:, h * main : (h + 1) * main].T.astype(BF)
    edge = result[:, 2 * main :].T
    for h in range(2):
        lo[h, main:, :] = edge[h * rem : (h + 1) * rem].astype(BF)
    normed2, scale2 = normed_rows(residual[...], width)
    grad_low2 = acc[1, mine] + got[1]
    grad_out = cot[mine].astype(F32)
    lane = lax.broadcasted_iota(jnp.int32, grad_out.shape, 1)
    total = jnp.where(lane < width, grad_out + norm_back(grad_low2, normed2, scale2, vec[3:4], width), 0.0)
    grad_res[...] = total
    sums[...] = jnp.zeros_like(sums)
    sums[2:3] = jnp.sum(total.astype(BF).astype(F32), 0, keepdims=True)
    sums[3:4] = jnp.sum(grad_low2 * normed2, 0, keepdims=True)
    sums[4:5] = jnp.sum(grad_low2, 0, keepdims=True)
    sums[5:6] = jnp.sum(grad_out, 0, keepdims=True)

    for i in range(wide):
        for copy in grad_copies(i):
            copy.wait()
    for d in range(part, outer):
        for copy in afar(d):
            copy.wait_send()
    swap_low.wait_send()
    swap_acc.wait_send()


def mlp(low2, cot_in, gm, residual, vec, fc, rem):
    wide = gm.shape[0]
    rows, padded = low2.shape
    nf = wide * fc
    main = gm.shape[3]
    extra = gm.shape[2] - 2 * fc
    vmem = pl.BlockSpec(memory_space=pltpu.VMEM)
    return pl.pallas_call(
        functools.partial(mlp_kernel, wide, fc, rem),
        out_shape=(
            jax.ShapeDtypeStruct(gm.shape, BF),
            jax.ShapeDtypeStruct((2, main + rem, rows), BF),
            jax.ShapeDtypeStruct((rows, padded), F32),
            jax.ShapeDtypeStruct((16, padded), F32),
        ),
        in_specs=[vmem, vmem, ANY, vmem, vmem],
        out_specs=(ANY, vmem, vmem, vmem),
        scratch_shapes=[
            pltpu.VMEM((2, nf, padded), BF),
            pltpu.VMEM((2, nf, padded), BF),
            pltpu.VMEM((wide, 2, extra, main), BF),
            pltpu.VMEM((2 * rows, padded), BF),
            pltpu.VMEM((2 * rows, padded), BF),
            pltpu.VMEM((2, 2 * rows, padded), F32),
            pltpu.VMEM((2, rows, padded), F32),
            DMA((wide // 2, 4, 3)),
            DMA((wide // 2, 2, 3)),
            DMA((wide // 2, 2, 3)),
            DMA((wide, 2, 3)),
            DMA((2,)),
            DMA((2,)),
        ],
        compiler_params=pltpu.CompilerParams(
            collective_id=2, has_side_effects=True, vmem_limit_bytes=LIMIT
        ),
    )(low2, cot_in, gm, residual, vec)


def fill_mask(q_seg, k_seg, mask):
    keys, queries = mask.shape
    key = lax.broadcasted_iota(jnp.int32, (keys, queries), 0)
    query = lax.broadcasted_iota(jnp.int32, (keys, queries), 1) + (keys - queries)
    allowed = (k_seg[...] == q_seg[...]) & (key <= query)
    mask[...] = jnp.where(allowed, 0.0, NEGATIVE)


def turned(block):
    return block.astype(F32).T


def attend_pair(q, k, v, mask):
    q_t = turned(q) * SCALE
    row = lax.broadcasted_iota(jnp.int32, q_t.shape, 0)
    parts, logs = [], []
    for h in range(2):
        mine = (row >= h * HEAD) & (row < (h + 1) * HEAD)
        s = dot(k, jnp.where(mine, q_t, 0.0).astype(BF), NN) + mask[...]
        top = jnp.max(s, 0, keepdims=True)
        p = jnp.exp(s - top)
        total = jnp.sum(p, 0, keepdims=True)
        p = (p * (1.0 / total)).astype(BF)
        parts.append(dot(v, p, TN)[h * HEAD : (h + 1) * HEAD])
        logs.append(top + jnp.log(total))
    return jnp.concatenate(parts, 0).T.astype(BF), logs


def normed_rows(values, width):
    lane = lax.broadcasted_iota(jnp.int32, values.shape, 1)
    mean = jnp.sum(values, 1, keepdims=True) * (1.0 / width)
    centred = jnp.where(lane < width, values - mean, 0.0)
    scale = lax.rsqrt(jnp.sum(centred * centred, 1, keepdims=True) * (1.0 / width) + EPS)
    return centred * scale, scale


def norm_back(grad, normed, scale, gain, width):
    lane = lax.broadcasted_iota(jnp.int32, grad.shape, 1)
    scaled = jnp.where(lane < width, grad * gain, 0.0)
    first = jnp.sum(scaled, 1, keepdims=True) * (1.0 / width)
    second = jnp.sum(scaled * normed, 1, keepdims=True) * (1.0 / width)
    return scale * (scaled - first - normed * second)


def edge_tile(tails, rows, rem, base=None):
    tails = [t.astype(F32) for t in tails]
    parts = [spread(t, rows, rem) for t in tails]
    used = 2 * rem
    if base is not None:
        parts.append(spread(tails[0][:, base:], rows, 1))
        used += 1
    parts.append(jnp.zeros((rows, LANES - used), F32))
    return jnp.concatenate(parts, 1).astype(BF)


def forward_kernel(
    outer, hc, rem, x_in, cot_in, sa, sm, q_seg, k_seg, v0, v1, v2, v3, v4, v5,
    cot_out, gm, wa_out, x_out, low1_out, k_out, v_out, q, mixed, lse, residual, low2, vec,
    xin, cot, lines, ga, xs6, wa, x5, low1, k, v, mask, xs, xr, hs, hr, ks, kr, ls, os, *sems
):
    c, z, y, n, first, second = place()
    me = wide_of(z, y)
    wide = 2 * outer
    for src, dst in ((x_in, xin), (cot_in, cot)):
        store_rows(dst, src, sa.shape[1], rem)
    lines[...] = jnp.zeros_like(lines)
    for i, line in enumerate((v0, v1, v2, v3, v4, v5)):
        lines[n, i : i + 1, :] = line[...].astype(F32).reshape(1, -1)
    greet(partners(outer))
    other_n = (c, me, 1 - n)
    other_y = (c, wide_of(z, 1 - y), n)
    other_c = (1 - c, me, n)
    later = (c, wide_of(lax.rem(z + 1, outer), y), n)
    main = sa.shape[1]
    width = 2 * (main + rem)
    rows = q.shape[0]
    span = x5.shape[0]
    cols = 2 * hc
    sent = []

    def go(copy):
        copy.start()
        sent.append(copy)

    def arrived(dst, recv):
        remote(dst, dst, recv, recv, other_c).wait_recv()

    def x_send(j):
        src = xs6.at[n, j + 1 - n] if j < 4 else xin.at[1 - n]
        go(remote(src, xs6.at[n, j + 1 - n], hs.at[j], hr.at[j], other_n))

    own = xs6.at[n, pl.ds(4, 2)]
    keep = pltpu.make_async_copy(xin, own, ls.at[0])
    keep.start()
    keep_cot = pltpu.make_async_copy(cot.at[n], cot_out.at[c, n], ls.at[1])
    keep_cot.start()
    go(remote(lines.at[n], lines.at[n], xs.at[2], xr.at[2], other_n))
    go(remote(xin, xs6.at[n, pl.ds(0, 2)], xs.at[0], xr.at[0], later))
    x_send(4)
    heads = Gather(outer, sa, ga, True, (y, 1 - n), (1 - y, n), sems[:9])
    heads.start()
    heads.start_rest()
    fill_mask(q_seg, k_seg, mask)
    wa[:, width:, :] = jnp.zeros((4, wa.shape[1] - width, wa.shape[2]), BF)
    arrived(xs6.at[n, pl.ds(0, 2)], xr.at[0])
    keep.wait()
    x_send(0)
    go(remote(xs6.at[n, pl.ds(4 * (1 - y), 2)], xs6.at[n, pl.ds(2, 2)], xs.at[1], xr.at[1], other_y))
    for d in range(1, outer):
        heads.along_z(d)
    feed = Gather(outer, sm, gm, False, first, second, sems[9:], (outer + 1) // 2)
    feed.start()
    arrived(xs6.at[n, pl.ds(2, 2)], xr.at[1])
    for j in (1, 2, 3):
        x_send(j)
    for d in range(outer):
        heads.along_first(d)
    go(remote(cot.at[1 - n], cot_out.at[c, n], ks.at[0], kr.at[0], other_n))
    go(remote(cot.at[n], cot_out.at[c, n], ks.at[1], kr.at[1], other_c))
    feed.start_rest()

    arrived(lines.at[1 - n], xr.at[2])
    row = lax.broadcasted_iota(jnp.int32, (8, LANES), 0)
    lane = lax.broadcasted_iota(jnp.int32, (8, LANES), 1)
    unit = jnp.where(((row == 1) | (row == 4)) & (lane == 2 * rem), 1.0, 0.0)
    vec[...] = jnp.zeros_like(vec)
    for h in range(2):
        vec[0:8, h * main : (h + 1) * main] = lines[h, :, 0:main]
    edges = [lines[h, :, main:] for h in range(2)]
    vec[0:8, 2 * main :] = unit + jnp.concatenate(edges + [jnp.zeros((8, LANES - 2 * rem), F32)], 1)
    for j in range(5):
        arrived(xs6.at[1 - n, j + n], hr.at[j])
    for j in range(5):
        at = slice(j * rows, (j + 1) * rows)
        for h in range(2):
            x5[at, h * main : (h + 1) * main] = xs6[h, n + j, 0:rows, :]
        x5[at, 2 * main :] = edge_tile([xs6[h, n + j, rows:, :] for h in range(2)], rows, rem)
    outs = [pltpu.make_async_copy(x5, x_out, os.at[0])]
    outs[0].start()
    for kk in range(2):
        for d in range(outer):
            heads.along_second(d, kk)
    heads.finish()

    block_rows = up16(4 * hc)
    extra = ga.shape[3] - block_rows
    base = -(-block_rows // extra) * rem
    for i in range(wide):
        for half in range(2):
            edge = edge_tile([ga[half, i, h, block_rows:, :] for h in range(2)], block_rows, rem, base)
            for s in range(4):
                src = slice(s * hc, (s + 1) * hc)
                to = slice(i * cols + half * hc, i * cols + (half + 1) * hc)
                for h in range(2):
                    wa[s, to, h * main : (h + 1) * main] = ga[half, i, h, src, :]
                wa[s, to, 2 * main :] = edge[src]
    outs.append(pltpu.make_async_copy(wa, wa_out, os.at[1]))
    outs[1].start()
    feed.along_z(1)

    @pl.loop(0, span // rows)
    def _(j):
        at = pl.ds(pl.multiple_of(j * rows, rows), rows)
        normed, _ = normed_rows(x5[at, :].astype(F32), width)
        low1[at, :] = (normed * vec[0:1] + vec[1:2]).astype(BF)
        k[at, :] = dot(low1[at, :], wa[1], NT).astype(BF)
        v[at, :] = dot(low1[at, :], wa[2], NT).astype(BF)

    q[...] = dot(low1[span - rows :, :], wa[0], NT).astype(BF)
    for src, dst in ((low1, low1_out), (k, k_out), (v, v_out)):
        outs.append(pltpu.make_async_copy(src, dst, os.at[len(outs)]))
        outs[-1].start()

    pairs = q.shape[1] // LANES
    lse[...] = jnp.zeros_like(lse)

    def some(begin, end):
        @pl.loop(begin, end)
        def _(i):
            at = pl.ds(pl.multiple_of(i * LANES, LANES), LANES)
            out, logs = attend_pair(q[:, at], k[:, at], v[:, at], mask)
            mixed[:, at] = out
            for h in range(2):
                lse[i, pl.ds(h, 1), :] = logs[h]

    for d in range(2, outer):
        feed.along_z(d)
    cuts = [0, pairs // 3, 2 * pairs // 3, pairs]
    some(cuts[0], cuts[1])
    for d in range(feed.part):
        feed.along_first(d)
    arrived(cot_out.at[c, 1 - n], kr.at[0])
    go(remote(cot_out.at[c, 1 - n], cot_out.at[c, 1 - n], ks.at[2], kr.at[2], other_c))
    some(cuts[1], cuts[2])
    some(cuts[2], cuts[3])
    value = x5[span - rows :, :].astype(F32) + dot(mixed[...], wa[3], NN) + vec[2:3]
    residual[...] = value
    normed, _ = normed_rows(value, width)
    low2[...] = (normed * vec[3:4] + vec[4:5]).astype(BF)

    for d in range(feed.part, outer):
        feed.along_first(d)
    for kk in range(2):
        for d in range(outer):
            feed.along_second(d, kk)
    arrived(cot_out.at[1 - c, n], kr.at[1])
    arrived(cot_out.at[1 - c, 1 - n], kr.at[2])
    keep_cot.wait()
    for copy in outs:
        copy.wait()
    for copy in sent:
        copy.wait_send()
    feed.finish()


def forward(x_in, cot_in, sa, sm, q_seg, k_seg, vectors, hc, rem):
    wide = lax.axis_size("wide")
    outer = wide // 2
    main = sa.shape[1]
    width = 2 * (main + rem)
    padded = -(-(width + 1) // LANES) * LANES
    rows = q_seg.shape[1]
    span = k_seg.shape[0]
    block = (2, rows + rem_rows(rows, main + rem), main)
    pairs = padded // LANES
    vmem = pl.BlockSpec(memory_space=pltpu.VMEM)
    shape = jax.ShapeDtypeStruct
    return pl.pallas_call(
        functools.partial(forward_kernel, outer, hc, rem),
        out_shape=(
            shape((2,) + block, BF),
            shape((wide, 2) + sm.shape, BF),
            shape((4, padded, padded), BF),
            shape((span, padded), BF),
            shape((span, padded), BF),
            shape((span, padded), BF),
            shape((span, padded), BF),
            shape((rows, padded), BF),
            shape((rows, padded), BF),
            shape((pairs, 8, rows), F32),
            shape((rows, padded), F32),
            shape((rows, padded), BF),
            shape((16, padded), F32),
        ),
        in_specs=[vmem] * 2 + [ANY] * 2 + [vmem] * (2 + len(vectors)),
        out_specs=(ANY,) * 7 + (vmem,) * 6,
        scratch_shapes=[
            pltpu.VMEM(block, BF),
            pltpu.VMEM(block, BF),
            pltpu.VMEM((2, 8, main + rem), F32),
            pltpu.VMEM((2, wide, 2) + sa.shape, BF),
            pltpu.VMEM((2, 6) + block[1:], BF),
            pltpu.VMEM((4, padded, padded), BF),
            pltpu.VMEM((span, padded), BF),
            pltpu.VMEM((span, padded), BF),
            pltpu.VMEM((span, padded), BF),
            pltpu.VMEM((span, padded), BF),
            pltpu.VMEM((span, rows), F32),
        ]
        + [DMA((3,)), DMA((3,)), DMA((5,)), DMA((5,)), DMA((3,)), DMA((3,)), DMA((2,)), DMA((5,))]
        + gather_sems(outer)
        + gather_sems(outer),
        compiler_params=pltpu.CompilerParams(
            collective_id=0, has_side_effects=True, vmem_limit_bytes=LIMIT
        ),
    )(x_in, cot_in, sa, sm, q_seg, k_seg, *vectors)


def attend_back_pair(q, k, v, g, lse, mask):
    q_n = q.astype(F32) * SCALE
    g_n = g.astype(F32)
    q_t, g_t = q_n.T, g_n.T
    row = lax.broadcasted_iota(jnp.int32, q_t.shape, 0)
    lane = lax.broadcasted_iota(jnp.int32, q_n.shape, 1)
    parts = []
    dk_sum = dv_sum = None
    for h in range(2):
        in_row = (row >= h * HEAD) & (row < (h + 1) * HEAD)
        in_lane = (lane >= h * HEAD) & (lane < (h + 1) * HEAD)
        s = dot(k, jnp.where(in_row, q_t, 0.0).astype(BF), NN) + mask[...]
        p = jnp.exp(s - lse[h : h + 1])
        dp = dot(v, jnp.where(in_row, g_t, 0.0).astype(BF), NN)
        delta = jnp.sum(p * dp, 0, keepdims=True)
        ds = (p * (dp - delta)).astype(BF)
        one = dot(ds, jnp.where(in_lane, q_n, 0.0).astype(BF), NN)
        two = dot(p.astype(BF), jnp.where(in_lane, g_n, 0.0).astype(BF), NN)
        dk_sum = one if dk_sum is None else dk_sum + one
        dv_sum = two if dv_sum is None else dv_sum + two
        parts.append(dot(k, ds, TN)[h * HEAD : (h + 1) * HEAD] * SCALE)
    return jnp.concatenate(parts, 0).T.astype(BF), dk_sum.astype(BF), dv_sum.astype(BF)


def backward_kernel(
    outer, hc, rem, grad_res, q, lse, q_seg, k_seg, vec, sums_in, k_in, v_in, wa_in, x_in, low1_in, mixed_in, pm, lo,
    mo, ao, em, ea, xg, vec_out, lo_out, m1, m2, m3, pcore,
    pool, k, v, dk, dv, dq, g, branch, mask, stage, firsts, a1, a2, a3, pa, po, edge,
    pg, got_x, got_y, got_z, out_y, out_z, sums, vx, vz,
    ls, xs, xr, hs, hr, cs, cr, vs, vr, ps, ms, es, *sems
):
    c, z, y, n, first, second = place()
    me = wide_of(z, y)
    wide = 2 * outer
    greet(partners(outer))
    other_n = (c, me, 1 - n)
    other_y = (c, wide_of(z, 1 - y), n)
    other_c = (1 - c, me, n)
    earlier = (c, wide_of(lax.rem(z + outer - 1, outer), y), n)
    main = pm.shape[3]
    width = 2 * (main + rem)
    rows, padded = q.shape
    span = k.shape[0]
    blocks = span // rows
    cols = 2 * hc
    block_rows = edge.shape[0]
    extra = pa.shape[2] - block_rows
    sent = []

    def go(copy):
        copy.start()
        sent.append(copy)

    def arrived(dst, recv):
        remote(dst, dst, recv, recv, other_c).wait_recv()

    feed = StagedScatter(
        outer, first, second, lambda z, y, n: pm.at[wide_of(z, y), n], m1, m2, m3, mo, sems[:8]
    )
    feed.stage(stage, ms, firsts)
    loads = [
        pltpu.make_async_copy(src, dst, ls.at[i])
        for i, (src, dst) in enumerate(
            (
                (wa_in.at[3], pool.at[0]),
                (k_in, k),
                (v_in, v),
                (wa_in.at[1], pool.at[1]),
                (wa_in.at[2], pool.at[2]),
                (wa_in.at[0], pool.at[0]),
                (x_in, v),
                (low1_in, k),
                (mixed_in, g),
                (lo.at[n], lo_out.at[:, pl.ds(pl.multiple_of(n * rows, LANES), rows)]),
            )
        )
    ]
    for copy in loads[:5] + loads[9:]:
        copy.start()
    feed.start()
    mine = lo_out.at[:, pl.ds(pl.multiple_of(n * rows, LANES), rows)]
    go(remote(lo.at[1 - n], mine, xs.at[2], xr.at[2], other_n))
    fill_mask(q_seg, k_seg, mask)
    branch[...] = grad_res[...].astype(BF)
    loads[0].wait()
    g[...] = dot(branch[...], pool[0], NT).astype(BF)
    loads[5].start()
    loads[1].wait()
    loads[2].wait()
    pairs = padded // LANES

    def some(begin, end):
        @pl.loop(begin, end)
        def _(i):
            at = pl.ds(pl.multiple_of(i * LANES, LANES), LANES)
            one, two, three = attend_back_pair(q[:, at], k[:, at], v[:, at], g[:, at], lse[i], mask)
            dq[:, at] = one
            dk[:, at] = two
            dv[:, at] = three

    steps = feed.steps()

    def pump(count):
        for _ in range(min(count, len(steps))):
            steps.pop(0)()

    some(0, pairs // 2)
    pump(1)
    some(pairs // 2, pairs)
    for copy in loads[6:9]:
        copy.start()
    sums[...] = sums_in[...]
    for copy in loads[3:7]:
        copy.wait()

    def input_part(j, extra_part):
        at = pl.ds(j * rows, rows)
        grad = dot(dk[at, :], pool[1], NN) + dot(dv[at, :], pool[2], NN)
        if extra_part:
            grad = grad + dot(dq[...], pool[0], NN)
        normed, scale = normed_rows(v[at, :].astype(F32), width)
        sums[0:1] += jnp.sum(grad * normed, 0, keepdims=True)
        sums[1:2] += jnp.sum(grad, 0, keepdims=True)
        back = norm_back(grad, normed, scale, vec[0:1], width)
        if extra_part:
            back = back + grad_res[...]
        store_packed(pg, (j,), back, main, rem)

    def x_back(j):
        go(remote(pg.at[1 - n, j], got_x.at[j], hs.at[j], hr.at[j], other_n))

    for j in (2, 1, 3, 0):
        input_part(j, False)
        x_back(j)
        if j == 1:
            pump(1)
    input_part(blocks - 1, True)
    x_back(blocks - 1)
    vx[0] = sums[...]
    go(remote(vx.at[0], vx.at[1], vs.at[0], vr.at[0], other_c))

    def products(s, left, right):
        size = 256
        for begin in range(0, padded, size):
            stop = min(begin + size, padded)
            pool[s, begin:stop, :] = dot(left[:, begin:stop], right, TN).astype(BF)

    for copy in loads[7:9]:
        copy.wait()
    products(3, g, branch[...])
    pump(1)
    products(0, dq, k[span - rows :, :])
    arrived(vx.at[1], vr.at[0])
    vz[z] = vx[0] + vx[1]
    for d in range(1, outer):
        device = (c, wide_of(lax.rem(z + d, outer), y), n)
        go(remote(vz.at[z], vz.at[z], vs.at[2 + d], vr.at[2 + d], device))
    products(1, dk, k[...])
    pump(2)
    products(2, dv, k[...])
    pump(1)

    def place_rows(i, core, out):
        for s in range(4):
            to = slice(s * hc, (s + 1) * hc)
            src = slice(i * cols + core * hc, i * cols + (core + 1) * hc)
            for h in range(2):
                out[h, to, :] = pool[s, src, h * main : (h + 1) * main]
            edge[to, :] = pool[s, src, 2 * main :]
        if block_rows > 4 * hc:
            gap = slice(4 * hc, block_rows)
            for h in range(2):
                out[h, gap, :] = jnp.zeros((block_rows - 4 * hc, main), BF)
            edge[gap, :] = jnp.zeros((block_rows - 4 * hc, LANES), BF)
        low = edge[...].astype(F32)
        for h in range(2):
            out[h, block_rows:, :] = squeezed(
                low[:, h * rem : (h + 1) * rem], extra, main, low[:, 2 * rem : 2 * rem + 1]
            ).astype(BF)

    def to_core(i):
        return remote(po.at[i % 2], pcore.at[i], cs.at[i], cr.at[i], other_c)

    for i in range(wide):
        if i >= 2:
            to_core(i - 2).wait_send()
        for core in range(2):
            pl.when(c == core)(functools.partial(place_rows, i, 1 - core, po.at[i % 2]))
        to_core(i).start()

    for i in range(wide):
        for core in range(2):
            pl.when(c == core)(functools.partial(place_rows, i, core, pa.at[i]))
    def fetch(i):
        arrived(pcore.at[i], cr.at[i])
        copy = pltpu.make_async_copy(pcore.at[i], po.at[i % 2], ps.at[i % 2])
        copy.start()
        return copy

    for i in range(max(wide - 2, 0), wide):
        to_core(i).wait_send()
    copies = [fetch(0)]
    for i in range(wide):
        if i + 1 < wide:
            copies.append(fetch(i + 1))
        copies[i].wait()
        for h in range(2):
            pa[i, h] = (pa[i, h].astype(F32) + po[i % 2, h].astype(F32)).astype(BF)
    heads = Scatter(
        outer, first, second, lambda z, y, n: pa.at[wide_of(z, y), n], a1, a2, a3, ao, sems[8:]
    )
    heads.start(0, 1)
    pump(len(steps))
    late = heads.steps()
    for d in range(1, outer):
        arrived(vz.at[lax.rem(z + outer - d, outer)], vr.at[2 + d])
    total = vz[0]
    for i in range(1, outer):
        total = total + vz[i]
    vx[2] = total
    go(remote(vx.at[2], vx.at[3], vs.at[1], vr.at[1], other_y))

    def summed(b):
        if b == 0:
            return jnp.where(n == 0, pg[n, 0].astype(F32), got_x[0].astype(F32))
        if b == 5:
            return jnp.where(n == 1, pg[n, 4].astype(F32), got_x[4].astype(F32))
        return pg[n, b - n].astype(F32) + got_x[b - 1 + n].astype(F32)

    for j in (2, 1, 3):
        arrived(got_x.at[j], hr.at[j])
    for b in range(2):
        out_y[b] = summed(2 + b).astype(BF)
    go(remote(out_y, got_y, xs.at[0], xr.at[0], other_y))
    heads.start(1)
    late.pop(0)()
    arrived(vx.at[3], vr.at[1])
    vx[4] = vx[2] + vx[3]
    go(remote(vx.at[4], vx.at[5], vs.at[2], vr.at[2], other_n))
    for j in (0, 4):
        arrived(got_x.at[j], hr.at[j])
    arrived(got_y, xr.at[0])
    for b in range(2):
        out_z[b] = (summed(b) + jnp.where(y == 1, got_y[b].astype(F32), 0.0)).astype(BF)
    go(remote(out_z, got_z, xs.at[1], xr.at[1], earlier))
    for _ in range(min(2, len(late))):
        late.pop(0)()
    feed.close(em, rem, es.at[0])
    for step in late:
        step()
    arrived(got_z, xr.at[1])
    for b in range(2):
        value = summed(4 + b) + jnp.where(y == 0, got_y[b].astype(F32), 0.0)
        value = value + got_z[b].astype(F32)
        at = slice(b * rows, (b + 1) * rows)
        xg[0:main, at] = value[0:rows].T.astype(BF)
        edge_x = jnp.concatenate([spread(value[rows:], rows, rem), jnp.zeros((rows, LANES - rem), F32)], 1)
        xg[main:, at] = edge_x.T[0:rem].astype(BF)
    arrived(vx.at[5], vr.at[2])
    total = vx[4] + vx[5]
    vec_out[:, 0:main] = jnp.where(n == 0, total[:, 0:main], total[:, main : 2 * main])
    edge_a, edge_b = total[:, 2 * main : 2 * main + rem], total[:, 2 * main + rem : 2 * main + 2 * rem]
    vec_out[:, main:] = jnp.where(n == 0, edge_a, edge_b)
    heads.close(ea, rem, es.at[1])
    loads[9].wait()
    arrived(lo_out.at[:, pl.ds(pl.multiple_of((1 - n) * rows, LANES), rows)], xr.at[2])
    for copy in sent:
        copy.wait_send()
    feed.finish()
    heads.finish()


def backward(grad_res, q, lse, q_seg, k_seg, vec, sums, k, v, wa, x5, low1, mixed, pm, lo, hc, fc2, rem):
    wide = pm.shape[0]
    outer = wide // 2
    rows, padded = q.shape
    span = k.shape[0]
    main = pm.shape[3]
    half = main + rem
    bm, bx = pm.shape[2:], (rows + rem_rows(rows, half), main)
    block_rows = up16(4 * hc)
    ba = (block_rows + rem_rows(block_rows, main + rem), main)
    vmem = pl.BlockSpec(memory_space=pltpu.VMEM)
    shape = jax.ShapeDtypeStruct
    few = max(outer - 1, 1)
    return pl.pallas_call(
        functools.partial(backward_kernel, outer, hc, rem),
        out_shape=(
            shape((2,) + bm, F32),
            shape((2,) + ba, F32),
            shape((2, fc2, LANES), F32),
            shape((2, block_rows, LANES), F32),
            shape((half, 2 * rows), BF),
            shape((sums.shape[0], half), F32),
            shape((half, 2 * rows), BF),
            shape((2 * outer,) + bm, BF),
            shape((outer,) + bm, BF),
            shape((few,) + bm, BF),
            shape((wide, 2) + ba, BF),
        ),
        in_specs=[vmem] * 7 + [ANY] * 8,
        out_specs=(vmem,) * 6 + (ANY,) * 5,
        scratch_shapes=[
            pltpu.VMEM((4, padded, padded), BF),
            pltpu.VMEM((span, padded), BF),
            pltpu.VMEM((span, padded), BF),
            pltpu.VMEM((span, padded), BF),
            pltpu.VMEM((span, padded), BF),
            pltpu.VMEM((rows, padded), BF),
            pltpu.VMEM((rows, padded), BF),
            pltpu.VMEM((rows, padded), BF),
            pltpu.VMEM((span, rows), F32),
            pltpu.VMEM((3,) + bm, BF),
            pltpu.VMEM((outer,) + bm, BF),
        ]
        + scatter_scratch(outer, ba)
        + [
            pltpu.VMEM((wide, 2) + ba, BF),
            pltpu.VMEM((2, 2) + ba, BF),
            pltpu.VMEM((block_rows, LANES), BF),
            pltpu.VMEM((2, span // rows) + bx, BF),
            pltpu.VMEM((5,) + bx, BF),
            pltpu.VMEM((2,) + bx, BF),
            pltpu.VMEM((2,) + bx, BF),
            pltpu.VMEM((2,) + bx, BF),
            pltpu.VMEM((2,) + bx, BF),
            pltpu.VMEM(sums.shape, F32),
            pltpu.VMEM((6,) + sums.shape, F32),
            pltpu.VMEM((outer,) + sums.shape, F32),
        ]
        + [DMA((10,)), DMA((3,)), DMA((3,)), DMA((5,)), DMA((5,)), DMA((wide,)), DMA((wide,))]
        + [DMA((2 + outer,)), DMA((2 + outer,)), DMA((2,)), DMA((3,)), DMA((2, 2))]
        + scatter_sems(outer)
        + scatter_sems(outer),
        compiler_params=pltpu.CompilerParams(
            collective_id=1, has_side_effects=True, vmem_limit_bytes=LIMIT
        ),
    )(grad_res, q, lse, q_seg, k_seg, vec, sums, k, v, wa, x5, low1, mixed, pm, lo)


def shards(
    layer_input,
    doc_segments,
    first_gain,
    first_shift,
    heads_weight,
    query_bias,
    value_bias,
    merge_weight,
    merge_bias,
    second_gain,
    second_shift,
    up_weight,
    up_bias,
    down_weight,
    down_bias,
    out_cotangent,
):
    parts = lax.axis_size("narrow")
    wide = lax.axis_size("wide")
    c, w, n = lax.axis_index("dp"), lax.axis_index("wide"), lax.axis_index("narrow")
    half = heads_weight.shape[0]
    width = half * parts
    padded = -(-width // LANES) * LANES
    cols = heads_weight.shape[2]
    units = up_weight.shape[1]
    hc, fc = cols // 2, up16(units // 2)
    short = fc - units // 2
    rows = layer_input.shape[0] // parts
    span = (REACH + 1) * rows

    by_half = heads_weight.transpose(1, 2, 0).reshape(3, 2, hc, half)
    heads_rows = lax.dynamic_index_in_dim(by_half, c, 1, False).reshape(3 * hc, half)
    merge_rows = lax.dynamic_slice_in_dim(merge_weight, c * hc, hc, 0)
    up_rows = lax.dynamic_slice_in_dim(up_weight, c * (units // 2), units // 2, 1).T
    down_rows = lax.dynamic_slice_in_dim(down_weight, c * (units // 2), units // 2, 0)
    up_rows = jnp.pad(up_rows, ((0, short), (0, 0)))
    down_rows = jnp.pad(down_rows, ((0, short), (0, 0)))
    line = lambda *v: jnp.pad(jnp.concatenate(v), (0, half - sum(e.shape[0] for e in v)))
    vectors = [first_gain, first_shift, merge_bias, second_gain, second_shift, down_bias]
    gap = up16(4 * hc) - 4 * hc
    sa = jnp.concatenate([heads_rows, merge_rows] + ([jnp.zeros((gap, half), BF)] if gap else []), 0)
    part = lambda v, size: lax.dynamic_slice_in_dim(v, c * size, size, 0)
    zero = lambda size: jnp.zeros((size,), BF)
    column_a = jnp.concatenate([part(query_bias, hc), zero(hc), part(value_bias, hc), zero(hc + gap)])
    sm = jnp.concatenate([up_rows, down_rows], 0)
    column_m = jnp.concatenate([part(up_bias, units // 2), zero(short + fc)])
    start = (w * parts + n) * rows
    ahead = jnp.pad(doc_segments, ((0, 0), (REACH * rows, 0)), constant_values=-1)
    segments = lax.dynamic_slice(ahead, (c, start), (1, span))
    k_seg = segments.reshape(span, 1)
    q_seg = segments[:, span - rows :]

    rem = widths(half)[1]
    cot_all, gm, wa, x5, low1, key, value, query, mixed, lse, residual, low2, vec = forward(
        layer_input.T, out_cotangent.T, pack(sa, column_a), pack(sm, column_m), q_seg, k_seg, vectors, hc, rem
    )
    pm, lo, grad_residual, sums = mlp(low2, cot_all, gm, residual, vec, fc, rem)

    mo, ao, em, ea, input_grad, lines, layer_output, _, _, _, _ = backward(
        grad_residual, query, lse, q_seg, k_seg, vec, sums, key, value, wa, x5, low1, mixed, pm, lo, hc, 2 * fc, rem
    )

    def total(block, edge, begin, size):
        at = slice(begin, begin + size)
        return jnp.concatenate([block[:, at], edge[:, at, :rem]], -1)

    input_grad, layer_output = input_grad.T, layer_output.T
    heads_total = total(ao, ea, 0, 3 * hc).reshape(2, 3, hc, half).transpose(3, 1, 0, 2).reshape(half, 3, cols)
    merge_total = total(ao, ea, 3 * hc, hc).reshape(cols, half)
    up_total = total(mo, em, 0, units // 2).reshape(units, half).T
    down_total = total(mo, em, fc, units // 2).reshape(units, half)
    up_bias_total = em[:, : units // 2, rem].reshape(units)
    query_total = ea[:, :hc, rem].reshape(cols)
    value_total = ea[:, 2 * hc : 3 * hc, rem].reshape(cols)
    return (
        layer_output,
        input_grad,
        lines[0],
        lines[1],
        heads_total,
        query_total,
        value_total,
        merge_total,
        lines[2],
        lines[3],
        lines[4],
        up_total,
        up_bias_total,
        down_total,
        lines[5],
    )


def solution(mesh):
    return jax.shard_map(
        shards,
        mesh=mesh,
        in_specs=(
            P(("dp", "wide"), "narrow"),
            P(),
            P("narrow"),
            P("narrow"),
            P("narrow", None, "wide"),
            P("wide"),
            P("wide"),
            P("wide", "narrow"),
            P("narrow"),
            P("narrow"),
            P("narrow"),
            P("narrow", "wide"),
            P("wide"),
            P("wide", "narrow"),
            P("narrow"),
            P(("dp", "wide"), "narrow"),
        ),
        out_specs=(
            P(("dp", "wide"), "narrow"),
            P(("dp", "wide"), "narrow"),
            P("narrow"),
            P("narrow"),
            P("narrow", None, "wide"),
            P("wide"),
            P("wide"),
            P("wide", "narrow"),
            P("narrow"),
            P("narrow"),
            P("narrow"),
            P("narrow", "wide"),
            P("wide"),
            P("wide", "narrow"),
            P("narrow"),
        ),
        check_vma=False,
    )
```
